32 devices in a mesh: grp: 1, row: 32 (over z, y, x, core).
Axes of the slice: x: 2, y: 2, z: 4, core: 2. Of those that a mesh axis runs over, the one named last changes fastest.
Arguments:
- pair: bfloat16 [384, 384, 128], P(('grp', 'row')), may hold values from -6 to 6
- residue_mask: int32 [384], P('grp'), may hold values 0 or 1
- chain_ids: int32 [384], P('grp'), may hold values from 0 to 5, never falling along the last dimension, each value on 1 to 96 neighbouring positions
- ln_in_gain: float32 [2, 128], replicated, may hold values from 0.5 to 1.5
- ln_in_bias: float32 [2, 128], replicated, may hold values from -3 to 3
- chain_embed: float32 [2, 128], replicated, may hold values from -4 to 4
- w_ab: bfloat16 [2, 128, 512], replicated, may hold values from -0.5 to 0.5
- w_gate: bfloat16 [2, 128, 128], replicated, may hold values from -0.5 to 0.5
- ln_mid_gain: float32 [2, 128], replicated, may hold values from 0.5 to 1.5
- ln_mid_bias: float32 [2, 128], replicated, may hold values from -3 to 3
- w_out: bfloat16 [2, 128, 128], replicated, may hold values from -0.5 to 0.5
Outputs:
- updated_pair: bfloat16 [384, 384, 128], P(('grp', 'row'))
The draws below stay inside these ranges and needn't reach their ends.
Inputs may be any that keep to these rules, and one draw needn't show every extreme that they name: `chain_ids`: never falls along the residues; each chain holds 1 to 96 residues and one holds exactly 96.
All inputs are finite; a program needn't handle non-finite values.
Results may differ from the reference program's by a relative error of at most 0.0055.
Values may be sent and summed in bfloat16 or wider, within the bound.
No kernel may reach another device: no remote copies, remote signals or barrier semaphores. Data moves between devices by JAX's collectives and lax.ppermute only.
A program may use at most 64 MiB of HBM per device.

```python
import math
import jax
import jax.numpy as jnp
import numpy as np
from jax import lax

C = 128
HC = 128
N = 384


def plant(array, own_key, smallest, high):
    place = [jax.random.randint(jax.random.fold_in(own_key, axis), (), 0, length) for axis, length in enumerate(array.shape)]
    main_axis = array.shape.index(max(array.shape))
    beside = place[:main_axis] + [(place[main_axis] + 1) % array.shape[main_axis]] + place[main_axis + 1:]
    return array.at[tuple(place)].set(smallest).at[tuple(beside)].set(high)


def level_of(rng, dims, split, low, high):
    def one(position, blocks):
        heights = jax.random.uniform(jax.random.fold_in(jax.random.fold_in(rng, 6), position), (blocks,), jnp.float32, low / len(split), high / len(split))
        return jnp.repeat(jnp.exp(heights), dims[position] // blocks).reshape((-1,) + (1,) * (len(dims) - position - 1))

    level = one(*split[0])
    for cut in split[1:]:
        level = level * one(*cut)
    return level


def length_profile(count, total, limit, slope):
    portions = [(1 << 20) // math.isqrt(grade ** slope) + 1 for grade in range(2, count + 1)]
    spare, given = total - limit - (count - 1), [1] * (count - 1)
    while spare > 0:
        movable = [i for i in range(count - 1) if given[i] < limit]
        pool, remaining = sum([portions[i] for i in movable]), spare
        for i in movable:
            more = min(limit - given[i], max(1, remaining * portions[i] // pool), spare)
            given[i] = given[i] + more
            spare = spare - more
    return np.array([limit] + given)


def ragged_sizes(stream_key, number_of, total, reach, skew):
    if number_of == 2:
        one = jax.random.randint(stream_key, (), max(1, total - reach), min(reach, total - 1) + 1)
        return jnp.stack([one, total - one])
    sizes = jnp.asarray(length_profile(number_of, total, reach, skew), jnp.int32)
    twos = (number_of - 1) // 2
    donor, receiver = sizes[1:1 + 2 * twos:2], sizes[2:2 + 2 * twos:2]
    margin = jnp.minimum(donor - 1, reach - receiver)
    moved = jax.random.randint(jax.random.fold_in(stream_key, 1), (twos,), 0, 1 << 20) % (margin + 1)
    sizes = sizes.at[1:1 + 2 * twos:2].set(donor - moved).at[2:2 + 2 * twos:2].set(receiver + moved)
    return sizes[jax.random.permutation(jax.random.fold_in(stream_key, 2), number_of)]


def scatter_about(stream_key, extent, width, most, shards=(), dtype=jnp.bfloat16):
    level = level_of(stream_key, extent, shards, -0.22, 0.18) if shards else 1.0
    array = jax.random.normal(stream_key, extent, jnp.float32) * width * level
    return jnp.minimum(jnp.maximum(array, -most), most).astype(dtype)


def setup_inputs(seed: int = 0, part: int = 0) -> dict:
    splits = jax.random.split(jax.random.key(seed), 12)
    own_keys = jax.random.split(jax.random.fold_in(splits[11], part), 12)
    pair = scatter_about(own_keys[0], (N, N, C), 1.0, 6.0, ((0, 32),))
    residue_mask = plant((jax.random.randint(own_keys[1], (N,), 0, 8) < 7).astype(jnp.int32), jax.random.fold_in(own_keys[1], 1), 0, 1)
    chain_ids = jnp.searchsorted(jnp.cumsum(ragged_sizes(own_keys[2], 6, N, N // 4, 0)), jnp.arange(N), side="right").astype(jnp.int32)
    ln_in_gain = jnp.clip(jax.random.uniform(splits[3], (2, C), jnp.float32, 0.5, 1.5), 0.5, 1.5)
    ln_in_bias = scatter_about(splits[4], (2, C), 0.5, 3.0, (), jnp.float32)
    chain_embed = scatter_about(splits[5], (2, C), 1.0, 4.0, (), jnp.float32)
    w_ab = scatter_about(splits[6], (2, C, 4 * HC), C ** -0.5, 0.5)
    w_gate = scatter_about(splits[7], (2, C, C), C ** -0.5, 0.5)
    ln_mid_gain = jnp.clip(jax.random.uniform(splits[8], (2, HC), jnp.float32, 0.5, 1.5), 0.5, 1.5)
    ln_mid_bias = scatter_about(splits[9], (2, HC), 0.5, 3.0, (), jnp.float32)
    w_out = scatter_about(splits[10], (2, HC, C), HC ** -0.5, 0.5)
    return {"pair": pair, "residue_mask": residue_mask, "chain_ids": chain_ids, "ln_in_gain": ln_in_gain, "ln_in_bias": ln_in_bias, "chain_embed": chain_embed, "w_ab": w_ab, "w_gate": w_gate, "ln_mid_gain": ln_mid_gain, "ln_mid_bias": ln_mid_bias, "w_out": w_out}


EPS = 1e-05

def norm_last(values, gain, bias):
    mean = lax.optimization_barrier(jnp.mean(values, axis=-1, keepdims=True))
    centred = values - mean
    var = lax.optimization_barrier(jnp.mean(centred * centred, axis=-1, keepdims=True))
    return centred * lax.rsqrt(var + EPS) * gain + bias

def one_update(pair, pair_mask, same_chain, weights, incoming):
    g_in, b_in, embed, w_ab, w_gate, g_mid, b_mid, w_out = weights
    block = math.gcd(N, 128)
    count = N // block
    rows = pair.reshape(count, block, N, C)
    mask_rows = pair_mask.reshape(count, block, N)
    same_rows = same_chain.reshape(count, block, N)

    def project(item):
        x_rows, m_rows, s_rows = item
        normed = norm_last(x_rows.astype(jnp.float32), g_in, b_in) + s_rows[..., None] * embed
        normed = normed.astype(jnp.bfloat16)
        flat = normed.reshape(-1, C)
        proj = jnp.dot(flat, w_ab, preferred_element_type=jnp.float32).reshape(block, N, 4 * HC)
        left = jax.nn.sigmoid(proj[..., :HC]) * proj[..., HC:2 * HC] * m_rows[..., None]
        right = jax.nn.sigmoid(proj[..., 2 * HC:3 * HC]) * proj[..., 3 * HC:] * m_rows[..., None]
        gate = jax.nn.sigmoid(jnp.dot(flat, w_gate, preferred_element_type=jnp.float32)).reshape(block, N, C)
        return (left.astype(jnp.bfloat16), right.astype(jnp.bfloat16), gate)
    left, right, gate = lax.map(project, (rows, mask_rows, same_rows))
    left = left.reshape(N, N, HC).astype(jnp.float32)
    right = right.reshape(N, N, HC).astype(jnp.float32)
    if incoming:
        tri = jnp.einsum('kic,kjc->ijc', left, right)
    else:
        tri = jnp.einsum('ikc,jkc->ijc', left, right)
    tri = tri.astype(jnp.bfloat16)

    def finish(item):
        t_rows, x_rows, g_rows = item
        tri_norm = norm_last(t_rows.astype(jnp.float32), g_mid, b_mid).astype(jnp.bfloat16)
        branch = jnp.dot(tri_norm.reshape(-1, HC), w_out, preferred_element_type=jnp.float32).reshape(block, N, C)
        return (x_rows.astype(jnp.float32) + g_rows * branch).astype(jnp.bfloat16)
    result = lax.map(finish, (tri.reshape(count, block, N, HC), rows, gate))
    return result.reshape(N, N, C)

def reference(pair, residue_mask, chain_ids, ln_in_gain, ln_in_bias, chain_embed, w_ab, w_gate, ln_mid_gain, ln_mid_bias, w_out):
    mask_f = residue_mask.astype(jnp.float32)
    pair_mask = mask_f[:, None] * mask_f[None, :]
    same_chain = (chain_ids[:, None] == chain_ids[None, :]).astype(jnp.float32)
    state = pair
    for layer in range(2):
        weights = (ln_in_gain[layer], ln_in_bias[layer], chain_embed[layer], w_ab[layer], w_gate[layer], ln_mid_gain[layer], ln_mid_bias[layer], w_out[layer])
        state = one_update(state, pair_mask, same_chain, weights, layer == 1)
    return state
```

```python
import functools

import jax
import jax.numpy as jnp
from jax import lax
from jax.experimental import pallas as pl
from jax.experimental.pallas import tpu as pltpu
from jax.sharding import PartitionSpec as P

C = 128
HC = 128
EPS = 1e-05
F32 = jnp.float32
BF16 = jnp.bfloat16
VMEM_LIMIT = 48 * 1024 * 1024

WHOLE = pl.BlockSpec(memory_space=pltpu.VMEM)
SCALARS = pl.BlockSpec(memory_space=pltpu.SMEM)


def blocks(width):
    return [(j, slice(j * 128, (j + 1) * 128)) for j in range(width // 128)]


def column(vector_ref, layer, width):
    square = jnp.broadcast_to(vector_ref[layer : layer + 1, :], (C, C)).T
    return jnp.concatenate([square] * (width // C), axis=1)


def norm_channels(values, gain, bias):
    mean = jnp.sum(values, axis=0, keepdims=True) * (1.0 / C)
    centred = values - mean
    var = jnp.sum(centred * centred, axis=0, keepdims=True) * (1.0 / C)
    return centred * lax.rsqrt(var + EPS) * gain + bias


def norm_input(x_t, chain_row, chain_ref, gain, bias, embed):
    same = (chain_ref[...] == chain_row).astype(F32)
    return (norm_channels(x_t, gain, bias) + same * embed).astype(BF16)


def project_row(r, normed, mask_row, mask_ref, w_t, slabs):
    rows = slabs.shape[1] // (2 * HC)
    proj = jnp.dot(w_t[...], normed, preferred_element_type=F32)
    mask = mask_ref[...] * mask_row
    for side in range(2):
        p = proj[2 * side * HC : (2 * side + 2) * HC]
        value = jax.nn.sigmoid(p[:HC]) * p[HC:] * mask
        for j, columns in blocks(value.shape[1]):
            slabs[j, pl.ds(side * HC * rows + r, HC, stride=rows), :] = value[:, columns]


def write_slabs(slabs, out):
    devices, depth, width = out.shape
    half = depth // 2
    for side in range(2):
        for d in range(devices):
            start = (side * devices + d) * half
            for j, columns in blocks(width):
                out[d, side * half : (side + 1) * half, columns] = slabs[j, start : start + half, :].astype(BF16)


def first_kernel(
    mask_rows, chain_rows, x, mask, chain, gain, bias, embed, w_ab, out, x_t, w_t, g, b, e, slabs
):
    rows, width, _ = x.shape
    w_t[...] = w_ab[0].astype(F32).T.astype(BF16)
    g[...] = column(gain, 0, width)
    b[...] = column(bias, 0, width)
    e[...] = column(embed, 0, width)
    eye = (
        lax.broadcasted_iota(jnp.int32, (C, C), 0) == lax.broadcasted_iota(jnp.int32, (C, C), 1)
    ).astype(BF16)

    def step(r, carry):
        turned = lax.dot_general(
            eye, x[r], (((1,), (1,)), ((), ())), preferred_element_type=F32
        )
        x_t[r] = turned.astype(BF16)
        normed = norm_input(turned, chain_rows[r], chain, g[...], b[...], e[...])
        project_row(r, normed, mask_rows[r], mask, w_t, slabs)
        return carry

    lax.fori_loop(0, rows, step, 0)
    write_slabs(slabs, out)


def gate_kernel(layer, chain_rows, x_t, chain, gain, bias, embed, w_gate, out, w_t, g, b, e):
    rows, _, width = x_t.shape
    w_t[...] = w_gate[layer].astype(F32).T.astype(BF16)
    g[...] = column(gain, layer, width)
    b[...] = column(bias, layer, width)
    e[...] = column(embed, layer, width)

    def step(r, carry):
        normed = norm_input(x_t[r].astype(F32), chain_rows[r], chain, g[...], b[...], e[...])
        out[r] = jax.nn.sigmoid(jnp.dot(w_t[...], normed, preferred_element_type=F32))
        return carry

    lax.fori_loop(0, rows, step, 0)


def products_kernel(incoming, rows, recv, out, wide, square, turned):
    devices, depth, width = recv.shape
    channels = depth // (2 * rows)
    widen(recv, wide)

    def gathered(side, c, where):
        for j, _ in blocks(width):
            for r in range(rows):
                start = (side * channels + c) * rows + r
                where[j, pl.ds(r, devices, stride=rows), :] = wide[j, pl.ds(start, devices, stride=depth), :]
        return jnp.concatenate([where[j].astype(BF16) for j, _ in blocks(width)], axis=1)

    for c in range(channels):
        left = gathered(0, c, square)
        right = gathered(1, c, square)
        dims = (((0,), (0,)), ((), ())) if incoming else (((1,), (1,)), ((), ()))
        product = lax.dot_general(left, right, dims, preferred_element_type=F32)
        for j, columns in blocks(width):
            square[j] = product[:, columns]
            for r in range(rows):
                turned[j, pl.ds(c * rows + r, devices, stride=channels * rows), :] = square[
                    j, pl.ds(r, devices, stride=rows), :
                ]
    for s in range(devices):
        for j, columns in blocks(width):
            out[s, :, columns] = turned[j, s * channels * rows : (s + 1) * channels * rows, :].astype(BF16)


def finish_row(r, tri, gate, x_t, g, b, w_t):
    rows = tri.shape[1] // HC
    values = jnp.concatenate([tri[j, pl.ds(r, HC, stride=rows), :] for j in range(tri.shape[0])], axis=1)
    normed = norm_channels(values, g[...], b[...]).astype(BF16)
    branch = jnp.dot(w_t[...], normed, preferred_element_type=F32)
    return (x_t[r].astype(F32) + gate[r] * branch).astype(BF16)


def widen(recv, wide):
    devices, depth, width = recv.shape
    for s in range(devices):
        for j, columns in blocks(width):
            wide[j, s * depth : (s + 1) * depth, :] = recv[s, :, columns].astype(F32)


def middle_kernel(
    mask_rows, chain_rows, recv, gate, x_t, mask, chain, gain, bias, embed, w_ab, mid_gain, mid_bias, w_out,
    out, new_t, w_t, g, b, e, slabs, w_out_t, mg, mb, tri,
):
    rows, _, width = x_t.shape
    w_t[...] = w_ab[1].astype(F32).T.astype(BF16)
    g[...] = column(gain, 1, width)
    b[...] = column(bias, 1, width)
    e[...] = column(embed, 1, width)
    w_out_t[...] = w_out[0].astype(F32).T.astype(BF16)
    mg[...] = column(mid_gain, 0, width)
    mb[...] = column(mid_bias, 0, width)
    widen(recv, tri)

    def step(r, carry):
        state = finish_row(r, tri, gate, x_t, mg, mb, w_out_t)
        new_t[r] = state
        normed = norm_input(state.astype(F32), chain_rows[r], chain, g[...], b[...], e[...])
        project_row(r, normed, mask_rows[r], mask, w_t, slabs)
        return carry

    lax.fori_loop(0, rows, step, 0)
    write_slabs(slabs, out)


def last_kernel(recv, gate, x_t, mid_gain, mid_bias, w_out, out, w_out_t, mg, mb, tri):
    rows, _, width = x_t.shape
    w_out_t[...] = w_out[1].astype(F32).T.astype(BF16)
    mg[...] = column(mid_gain, 1, width)
    mb[...] = column(mid_bias, 1, width)
    widen(recv, tri)

    def step(r, carry):
        out[r] = finish_row(r, tri, gate, x_t, mg, mb, w_out_t).astype(F32).T.astype(BF16)
        return carry

    lax.fori_loop(0, rows, step, 0)


def call(kernel, outs, scratch, scalars, arrays, flops):
    size = sum(a.size * a.dtype.itemsize for a in list(arrays) + list(outs))
    return pl.pallas_call(
        kernel,
        out_shape=outs,
        in_specs=[SCALARS] * len(scalars) + [WHOLE] * len(arrays),
        out_specs=[WHOLE] * len(outs),
        scratch_shapes=[pltpu.VMEM(shape, dtype) for shape, dtype in scratch],
        compiler_params=pltpu.CompilerParams(vmem_limit_bytes=VMEM_LIMIT),
        cost_estimate=pl.CostEstimate(flops=flops, bytes_accessed=size, transcendentals=0),
    )(*scalars, *arrays)


def local(
    pair, residue_mask, chain_ids, ln_in_gain, ln_in_bias, chain_embed, w_ab, w_gate, ln_mid_gain, ln_mid_bias, w_out
):
    rows, width, _ = pair.shape
    devices = lax.axis_size("row")
    channels = HC // devices
    start = lax.axis_index("row") * rows
    mask = residue_mask.astype(F32)
    mask_rows = lax.dynamic_slice_in_dim(mask, start, rows)
    chain_rows = lax.dynamic_slice_in_dim(chain_ids, start, rows)
    mask = mask[None, :]
    chain = chain_ids[None, :]

    sent = jax.ShapeDtypeStruct((devices, 2 * channels * rows, width), BF16)
    back = jax.ShapeDtypeStruct((devices, channels * rows, width), BF16)
    state_t = jax.ShapeDtypeStruct((rows, C, width), BF16)
    gate_t = jax.ShapeDtypeStruct((rows, C, width), F32)
    vector = ((C, width), F32)
    square = ((C, C), BF16)
    head = [((4 * HC, C), BF16), vector, vector, vector, ((width // 128, 2 * HC * rows, 128), F32)]
    tail = [square, vector, vector, ((width // 128, HC * rows, 128), F32)]
    pairs = rows * width
    norms = (ln_in_gain, ln_in_bias, chain_embed)
    mids = (ln_mid_gain, ln_mid_bias, w_out)

    def exchange(slabs):
        return lax.all_to_all(slabs, "row", split_axis=0, concat_axis=0, tiled=True)

    def gates(layer, state):
        return call(
            functools.partial(gate_kernel, layer), [gate_t], [square, vector, vector, vector], (chain_rows,),
            (state, chain, *norms, w_gate), 2 * pairs * C * C,
        )[0]

    def products(recv, incoming):
        return call(
            functools.partial(products_kernel, incoming, rows), [back],
            [((width // 128, depth, 128), F32) for depth in (2 * HC * rows, width, HC * rows)], (),
            (recv,), 2 * channels * width**3,
        )[0]

    slabs, x_t = call(
        first_kernel, [sent, state_t], head, (mask_rows, chain_rows), (pair, mask, chain, *norms, w_ab),
        2 * pairs * C * 5 * HC,
    )
    recv = exchange(slabs)
    gate = gates(0, x_t)
    tri = exchange(products(recv, False))
    slabs, x_t = call(
        middle_kernel, [sent, state_t], head + tail, (mask_rows, chain_rows),
        (tri, gate, x_t, mask, chain, *norms, w_ab, *mids), 2 * pairs * C * 5 * HC,
    )
    recv = exchange(slabs)
    gate = gates(1, x_t)
    tri = exchange(products(recv, True))
    return call(
        last_kernel, [jax.ShapeDtypeStruct(pair.shape, BF16)], tail, (), (tri, gate, x_t, *mids), 2 * pairs * C * C
    )[0]


def solution(mesh):
    in_specs = (P(("grp", "row"), None, None), P("grp"), P("grp")) + (P(),) * 8
    out_specs = P(("grp", "row"), None, None)
    return jax.shard_map(local, mesh=mesh, in_specs=in_specs, out_specs=out_specs, check_vma=False)
```

```python
import functools

import jax
import jax.numpy as jnp
from jax import lax
from jax.experimental import pallas as pl
from jax.experimental.pallas import tpu as pltpu
from jax.sharding import PartitionSpec as P

C = 128
HC = 128
EPS = 1e-05
F32 = jnp.float32
BF16 = jnp.bfloat16
VMEM_LIMIT = 32 * 1024 * 1024
GROUP = 2

WHOLE = pl.BlockSpec(memory_space=pltpu.VMEM)
SCALARS = pl.BlockSpec(memory_space=pltpu.SMEM)
ANYWHERE = pl.BlockSpec(memory_space=pl.ANY)


def blocks(width):
    return [(j, slice(j * 128, (j + 1) * 128)) for j in range(width // 128)]


def column(vector_ref, layer):
    return jnp.broadcast_to(vector_ref[layer : layer + 1, :], (C, C)).T


def turn(ref):
    return ref[...].astype(F32).T.astype(BF16)


def norm_channels(values, gain, bias):
    mean = jnp.sum(values, axis=0, keepdims=True) * (1.0 / C)
    centred = values - mean
    var = jnp.sum(centred * centred, axis=0, keepdims=True) * (1.0 / C)
    return centred * lax.rsqrt(var + EPS) * gain + bias


def norm_input(values, same, g, b, e):
    return (norm_channels(values, g[...], b[...]) + same * e[...]).astype(BF16)


def same_chain(chain_ids, chain, place, columns):
    return (chain[:, columns] == chain_ids[place]).astype(F32)


def project(first, normed, masks, mask, w_t, slabs):
    rows = slabs.shape[1] // (2 * HC)
    width = slabs.shape[0] * 128
    proj = jnp.dot(w_t[...], normed, preferred_element_type=F32)
    for k, mask_row in enumerate(masks):
        for side in range(2):
            for j, columns in blocks(width):
                p = proj[2 * side * HC : (2 * side + 2) * HC, k * width + j * 128 : k * width + (j + 1) * 128]
                value = jax.nn.sigmoid(p[:HC]) * p[HC:] * (mask[:, columns] * mask_row)
                slabs[j, pl.ds(side * HC * rows + first + k, HC, stride=rows), :] = value


def write_slabs(slabs, out):
    devices, depth, width = out.shape
    half = depth // 2
    for side in range(2):
        for d in range(devices):
            start = (side * devices + d) * half
            for j, columns in blocks(width):
                out[d, side * half : (side + 1) * half, columns] = slabs[j, start : start + half, :].astype(BF16)


def widen(recv, wide):
    devices, depth, width = recv.shape
    for s in range(devices):
        for j, columns in blocks(width):
            wide[j, s * depth : (s + 1) * depth, :] = recv[s, :, columns].astype(F32)


def fetch(pairs, sems):
    copies = [pltpu.make_async_copy(src, dst, sems.at[i]) for i, (src, dst) in enumerate(pairs)]
    for copy in copies:
        copy.start()
    return copies


def groups(rows):
    return [range(i, min(i + GROUP, rows)) for i in range(0, rows, GROUP)]


def overlapped(rows, prepare, consume):
    todo = groups(rows)
    ready = prepare(todo[0])
    for i, group in enumerate(todo):
        current = ready
        if i + 1 < len(todo):
            ready = prepare(todo[i + 1])
        consume(group, current)


def first_kernel(
    residue_mask, chain_ids, marks, x_in, gain, bias, embed, w_ab, out, x_t,
    x, w, vectors, ids, w_t, g, b, e, slabs, sems, x_sems,
):
    rows, width, _ = x.shape
    start = lax.axis_index("row") * rows
    smalls = fetch(
        [(gain, vectors.at[0]), (bias, vectors.at[1]), (embed, vectors.at[2]), (marks, ids), (w_ab.at[0], w)], sems
    )
    larges = fetch([(x_in.at[pl.ds(r[0], len(r))], x.at[pl.ds(r[0], len(r))]) for r in groups(rows)], x_sems)
    for copy in smalls:
        copy.wait()
    w_t[...] = turn(w)
    g[...] = column(vectors.at[0], 0)
    b[...] = column(vectors.at[1], 0)
    e[...] = column(vectors.at[2], 0)
    mask = ids[0:1, :].astype(F32)
    chain = ids[1:2, :]

    def prepare(group):
        larges[group[0] // GROUP].wait()
        parts = []
        for r in group:
            for _, columns in blocks(width):
                values = x[r, columns, :].astype(F32).T
                x_t[r, :, columns] = values.astype(BF16)
                parts.append(norm_input(values, same_chain(chain_ids, chain, start + r, columns), g, b, e))
        return jnp.concatenate(parts, axis=1)

    def consume(group, normed):
        project(group[0], normed, [residue_mask[start + r].astype(F32) for r in group], mask, w_t, slabs)

    overlapped(rows, prepare, consume)
    write_slabs(slabs, out)


def gate_kernel(layer, chain_ids, marks, x_t, gain, bias, embed, w_gate, out, w, vectors, ids, w_t, g, b, e, sems):
    rows, _, width = x_t.shape
    start = lax.axis_index("row") * rows
    smalls = fetch(
        [(gain, vectors.at[0]), (bias, vectors.at[1]), (embed, vectors.at[2]), (marks, ids), (w_gate.at[layer], w)],
        sems,
    )
    for copy in smalls:
        copy.wait()
    w_t[...] = turn(w)
    g[...] = column(vectors.at[0], layer)
    b[...] = column(vectors.at[1], layer)
    e[...] = column(vectors.at[2], layer)
    chain = ids[1:2, :]

    def prepare(group):
        return jnp.concatenate(
            [
                norm_input(x_t[r, :, columns].astype(F32), same_chain(chain_ids, chain, start + r, columns), g, b, e)
                for r in group
                for _, columns in blocks(width)
            ],
            axis=1,
        )

    def consume(group, normed):
        gates = jax.nn.sigmoid(jnp.dot(w_t[...], normed, preferred_element_type=F32))
        for k, r in enumerate(group):
            out[r] = gates[:, k * width : (k + 1) * width]

    overlapped(rows, prepare, consume)


def products_kernel(incoming, rows, recv, out, wide, natural, turned):
    devices, depth, width = recv.shape
    channels = depth // (2 * rows)
    widen(recv, wide)

    def rows_of(side, c, r, j):
        return wide[j, pl.ds((side * channels + c) * rows + r, devices, stride=depth), :]

    def by_row(side, c):
        return jnp.concatenate(
            [
                jnp.concatenate([rows_of(side, c, r, j).astype(BF16) for r in range(rows)], axis=0)
                for j, _ in blocks(width)
            ],
            axis=1,
        )

    def put(c, r, j, values):
        turned[j, pl.ds(c * rows + r, devices, stride=channels * rows), :] = values

    for c in range(channels):
        left = by_row(0, c)
        if incoming:
            right = by_row(1, c)
            product = lax.dot_general(left, right, (((0,), (0,)), ((), ())), preferred_element_type=F32)
            for j, columns in blocks(width):
                natural[c, j] = product[:, columns]
                for r in range(rows):
                    put(c, r, j, natural[c, j, pl.ds(r, devices, stride=rows), :])
        else:
            for j, _ in blocks(width):
                for r in range(rows):
                    natural[c, j, pl.ds(r, devices, stride=rows), :] = rows_of(1, c, r, j)
            right = jnp.concatenate([natural[c, j].astype(BF16) for j, _ in blocks(width)], axis=1)
            product = lax.dot_general(left, right, (((1,), (1,)), ((), ())), preferred_element_type=F32)
            for j, columns in blocks(width):
                for r in range(rows):
                    put(c, r, j, product[r * devices : (r + 1) * devices, columns])
    for s in range(devices):
        for j, columns in blocks(width):
            out[s, :, columns] = turned[j, s * channels * rows : (s + 1) * channels * rows, :].astype(BF16)


def finish(group, width, tri, gate, x_t, g, b, w_t):
    rows = tri.shape[1] // HC
    normed = jnp.concatenate(
        [
            norm_channels(tri[j, pl.ds(r, HC, stride=rows), :], g[...], b[...]).astype(BF16)
            for r in group
            for j, _ in blocks(width)
        ],
        axis=1,
    )
    branch = jnp.dot(w_t[...], normed, preferred_element_type=F32)
    return {
        (r, j): (
            x_t[r, :, columns].astype(F32)
            + gate[r, :, columns] * branch[:, k * width + j * 128 : k * width + (j + 1) * 128]
        ).astype(BF16)
        for k, r in enumerate(group)
        for j, columns in blocks(width)
    }


def middle_kernel(
    residue_mask, chain_ids, recv, gate, x_t, marks, gain, bias, embed, w_ab, mid_gain, mid_bias, w_out, out, new_t,
    w, vectors, ids, w_t, g, b, e, slabs, w_mid, w_out_t, mg, mb, tri, sems,
):
    rows, _, width = x_t.shape
    start = lax.axis_index("row") * rows
    smalls = fetch(
        [
            (gain, vectors.at[0]), (bias, vectors.at[1]), (embed, vectors.at[2]), (marks, ids), (w_ab.at[1], w),
            (mid_gain, vectors.at[3]), (mid_bias, vectors.at[4]), (w_out.at[0], w_mid),
        ],
        sems,
    )
    widen(recv, tri)
    for copy in smalls:
        copy.wait()
    w_t[...] = turn(w)
    g[...] = column(vectors.at[0], 1)
    b[...] = column(vectors.at[1], 1)
    e[...] = column(vectors.at[2], 1)
    w_out_t[...] = turn(w_mid)
    mg[...] = column(vectors.at[3], 0)
    mb[...] = column(vectors.at[4], 0)
    mask = ids[0:1, :].astype(F32)
    chain = ids[1:2, :]

    def prepare(group):
        states = finish(group, width, tri, gate, x_t, mg, mb, w_out_t)
        parts = []
        for r in group:
            for j, columns in blocks(width):
                new_t[r, :, columns] = states[r, j]
                same = same_chain(chain_ids, chain, start + r, columns)
                parts.append(norm_input(states[r, j].astype(F32), same, g, b, e))
        return jnp.concatenate(parts, axis=1)

    def consume(group, normed):
        project(group[0], normed, [residue_mask[start + r].astype(F32) for r in group], mask, w_t, slabs)

    overlapped(rows, prepare, consume)
    write_slabs(slabs, out)


def last_kernel(recv, gate, x_t, mid_gain, mid_bias, w_out, out, vectors, w_mid, w_out_t, mg, mb, tri, sems):
    rows, _, width = x_t.shape
    smalls = fetch([(mid_gain, vectors.at[0]), (mid_bias, vectors.at[1]), (w_out.at[1], w_mid)], sems)
    widen(recv, tri)
    for copy in smalls:
        copy.wait()
    w_out_t[...] = turn(w_mid)
    mg[...] = column(vectors.at[0], 1)
    mb[...] = column(vectors.at[1], 1)
    for group in groups(rows):
        for (r, j), state in finish(group, width, tri, gate, x_t, mg, mb, w_out_t).items():
            out[r, j * 128 : (j + 1) * 128, :] = state.astype(F32).T.astype(BF16)


def call(kernel, outs, scratch, scalars, arrays, anywhere, flops):
    size = sum(a.size * a.dtype.itemsize for a in list(arrays) + list(outs))
    return pl.pallas_call(
        kernel,
        out_shape=outs,
        in_specs=[SCALARS] * len(scalars) + [WHOLE] * len(arrays) + [ANYWHERE] * len(anywhere),
        out_specs=[WHOLE] * len(outs),
        scratch_shapes=scratch,
        compiler_params=pltpu.CompilerParams(vmem_limit_bytes=VMEM_LIMIT),
        cost_estimate=pl.CostEstimate(flops=flops, bytes_accessed=size, transcendentals=0),
    )(*scalars, *arrays, *anywhere)


def local(
    pair, residue_mask, chain_ids, ln_in_gain, ln_in_bias, chain_embed, w_ab, w_gate, ln_mid_gain, ln_mid_bias, w_out
):
    rows, width, _ = pair.shape
    devices = lax.axis_size("row")
    channels = HC // devices
    cols = width // 128
    marks = jnp.stack([residue_mask, chain_ids])

    sent = jax.ShapeDtypeStruct((devices, 2 * channels * rows, width), BF16)
    back = jax.ShapeDtypeStruct((devices, channels * rows, width), BF16)
    state_t = jax.ShapeDtypeStruct((rows, C, width), BF16)
    gate_t = jax.ShapeDtypeStruct((rows, C, width), F32)
    vector = pltpu.VMEM((C, 128), F32)
    square = pltpu.VMEM((C, C), BF16)
    ids = pltpu.VMEM((2, width), jnp.int32)

    def vectors(n):
        return pltpu.VMEM((n, 2, C), F32)

    head = [
        pltpu.VMEM((4 * HC, C), BF16), vector, vector, vector, pltpu.VMEM((cols, 2 * HC * rows, 128), F32),
    ]
    w_raw = pltpu.VMEM((C, 4 * HC), BF16)
    tri_wide = pltpu.VMEM((cols, HC * rows, 128), F32)
    pairs = rows * width
    norms = (ln_in_gain, ln_in_bias, chain_embed)
    mids = (ln_mid_gain, ln_mid_bias, w_out)

    def sems(n):
        return pltpu.SemaphoreType.DMA((n,))

    def exchange(slabs):
        return lax.all_to_all(slabs, "row", split_axis=0, concat_axis=0, tiled=True)

    def gates(layer, state):
        def kernel(chain_ids, x_t, marks, *rest):
            gate_kernel(layer, chain_ids, marks, x_t, *rest)

        return call(
            kernel, [gate_t], [square, vectors(3), ids, square, vector, vector, vector, sems(5)], (chain_ids,),
            (state,), (marks, *norms, w_gate), 2 * pairs * C * C,
        )[0]

    def products(recv, incoming):
        return call(
            functools.partial(products_kernel, incoming, rows), [back],
            [
                pltpu.VMEM((cols, 2 * HC * rows, 128), F32),
                pltpu.VMEM((channels, cols, width, 128), F32),
                pltpu.VMEM((cols, HC * rows, 128), F32),
            ],
            (), (recv,), (), 2 * channels * width**3,
        )[0]

    slabs, x_t = call(
        first_kernel, [sent, state_t],
        [pltpu.VMEM(pair.shape, BF16), w_raw, vectors(3), ids, *head, sems(5), sems(len(groups(rows)))],
        (residue_mask, chain_ids), (), (marks, pair, *norms, w_ab), 2 * pairs * C * 5 * HC,
    )
    recv = exchange(slabs)
    gate = gates(0, x_t)
    tri = exchange(products(recv, False))
    slabs, x_t = call(
        middle_kernel, [sent, state_t],
        [w_raw, vectors(5), ids, *head, square, square, vector, vector, tri_wide, sems(8)],
        (residue_mask, chain_ids), (tri, gate, x_t), (marks, *norms, w_ab, *mids), 2 * pairs * C * 5 * HC,
    )
    recv = exchange(slabs)
    gate = gates(1, x_t)
    tri = exchange(products(recv, True))
    return call(
        last_kernel, [jax.ShapeDtypeStruct(pair.shape, BF16)],
        [vectors(2), square, square, vector, vector, tri_wide, sems(3)], (), (tri, gate, x_t), mids,
        2 * pairs * C * C,
    )[0]


def solution(mesh):
    in_specs = (P(("grp", "row"), None, None), P("grp"), P("grp")) + (P(),) * 8
    out_specs = P(("grp", "row"), None, None)
    return jax.shard_map(local, mesh=mesh, in_specs=in_specs, out_specs=out_specs, check_vma=False)
```

```python
import functools

import jax
import jax.numpy as jnp
from jax import lax
from jax.experimental import pallas as pl
from jax.experimental.pallas import tpu as pltpu
from jax.sharding import PartitionSpec as P

C = 128
HC = 128
EPS = 1e-05
F32 = jnp.float32
BF16 = jnp.bfloat16
VMEM_LIMIT = 32 * 1024 * 1024
FIRST_VMEM_LIMIT = 60 * 1024 * 1024
GROUP = 2

WHOLE = pl.BlockSpec(memory_space=pltpu.VMEM)
ANYWHERE = pl.BlockSpec(memory_space=pl.ANY)


def blocks(width):
    return [(j, slice(j * 128, (j + 1) * 128)) for j in range(width // 128)]


def column(vector_ref, layer):
    return jnp.broadcast_to(vector_ref[layer : layer + 1, :], (C, C)).T


def turn(ref):
    return ref[...].astype(F32).T.astype(BF16)


def norm_channels(values, gain, bias):
    mean = jnp.sum(values, axis=0, keepdims=True) * (1.0 / C)
    centred = values - mean
    var = jnp.sum(centred * centred, axis=0, keepdims=True) * (1.0 / C)
    return centred * lax.rsqrt(var + EPS) * gain + bias


def norm_input(values, same, g, b, e):
    return (norm_channels(values, g, b) + same * e).astype(BF16)


def same_chain(marks, row_marks, r, columns):
    return (marks[1:2, columns] == row_marks[1, r : r + 1, :]).astype(F32)


def project(group, normed, marks, row_marks, w_t, slabs):
    rows = slabs.shape[1] // (2 * HC)
    width = slabs.shape[0] * 128
    proj = jnp.dot(w_t, normed, preferred_element_type=F32)
    for k, r in enumerate(group):
        for j, columns in blocks(width):
            mask = marks[0:1, columns] * row_marks[0, r : r + 1, :]
            for side in range(2):
                p = proj[2 * side * HC : (2 * side + 2) * HC, k * width + j * 128 : k * width + (j + 1) * 128]
                value = jax.nn.sigmoid(p[:HC]) * p[HC:] * mask
                slabs[j, pl.ds(side * HC * rows + r, HC, stride=rows), :] = value


def write_slabs(slabs, out):
    devices, depth, width = out.shape
    half = depth // 2
    for side in range(2):
        for d in range(devices):
            start = (side * devices + d) * half
            for j, columns in blocks(width):
                out[d, side * half : (side + 1) * half, columns] = slabs[j, start : start + half, :].astype(BF16)


def widen(recv, wide):
    devices, depth, width = recv.shape
    for s in range(devices):
        for j, columns in blocks(width):
            wide[j, s * depth : (s + 1) * depth, :] = recv[s, :, columns].astype(F32)


def fetch(pairs, sems):
    copies = [pltpu.make_async_copy(src, dst, sems.at[i]) for i, (src, dst) in enumerate(pairs)]
    for copy in copies:
        copy.start()
    return copies


def groups(rows):
    return [range(i, min(i + GROUP, rows)) for i in range(0, rows, GROUP)]


def overlapped(rows, prepare, consume):
    todo = groups(rows)
    ready = prepare(todo[0])
    for i, group in enumerate(todo):
        current = ready
        if i + 1 < len(todo):
            ready = prepare(todo[i + 1])
        consume(group, current)


def first_kernel(
    residue_mask, chain_ids, x_in, gain, bias, embed, w_ab, out, x_t, marks, row_marks,
    x, w, vectors, mask_ids, chain, w_t, g, b, e, slabs, sems, x_sems,
):
    rows, width, _ = x.shape
    smalls = fetch(
        [
            (residue_mask, mask_ids), (chain_ids, chain), (gain, vectors.at[0]), (bias, vectors.at[1]),
            (embed, vectors.at[2]), (w_ab.at[0], w),
        ],
        sems,
    )
    larges = fetch([(x_in.at[pl.ds(r[0], len(r))], x.at[pl.ds(r[0], len(r))]) for r in groups(rows)], x_sems)
    for copy in smalls:
        copy.wait()
    w_t[...] = turn(w)
    g[...] = column(vectors.at[0], 0)
    b[...] = column(vectors.at[1], 0)
    e[...] = column(vectors.at[2], 0)
    shape = (row_marks.shape[1], width)
    start = lax.axis_index("row") * rows
    own = lax.broadcasted_iota(jnp.int32, shape, 1) == lax.broadcasted_iota(jnp.int32, shape, 0) + start
    for i, ref in enumerate((mask_ids, chain)):
        values = ref[...].astype(F32).reshape(1, width)
        marks[i : i + 1, :] = values
        picked = jnp.sum(jnp.where(own, values, 0.0), axis=1, keepdims=True)
        row_marks[i] = jnp.broadcast_to(picked, row_marks.shape[1:])

    def prepare(group):
        larges[group[0] // GROUP].wait()
        parts = []
        for r in group:
            for _, columns in blocks(width):
                values = x[r, columns, :].astype(F32).T
                x_t[r, :, columns] = values.astype(BF16)
                same = same_chain(marks, row_marks, r, columns)
                parts.append(norm_input(values, same, g[...], b[...], e[...]))
        return jnp.concatenate(parts, axis=1)

    def consume(group, normed):
        project(group, normed, marks, row_marks, w_t[...], slabs)

    overlapped(rows, prepare, consume)
    write_slabs(slabs, out)


def write_gates(x_t, marks, row_marks, g, b, e, w_t, out):
    rows, _, width = x_t.shape

    def prepare(group):
        return jnp.concatenate(
            [
                norm_input(x_t[r, :, columns].astype(F32), same_chain(marks, row_marks, r, columns), g, b, e)
                for r in group
                for _, columns in blocks(width)
            ],
            axis=1,
        )

    def consume(group, normed):
        gates = jax.nn.sigmoid(jnp.dot(w_t, normed, preferred_element_type=F32))
        for k, r in enumerate(group):
            out[r] = gates[:, k * width : (k + 1) * width]

    overlapped(rows, prepare, consume)


W_AB, W_OUT, W_GATE = slice(0, 4 * HC), [slice(4 * HC, 5 * HC), slice(5 * HC, 6 * HC)], slice(6 * HC, 7 * HC)
GAIN, BIAS, EMBED, MID_GAIN, MID_BIAS = 0, 1, 2, [3, 5], [4, 6]


def gate_kernel(
    x_t, marks, row_marks, gain, bias, embed, w_gate, w_ab, mid_gain, mid_bias, w_out, out, weights, columns_out,
    vectors, w_square, w_wide, sems,
):
    copies = fetch(
        [
            (gain, vectors.at[0]), (bias, vectors.at[1]), (embed, vectors.at[2]), (mid_gain, vectors.at[3]),
            (mid_bias, vectors.at[4]), (w_gate, w_square.at[0]), (w_out, w_square.at[1]), (w_ab.at[1], w_wide),
        ],
        sems,
    )
    for copy in copies:
        copy.wait()
    weights[W_AB, :] = turn(w_wide)
    weights[W_GATE, :] = turn(w_square.at[0, 1])
    for layer in range(2):
        weights[W_OUT[layer], :] = turn(w_square.at[1, layer])
        columns_out[MID_GAIN[layer]] = column(vectors.at[3], layer)
        columns_out[MID_BIAS[layer]] = column(vectors.at[4], layer)
    for i in (GAIN, BIAS, EMBED):
        columns_out[i] = column(vectors.at[i], 1)
    first = [column(vectors.at[i], 0) for i in (GAIN, BIAS, EMBED)]
    write_gates(x_t, marks, row_marks, *first, turn(w_square.at[0, 0]), out)


def second_gate_kernel(x_t, marks, row_marks, weights, columns, out):
    write_gates(x_t, marks, row_marks, columns[GAIN], columns[BIAS], columns[EMBED], weights[W_GATE, :], out)


def products_kernel(incoming, rows, recv, out, wide, natural, turned):
    devices, depth, width = recv.shape
    channels = depth // (2 * rows)
    widen(recv, wide)

    def rows_of(side, c, r, j):
        return wide[j, pl.ds((side * channels + c) * rows + r, devices, stride=depth), :]

    def by_row(side, c):
        return jnp.concatenate(
            [
                jnp.concatenate([rows_of(side, c, r, j).astype(BF16) for r in range(rows)], axis=0)
                for j, _ in blocks(width)
            ],
            axis=1,
        )

    def put(c, r, j, values):
        turned[j, pl.ds(c * rows + r, devices, stride=channels * rows), :] = values

    for c in range(channels):
        left = by_row(0, c)
        if incoming:
            right = by_row(1, c)
            product = lax.dot_general(left, right, (((0,), (0,)), ((), ())), preferred_element_type=F32)
            for j, columns in blocks(width):
                natural[c, j] = product[:, columns]
                for r in range(rows):
                    put(c, r, j, natural[c, j, pl.ds(r, devices, stride=rows), :])
        else:
            for j, _ in blocks(width):
                for r in range(rows):
                    natural[c, j, pl.ds(r, devices, stride=rows), :] = rows_of(1, c, r, j)
            right = jnp.concatenate([natural[c, j].astype(BF16) for j, _ in blocks(width)], axis=1)
            product = lax.dot_general(left, right, (((1,), (1,)), ((), ())), preferred_element_type=F32)
            for j, columns in blocks(width):
                for r in range(rows):
                    put(c, r, j, product[r * devices : (r + 1) * devices, columns])
    for s in range(devices):
        for j, columns in blocks(width):
            out[s, :, columns] = turned[j, s * channels * rows : (s + 1) * channels * rows, :].astype(BF16)


def finish(layer, group, width, tri, gate, x_t, weights, vectors):
    rows = tri.shape[1] // HC
    gain, bias = vectors[MID_GAIN[layer]], vectors[MID_BIAS[layer]]
    normed = jnp.concatenate(
        [
            norm_channels(tri[j, pl.ds(r, HC, stride=rows), :], gain, bias).astype(BF16)
            for r in group
            for j, _ in blocks(width)
        ],
        axis=1,
    )
    branch = jnp.dot(weights[W_OUT[layer], :], normed, preferred_element_type=F32)
    return {
        (r, j): (
            x_t[r, :, columns].astype(F32)
            + gate[r, :, columns] * branch[:, k * width + j * 128 : k * width + (j + 1) * 128]
        ).astype(BF16)
        for k, r in enumerate(group)
        for j, columns in blocks(width)
    }


def middle_kernel(recv, gate, x_t, marks, row_marks, weights, vectors, out, new_t, slabs, tri):
    rows, _, width = x_t.shape
    widen(recv, tri)

    def prepare(group):
        states = finish(0, group, width, tri, gate, x_t, weights, vectors)
        parts = []
        for r in group:
            for j, columns in blocks(width):
                new_t[r, :, columns] = states[r, j]
                same = same_chain(marks, row_marks, r, columns)
                parts.append(
                    norm_input(states[r, j].astype(F32), same, vectors[GAIN], vectors[BIAS], vectors[EMBED])
                )
        return jnp.concatenate(parts, axis=1)

    def consume(group, normed):
        project(group, normed, marks, row_marks, weights[W_AB, :], slabs)

    overlapped(rows, prepare, consume)
    write_slabs(slabs, out)


def last_kernel(recv, gate, x_t, weights, vectors, out, tri):
    rows, _, width = x_t.shape
    widen(recv, tri)
    for group in groups(rows):
        for (r, j), state in finish(1, group, width, tri, gate, x_t, weights, vectors).items():
            out[r, j * 128 : (j + 1) * 128, :] = state.astype(F32).T.astype(BF16)


def call(kernel, outs, scratch, arrays, anywhere, flops, limit=VMEM_LIMIT):
    size = sum(a.size * a.dtype.itemsize for a in list(arrays) + list(outs))
    return pl.pallas_call(
        kernel,
        out_shape=outs,
        in_specs=[WHOLE] * len(arrays) + [ANYWHERE] * len(anywhere),
        out_specs=[WHOLE] * len(outs),
        scratch_shapes=scratch,
        compiler_params=pltpu.CompilerParams(vmem_limit_bytes=limit),
        cost_estimate=pl.CostEstimate(flops=flops, bytes_accessed=size, transcendentals=0),
    )(*arrays, *anywhere)


def local(
    pair, residue_mask, chain_ids, ln_in_gain, ln_in_bias, chain_embed, w_ab, w_gate, ln_mid_gain, ln_mid_bias, w_out
):
    rows, width, _ = pair.shape
    devices = lax.axis_size("row")
    channels = HC // devices
    cols = width // 128
    pairs = rows * width

    sent = jax.ShapeDtypeStruct((devices, 2 * channels * rows, width), BF16)
    back = jax.ShapeDtypeStruct((devices, channels * rows, width), BF16)
    state_t = jax.ShapeDtypeStruct((rows, C, width), BF16)
    gate_t = jax.ShapeDtypeStruct((rows, C, width), F32)
    mark = jax.ShapeDtypeStruct((2, width), F32)
    row_mark = jax.ShapeDtypeStruct((2, (rows + 7) // 8 * 8, 128), F32)
    turned = jax.ShapeDtypeStruct((7 * HC, C), BF16)
    columns = jax.ShapeDtypeStruct((7, C, 128), F32)

    vector = pltpu.VMEM((C, 128), F32)
    ids = pltpu.VMEM((width,), jnp.int32)
    w_wide = pltpu.VMEM((C, 4 * HC), BF16)
    slabs_wide = pltpu.VMEM((cols, 2 * HC * rows, 128), F32)
    tri_wide = pltpu.VMEM((cols, HC * rows, 128), F32)
    norms = (ln_in_gain, ln_in_bias, chain_embed)

    def sems(n):
        return pltpu.SemaphoreType.DMA((n,))

    def exchange(slabs):
        return lax.all_to_all(slabs, "row", split_axis=0, concat_axis=0, tiled=True)

    def products(recv, incoming):
        return call(
            functools.partial(products_kernel, incoming, rows), [back],
            [slabs_wide, pltpu.VMEM((channels, cols, width, 128), F32), tri_wide], (recv,), (),
            2 * channels * width**3,
        )[0]

    slabs, x_t, marks, row_marks = call(
        first_kernel, [sent, state_t, mark, row_mark],
        [
            pltpu.VMEM(pair.shape, BF16), w_wide, pltpu.VMEM((3, 2, C), F32), ids, ids, pltpu.VMEM((4 * HC, C), BF16),
            vector, vector, vector, slabs_wide, sems(6), sems(len(groups(rows))),
        ],
        (), (residue_mask, chain_ids, pair, *norms, w_ab), 2 * pairs * C * 4 * HC, FIRST_VMEM_LIMIT,
    )
    recv = exchange(slabs)
    gate, weights, vectors = call(
        gate_kernel, [gate_t, turned, columns],
        [pltpu.VMEM((5, 2, C), F32), pltpu.VMEM((2, 2, C, C), BF16), w_wide, sems(8)],
        (x_t, marks, row_marks), (*norms, w_gate, w_ab, ln_mid_gain, ln_mid_bias, w_out), 2 * pairs * C * C,
    )
    tri = exchange(products(recv, False))
    slabs, x_t = call(
        middle_kernel, [sent, state_t], [slabs_wide, tri_wide],
        (tri, gate, x_t, marks, row_marks, weights, vectors), (), 2 * pairs * C * 5 * HC,
    )
    recv = exchange(slabs)
    gate = call(
        second_gate_kernel, [gate_t], [], (x_t, marks, row_marks, weights, vectors), (), 2 * pairs * C * C
    )[0]
    tri = exchange(products(recv, True))
    return call(
        last_kernel, [jax.ShapeDtypeStruct(pair.shape, BF16)], [tri_wide], (tri, gate, x_t, weights, vectors), (),
        2 * pairs * C * C,
    )[0]


def solution(mesh):
    in_specs = (P(("grp", "row"), None, None), P("grp"), P("grp")) + (P(),) * 8
    out_specs = P(("grp", "row"), None, None)
    return jax.shard_map(local, mesh=mesh, in_specs=in_specs, out_specs=out_specs, check_vma=False)
```

```python
import functools

import jax
import jax.numpy as jnp
from jax import lax
from jax.experimental import pallas as pl
from jax.experimental.pallas import tpu as pltpu
from jax.sharding import PartitionSpec as P

C = 128
HC = 128
EPS = 1e-05
F32 = jnp.float32
BF16 = jnp.bfloat16
VMEM_LIMIT = 32 * 1024 * 1024
PRODUCTS_VMEM_LIMIT = 48 * 1024 * 1024
FIRST_VMEM_LIMIT = 60 * 1024 * 1024
GROUP = 2

WHOLE = pl.BlockSpec(memory_space=pltpu.VMEM)
ANYWHERE = pl.BlockSpec(memory_space=pl.ANY)


def blocks(width):
    return [(j, slice(j * 128, (j + 1) * 128)) for j in range(width // 128)]


def column(vector_ref, layer):
    return jnp.broadcast_to(vector_ref[layer : layer + 1, :], (C, C)).T


def turn(ref):
    return ref[...].astype(F32).T.astype(BF16)


def norm_channels(values, gain, bias):
    mean = jnp.sum(values, axis=0, keepdims=True) * (1.0 / C)
    centred = values - mean
    var = jnp.sum(centred * centred, axis=0, keepdims=True) * (1.0 / C)
    return centred * lax.rsqrt(var + EPS) * gain + bias


def norm_input(values, same, g, b, e):
    return (norm_channels(values, g, b) + same * e).astype(BF16)


def same_chain(marks, row_marks, r, columns):
    return (marks[1:2, columns] == row_marks[1, r : r + 1, :]).astype(F32)


def project(group, normed, marks, row_marks, w_t, slabs):
    rows = slabs.shape[1] // (2 * HC)
    width = slabs.shape[0] * 128
    proj = jnp.dot(w_t, normed, preferred_element_type=F32)
    for k, r in enumerate(group):
        for j, columns in blocks(width):
            mask = marks[0:1, columns] * row_marks[0, r : r + 1, :]
            for side in range(2):
                p = proj[2 * side * HC : (2 * side + 2) * HC, k * width + j * 128 : k * width + (j + 1) * 128]
                value = jax.nn.sigmoid(p[:HC]) * p[HC:] * mask
                slabs[j, pl.ds(side * HC * rows + r, HC, stride=rows), :] = value


def write_slabs(slabs, out):
    devices, depth, width = out.shape
    half = depth // 2
    for side in range(2):
        for d in range(devices):
            start = (side * devices + d) * half
            for j, columns in blocks(width):
                out[d, side * half : (side + 1) * half, columns] = slabs[j, start : start + half, :].astype(BF16)


def write_crossing(slabs, out, own):
    devices, depth, width = out.shape
    half = devices // 2
    me = lax.axis_index("row")
    side_rows = half * depth
    for d in range(devices):
        side = jnp.where(me // half == d // half, 0, side_rows)
        start = pl.multiple_of(side + d % half * depth, 8)
        for j, columns in blocks(width):
            out[d, :, columns] = slabs[j, pl.ds(start, depth), :].astype(BF16)
    for o, ref in enumerate(own):
        start = pl.multiple_of(side_rows + (me % half ^ o) * depth, 8)
        for j, columns in blocks(width):
            ref[:, columns] = slabs[j, pl.ds(start, depth), :].astype(BF16)


def widen(recv, wide):
    devices, depth, width = recv.shape
    for s in range(devices):
        for j, columns in blocks(width):
            wide[j, s * depth : (s + 1) * depth, :] = recv[s, :, columns].astype(F32)


def fetch(pairs, sems):
    copies = [pltpu.make_async_copy(src, dst, sems.at[i]) for i, (src, dst) in enumerate(pairs)]
    for copy in copies:
        copy.start()
    return copies


def groups(rows):
    return [range(i, min(i + GROUP, rows)) for i in range(0, rows, GROUP)]


def overlapped(rows, prepare, consume):
    todo = groups(rows)
    ready = prepare(todo[0])
    for i, group in enumerate(todo):
        current = ready
        if i + 1 < len(todo):
            ready = prepare(todo[i + 1])
        consume(group, current)


def first_kernel(residue_mask, chain_ids, x_in, gain, bias, embed, w_ab, *refs):
    own = refs[:-16]
    out, x_t, marks, row_marks, x, w, vectors, mask_ids, chain, w_t, g, b, e, slabs, sems, x_sems = refs[-16:]
    rows, width, _ = x.shape
    smalls = fetch(
        [
            (residue_mask, mask_ids), (chain_ids, chain), (gain, vectors.at[0]), (bias, vectors.at[1]),
            (embed, vectors.at[2]), (w_ab.at[0], w),
        ],
        sems,
    )
    larges = fetch([(x_in.at[pl.ds(r[0], len(r))], x.at[pl.ds(r[0], len(r))]) for r in groups(rows)], x_sems)
    for copy in smalls:
        copy.wait()
    w_t[...] = turn(w)
    g[...] = column(vectors.at[0], 0)
    b[...] = column(vectors.at[1], 0)
    e[...] = column(vectors.at[2], 0)
    shape = (row_marks.shape[1], width)
    start = lax.axis_index("row") * rows
    at_row = lax.broadcasted_iota(jnp.int32, shape, 1) == lax.broadcasted_iota(jnp.int32, shape, 0) + start
    for i, ref in enumerate((mask_ids, chain)):
        values = ref[...].astype(F32).reshape(1, width)
        marks[i : i + 1, :] = values
        picked = jnp.sum(jnp.where(at_row, values, 0.0), axis=1, keepdims=True)
        row_marks[i] = jnp.broadcast_to(picked, row_marks.shape[1:])

    def prepare(group):
        larges[group[0] // GROUP].wait()
        parts = []
        for r in group:
            for _, columns in blocks(width):
                values = x[r, columns, :].astype(F32).T
                x_t[r, :, columns] = values.astype(BF16)
                same = same_chain(marks, row_marks, r, columns)
                parts.append(norm_input(values, same, g[...], b[...], e[...]))
        return jnp.concatenate(parts, axis=1)

    def consume(group, normed):
        project(group, normed, marks, row_marks, w_t[...], slabs)

    overlapped(rows, prepare, consume)
    write_crossing(slabs, out, own)


def write_gates(x_t, marks, row_marks, g, b, e, w_t, out):
    rows, _, width = x_t.shape

    def prepare(group):
        return jnp.concatenate(
            [
                norm_input(x_t[r, :, columns].astype(F32), same_chain(marks, row_marks, r, columns), g, b, e)
                for r in group
                for _, columns in blocks(width)
            ],
            axis=1,
        )

    def consume(group, normed):
        gates = jax.nn.sigmoid(jnp.dot(w_t, normed, preferred_element_type=F32))
        for k, r in enumerate(group):
            out[r] = gates[:, k * width : (k + 1) * width]

    overlapped(rows, prepare, consume)


W_AB, W_OUT, W_GATE = slice(0, 4 * HC), [slice(4 * HC, 5 * HC), slice(5 * HC, 6 * HC)], slice(6 * HC, 7 * HC)
GAIN, BIAS, EMBED, MID_GAIN, MID_BIAS = 0, 1, 2, [3, 5], [4, 6]


def gate_kernel(
    x_t, marks, row_marks, gain, bias, embed, w_gate, w_ab, mid_gain, mid_bias, w_out, out, weights, columns_out,
    vectors, w_square, w_wide, sems,
):
    copies = fetch(
        [
            (gain, vectors.at[0]), (bias, vectors.at[1]), (embed, vectors.at[2]), (mid_gain, vectors.at[3]),
            (mid_bias, vectors.at[4]), (w_gate, w_square.at[0]), (w_out, w_square.at[1]), (w_ab.at[1], w_wide),
        ],
        sems,
    )
    for copy in copies:
        copy.wait()
    weights[W_AB, :] = turn(w_wide)
    weights[W_GATE, :] = turn(w_square.at[0, 1])
    for layer in range(2):
        weights[W_OUT[layer], :] = turn(w_square.at[1, layer])
        columns_out[MID_GAIN[layer]] = column(vectors.at[3], layer)
        columns_out[MID_BIAS[layer]] = column(vectors.at[4], layer)
    for i in (GAIN, BIAS, EMBED):
        columns_out[i] = column(vectors.at[i], 1)
    first = [column(vectors.at[i], 0) for i in (GAIN, BIAS, EMBED)]
    write_gates(x_t, marks, row_marks, *first, turn(w_square.at[0, 0]), out)


def second_gate_kernel(x_t, marks, row_marks, weights, columns, out):
    write_gates(x_t, marks, row_marks, columns[GAIN], columns[BIAS], columns[EMBED], weights[W_GATE, :], out)


def first_products_kernel(rows, recv, *refs):
    own, (out, left_wide, right_wide, natural, turned) = refs[:-5], refs[-5:]
    devices, depth, width = recv.shape
    half = devices // 2
    channels = depth // rows
    me = lax.axis_index("row")
    mine = me // half * half
    other = half - mine
    for q in range(half):
        to_other = pl.multiple_of((other + q) * depth, 8)
        to_own = pl.multiple_of((mine + (me % half ^ q)) * depth, 8)
        for j, columns in blocks(width):
            left_wide[j, q * depth : (q + 1) * depth, :] = recv[mine + q, :, columns].astype(F32)
            right_wide[j, pl.ds(to_other, depth), :] = recv[other + q, :, columns].astype(F32)
            right_wide[j, pl.ds(to_own, depth), :] = own[q][:, columns].astype(F32)
    for c in range(channels):
        left, right = [], []
        for j, _ in blocks(width):
            pieces = [left_wide[j, pl.ds(c * rows + r, half, stride=depth), :].astype(BF16) for r in range(rows)]
            left.append(jnp.concatenate(pieces, axis=0))
            for r in range(rows):
                natural[c, j, pl.ds(r, devices, stride=rows), :] = right_wide[
                    j, pl.ds(c * rows + r, devices, stride=depth), :
                ]
            right.append(natural[c, j].astype(BF16))
        product = lax.dot_general(
            jnp.concatenate(left, axis=1), jnp.concatenate(right, axis=1), (((1,), (1,)), ((), ())),
            preferred_element_type=F32,
        )
        for j, columns in blocks(width):
            for r in range(rows):
                turned[j, pl.ds(c * rows + r, half, stride=depth), :] = product[r * half : (r + 1) * half, columns]
    for q in range(half):
        for j, columns in blocks(width):
            out[q, :, columns] = turned[j, q * depth : (q + 1) * depth, :].astype(BF16)


def second_products_kernel(rows, recv, out, wide, natural, turned):
    devices, depth, width = recv.shape
    channels = depth // (2 * rows)
    widen(recv, wide)

    def by_row(side, c):
        return jnp.concatenate(
            [
                jnp.concatenate(
                    [
                        wide[j, pl.ds((side * channels + c) * rows + r, devices, stride=depth), :].astype(BF16)
                        for r in range(rows)
                    ],
                    axis=0,
                )
                for j, _ in blocks(width)
            ],
            axis=1,
        )

    for c in range(channels):
        product = lax.dot_general(
            by_row(0, c), by_row(1, c), (((0,), (0,)), ((), ())), preferred_element_type=F32
        )
        for j, columns in blocks(width):
            natural[c, j] = product[:, columns]
            for r in range(rows):
                turned[j, pl.ds(c * rows + r, devices, stride=channels * rows), :] = natural[
                    c, j, pl.ds(r, devices, stride=rows), :
                ]
    for s in range(devices):
        for j, columns in blocks(width):
            out[s, :, columns] = turned[j, s * channels * rows : (s + 1) * channels * rows, :].astype(BF16)


def finish(layer, group, width, tri, gate, x_t, weights, vectors):
    rows = tri.shape[1] // HC
    gain, bias = vectors[MID_GAIN[layer]], vectors[MID_BIAS[layer]]
    normed = jnp.concatenate(
        [
            norm_channels(tri[j, pl.ds(r, HC, stride=rows), :], gain, bias).astype(BF16)
            for r in group
            for j, _ in blocks(width)
        ],
        axis=1,
    )
    branch = jnp.dot(weights[W_OUT[layer], :], normed, preferred_element_type=F32)
    return {
        (r, j): (
            x_t[r, :, columns].astype(F32)
            + gate[r, :, columns] * branch[:, k * width + j * 128 : k * width + (j + 1) * 128]
        ).astype(BF16)
        for k, r in enumerate(group)
        for j, columns in blocks(width)
    }


def middle_kernel(recv, gate, x_t, marks, row_marks, weights, vectors, out, new_t, slabs, tri):
    rows, _, width = x_t.shape
    widen(recv, tri)

    def prepare(group):
        states = finish(0, group, width, tri, gate, x_t, weights, vectors)
        parts = []
        for r in group:
            for j, columns in blocks(width):
                new_t[r, :, columns] = states[r, j]
                same = same_chain(marks, row_marks, r, columns)
                parts.append(
                    norm_input(states[r, j].astype(F32), same, vectors[GAIN], vectors[BIAS], vectors[EMBED])
                )
        return jnp.concatenate(parts, axis=1)

    def consume(group, normed):
        project(group, normed, marks, row_marks, weights[W_AB, :], slabs)

    overlapped(rows, prepare, consume)
    write_slabs(slabs, out)


def last_kernel(recv, gate, x_t, weights, vectors, out, tri):
    rows, _, width = x_t.shape
    widen(recv, tri)
    for group in groups(rows):
        for (r, j), state in finish(1, group, width, tri, gate, x_t, weights, vectors).items():
            out[r, j * 128 : (j + 1) * 128, :] = state.astype(F32).T.astype(BF16)


def call(kernel, outs, scratch, arrays, anywhere, flops, limit=VMEM_LIMIT):
    size = sum(a.size * a.dtype.itemsize for a in list(arrays) + list(outs))
    return pl.pallas_call(
        kernel,
        out_shape=outs,
        in_specs=[WHOLE] * len(arrays) + [ANYWHERE] * len(anywhere),
        out_specs=[WHOLE] * len(outs),
        scratch_shapes=scratch,
        compiler_params=pltpu.CompilerParams(vmem_limit_bytes=limit),
        cost_estimate=pl.CostEstimate(flops=flops, bytes_accessed=size, transcendentals=0),
    )(*arrays, *anywhere)


def local(
    pair, residue_mask, chain_ids, ln_in_gain, ln_in_bias, chain_embed, w_ab, w_gate, ln_mid_gain, ln_mid_bias, w_out
):
    rows, width, _ = pair.shape
    devices = lax.axis_size("row")
    half = devices // 2
    channels = HC // devices
    cols = width // 128
    pairs = rows * width

    sent = jax.ShapeDtypeStruct((devices, 2 * channels * rows, width), BF16)
    back = jax.ShapeDtypeStruct((devices, channels * rows, width), BF16)
    own_back = jax.ShapeDtypeStruct((half, 2 * channels * rows, width), BF16)
    own_slab = jax.ShapeDtypeStruct((2 * channels * rows, width), BF16)
    state_t = jax.ShapeDtypeStruct((rows, C, width), BF16)
    gate_t = jax.ShapeDtypeStruct((rows, C, width), F32)
    mark = jax.ShapeDtypeStruct((2, width), F32)
    row_mark = jax.ShapeDtypeStruct((2, (rows + 7) // 8 * 8, 128), F32)
    turned = jax.ShapeDtypeStruct((7 * HC, C), BF16)
    columns = jax.ShapeDtypeStruct((7, C, 128), F32)

    vector = pltpu.VMEM((C, 128), F32)
    ids = pltpu.VMEM((width,), jnp.int32)
    w_wide = pltpu.VMEM((C, 4 * HC), BF16)
    slabs_wide = pltpu.VMEM((cols, 2 * HC * rows, 128), F32)
    tri_wide = pltpu.VMEM((cols, HC * rows, 128), F32)
    norms = (ln_in_gain, ln_in_bias, chain_embed)

    def sems(n):
        return pltpu.SemaphoreType.DMA((n,))

    def exchange(slabs, groups=None):
        return lax.all_to_all(
            slabs, "row", split_axis=0, concat_axis=0, tiled=True, axis_index_groups=groups
        )

    halves = [list(range(h * half, (h + 1) * half)) for h in range(2)]
    *own, slabs, x_t, marks, row_marks = call(
        first_kernel, [own_slab] * half + [sent, state_t, mark, row_mark],
        [
            pltpu.VMEM(pair.shape, BF16), w_wide, pltpu.VMEM((3, 2, C), F32), ids, ids, pltpu.VMEM((4 * HC, C), BF16),
            vector, vector, vector, slabs_wide, sems(6), sems(len(groups(rows))),
        ],
        (), (residue_mask, chain_ids, pair, *norms, w_ab), 2 * pairs * C * 4 * HC, FIRST_VMEM_LIMIT,
    )
    recv = exchange(slabs)
    own = [own[0]] + [lax.ppermute(own[o], "row", [(i, i ^ o) for i in range(devices)]) for o in range(1, half)]
    gate, weights, vectors = call(
        gate_kernel, [gate_t, turned, columns],
        [pltpu.VMEM((5, 2, C), F32), pltpu.VMEM((2, 2, C, C), BF16), w_wide, sems(8)],
        (x_t, marks, row_marks), (*norms, w_gate, w_ab, ln_mid_gain, ln_mid_bias, w_out), 2 * pairs * C * C,
    )
    products = call(
        functools.partial(first_products_kernel, rows), [own_back],
        [
            tri_wide, slabs_wide, pltpu.VMEM((2 * channels, cols, width, 128), F32), tri_wide,
        ],
        (recv, *own), (), 2 * channels * width**3, PRODUCTS_VMEM_LIMIT,
    )[0]
    tri = exchange(products, halves)
    slabs, x_t = call(
        middle_kernel, [sent, state_t], [slabs_wide, tri_wide],
        (tri, gate, x_t, marks, row_marks, weights, vectors), (), 2 * pairs * C * 5 * HC,
    )
    recv = exchange(slabs)
    gate = call(
        second_gate_kernel, [gate_t], [], (x_t, marks, row_marks, weights, vectors), (), 2 * pairs * C * C
    )[0]
    products = call(
        functools.partial(second_products_kernel, rows), [back],
        [slabs_wide, pltpu.VMEM((channels, cols, width, 128), F32), tri_wide], (recv,), (), 2 * channels * width**3,
    )[0]
    tri = exchange(products)
    return call(
        last_kernel, [jax.ShapeDtypeStruct(pair.shape, BF16)], [tri_wide], (tri, gate, x_t, weights, vectors), (),
        2 * pairs * C * C,
    )[0]


def solution(mesh):
    in_specs = (P(("grp", "row"), None, None), P("grp"), P("grp")) + (P(),) * 8
    out_specs = P(("grp", "row"), None, None)
    return jax.shard_map(local, mesh=mesh, in_specs=in_specs, out_specs=out_specs, check_vma=False)
```

```python
import functools

import jax
import jax.numpy as jnp
from jax import lax
from jax.experimental import pallas as pl
from jax.experimental.pallas import tpu as pltpu
from jax.sharding import PartitionSpec as P

C = 128
HC = 128
EPS = 1e-05
F32 = jnp.float32
BF16 = jnp.bfloat16
VMEM_LIMIT = 32 * 1024 * 1024
PRODUCTS_VMEM_LIMIT = 48 * 1024 * 1024
FIRST_VMEM_LIMIT = 60 * 1024 * 1024
GROUP = 2

WHOLE = pl.BlockSpec(memory_space=pltpu.VMEM)
ANYWHERE = pl.BlockSpec(memory_space=pl.ANY)


def blocks(width):
    return [(j, slice(j * 128, (j + 1) * 128)) for j in range(width // 128)]


def column(vector_ref, layer):
    return jnp.broadcast_to(vector_ref[layer : layer + 1, :], (C, C)).T


def turn(ref):
    return ref[...].astype(F32).T.astype(BF16)


def norm_channels(values, gain, bias):
    mean = jnp.sum(values, axis=0, keepdims=True) * (1.0 / C)
    centred = values - mean
    var = jnp.sum(centred * centred, axis=0, keepdims=True) * (1.0 / C)
    return centred * lax.rsqrt(var + EPS) * gain + bias


def norm_input(values, same, g, b, e):
    return (norm_channels(values, g, b) + same * e).astype(BF16)


def same_chain(marks, row_marks, r, columns):
    return (marks[1:2, columns] == row_marks[1, r : r + 1, :]).astype(F32)


def project(group, normed, marks, row_marks, w_t, slabs):
    rows = slabs.shape[1] // (2 * HC)
    width = slabs.shape[0] * 128
    proj = jnp.dot(w_t, normed, preferred_element_type=F32)
    for k, r in enumerate(group):
        for j, columns in blocks(width):
            mask = marks[0:1, columns] * row_marks[0, r : r + 1, :]
            for side in range(2):
                p = proj[2 * side * HC : (2 * side + 2) * HC, k * width + j * 128 : k * width + (j + 1) * 128]
                value = jax.nn.sigmoid(p[:HC]) * p[HC:] * mask
                slabs[j, pl.ds(side * HC * rows + r, HC, stride=rows), :] = value


def write_slabs(slabs, out):
    devices, depth, width = out.shape
    half = depth // 2
    for side in range(2):
        for d in range(devices):
            start = (side * devices + d) * half
            for j, columns in blocks(width):
                out[d, side * half : (side + 1) * half, columns] = slabs[j, start : start + half, :].astype(BF16)


def write_crossing(slabs, left, right, out, own, sems):
    half, depth, width = left.shape
    me = lax.axis_index("row")
    mine = me // half * half
    copies = []

    def send(src, dst):
        copies.append(pltpu.make_async_copy(src, dst, sems.at[len(copies)]))
        copies[-1].start()

    parts = [slice(q, min(q + half // 4, half)) for q in range(0, half, half // 4)]
    for side, ref, first in ((1, right, half - mine), (0, left, mine)):
        for part in parts:
            for q in range(part.start, part.stop):
                start = (side * half + q) * depth
                for j, columns in blocks(width):
                    ref[q, :, columns] = slabs[j, start : start + depth, :].astype(BF16)
            size = part.stop - part.start
            send(ref.at[pl.ds(part.start, size)], out.at[pl.ds(first + part.start, size)])
        if side == 1:
            for o, dst in enumerate(own):
                send(ref.at[me % half ^ o], dst)
    for copy in copies:
        copy.wait()


def widen(recv, wide):
    devices, depth, width = recv.shape
    for s in range(devices):
        for j, columns in blocks(width):
            wide[j, s * depth : (s + 1) * depth, :] = recv[s, :, columns].astype(F32)


def fetch(pairs, sems):
    copies = [pltpu.make_async_copy(src, dst, sems.at[i]) for i, (src, dst) in enumerate(pairs)]
    for copy in copies:
        copy.start()
    return copies


def groups(rows):
    return [range(i, min(i + GROUP, rows)) for i in range(0, rows, GROUP)]


def overlapped(rows, prepare, consume):
    todo = groups(rows)
    ready = prepare(todo[0])
    for i, group in enumerate(todo):
        current = ready
        if i + 1 < len(todo):
            ready = prepare(todo[i + 1])
        consume(group, current)


def first_kernel(residue_mask, chain_ids, x_in, gain, bias, embed, w_ab, *refs):
    own, (out, x_out, marks, row_marks) = refs[:-20], refs[-20:-16]
    x, x_t, w, vectors, mask_ids, chain, w_t, g, b, e, slabs, left, right, sems, x_sems, out_sems = refs[-16:]
    rows, width, _ = x.shape
    smalls = fetch(
        [
            (residue_mask, mask_ids), (chain_ids, chain), (gain, vectors.at[0]), (bias, vectors.at[1]),
            (embed, vectors.at[2]), (w_ab.at[0], w),
        ],
        sems,
    )
    larges = fetch([(x_in.at[pl.ds(r[0], len(r))], x.at[pl.ds(r[0], len(r))]) for r in groups(rows)], x_sems)
    for copy in smalls:
        copy.wait()
    w_t[...] = turn(w)
    g[...] = column(vectors.at[0], 0)
    b[...] = column(vectors.at[1], 0)
    e[...] = column(vectors.at[2], 0)
    shape = (row_marks.shape[1], width)
    start = lax.axis_index("row") * rows
    at_row = lax.broadcasted_iota(jnp.int32, shape, 1) == lax.broadcasted_iota(jnp.int32, shape, 0) + start
    for i, ref in enumerate((mask_ids, chain)):
        values = ref[...].astype(F32).reshape(1, width)
        marks[i : i + 1, :] = values
        picked = jnp.sum(jnp.where(at_row, values, 0.0), axis=1, keepdims=True)
        row_marks[i] = jnp.broadcast_to(picked, row_marks.shape[1:])

    def prepare(group):
        larges[group[0] // GROUP].wait()
        parts = []
        for r in group:
            for _, columns in blocks(width):
                values = x[r, columns, :].astype(F32).T
                x_t[r, :, columns] = values.astype(BF16)
                same = same_chain(marks, row_marks, r, columns)
                parts.append(norm_input(values, same, g[...], b[...], e[...]))
        return jnp.concatenate(parts, axis=1)

    turned = []

    def consume(group, normed):
        part = pl.ds(group[0], len(group))
        turned.append(pltpu.make_async_copy(x_t.at[part], x_out.at[part], x_sems.at[group[0] // GROUP]))
        turned[-1].start()
        project(group, normed, marks, row_marks, w_t[...], slabs)

    overlapped(rows, prepare, consume)
    write_crossing(slabs, left, right, out, own, out_sems)
    for copy in turned:
        copy.wait()


def write_gates(x_t, marks, row_marks, g, b, e, w_t, out):
    rows, _, width = x_t.shape

    def prepare(group):
        return jnp.concatenate(
            [
                norm_input(x_t[r, :, columns].astype(F32), same_chain(marks, row_marks, r, columns), g, b, e)
                for r in group
                for _, columns in blocks(width)
            ],
            axis=1,
        )

    def consume(group, normed):
        gates = jax.nn.sigmoid(jnp.dot(w_t, normed, preferred_element_type=F32))
        for k, r in enumerate(group):
            out[r] = gates[:, k * width : (k + 1) * width]

    overlapped(rows, prepare, consume)


W_AB, W_OUT, W_GATE = slice(0, 4 * HC), [slice(4 * HC, 5 * HC), slice(5 * HC, 6 * HC)], slice(6 * HC, 7 * HC)
GAIN, BIAS, EMBED, MID_GAIN, MID_BIAS = 0, 1, 2, [3, 5], [4, 6]


def gate_kernel(
    x_t, marks, row_marks, gain, bias, embed, w_gate, w_ab, mid_gain, mid_bias, w_out, out, weights, columns_out,
    vectors, w_square, w_wide, sems,
):
    copies = fetch(
        [
            (gain, vectors.at[0]), (bias, vectors.at[1]), (embed, vectors.at[2]), (mid_gain, vectors.at[3]),
            (mid_bias, vectors.at[4]), (w_gate, w_square.at[0]), (w_out, w_square.at[1]), (w_ab.at[1], w_wide),
        ],
        sems,
    )
    for copy in copies:
        copy.wait()
    weights[W_AB, :] = turn(w_wide)
    weights[W_GATE, :] = turn(w_square.at[0, 1])
    for layer in range(2):
        weights[W_OUT[layer], :] = turn(w_square.at[1, layer])
        columns_out[MID_GAIN[layer]] = column(vectors.at[3], layer)
        columns_out[MID_BIAS[layer]] = column(vectors.at[4], layer)
    for i in (GAIN, BIAS, EMBED):
        columns_out[i] = column(vectors.at[i], 1)
    first = [column(vectors.at[i], 0) for i in (GAIN, BIAS, EMBED)]
    write_gates(x_t, marks, row_marks, *first, turn(w_square.at[0, 0]), out)


def second_gate_kernel(x_t, marks, row_marks, weights, columns, out):
    write_gates(x_t, marks, row_marks, columns[GAIN], columns[BIAS], columns[EMBED], weights[W_GATE, :], out)


def first_products_kernel(rows, recv, *refs):
    own, (out, own_recv, left_wide, right_wide, natural, turned, sems) = refs[:-7], refs[-7:]
    devices, depth, width = recv.shape
    half = devices // 2
    channels = depth // rows
    me = lax.axis_index("row")
    mine = me // half * half
    other = half - mine
    copies = fetch([(src, own_recv.at[me % half ^ o]) for o, src in enumerate(own)], sems)

    def widen_part(wide, first, ref, start):
        def step(i, carry):
            for k in range(4):
                q = i * 4 + k
                place = pl.multiple_of((first + q) * depth, 8)
                for j, columns in blocks(width):
                    wide[j, pl.ds(place, depth), :] = ref[start + q, :, columns].astype(F32)
            return carry

        lax.fori_loop(0, half // 4, step, 0)

    widen_part(left_wide, 0, recv, mine)
    widen_part(right_wide, other, recv, other)
    for copy in copies:
        copy.wait()
    widen_part(right_wide, mine, own_recv, 0)
    for c in range(channels):
        left, right = [], []
        for j, _ in blocks(width):
            pieces = [left_wide[j, pl.ds(c * rows + r, half, stride=depth), :].astype(BF16) for r in range(rows)]
            left.append(jnp.concatenate(pieces, axis=0))
            for r in range(rows):
                natural[c, j, pl.ds(r, devices, stride=rows), :] = right_wide[
                    j, pl.ds(c * rows + r, devices, stride=depth), :
                ]
            right.append(natural[c, j].astype(BF16))
        product = lax.dot_general(
            jnp.concatenate(left, axis=1), jnp.concatenate(right, axis=1), (((1,), (1,)), ((), ())),
            preferred_element_type=F32,
        )
        for j, columns in blocks(width):
            for r in range(rows):
                turned[j, pl.ds(c * rows + r, half, stride=depth), :] = product[r * half : (r + 1) * half, columns]
    for q in range(half):
        for j, columns in blocks(width):
            out[q, :, columns] = turned[j, q * depth : (q + 1) * depth, :].astype(BF16)


def second_products_kernel(rows, recv, out, wide, natural, turned):
    devices, depth, width = recv.shape
    channels = depth // (2 * rows)
    widen(recv, wide)

    def by_row(side, c):
        return jnp.concatenate(
            [
                jnp.concatenate(
                    [
                        wide[j, pl.ds((side * channels + c) * rows + r, devices, stride=depth), :].astype(BF16)
                        for r in range(rows)
                    ],
                    axis=0,
                )
                for j, _ in blocks(width)
            ],
            axis=1,
        )

    for c in range(channels):
        product = lax.dot_general(
            by_row(0, c), by_row(1, c), (((0,), (0,)), ((), ())), preferred_element_type=F32
        )
        for j, columns in blocks(width):
            natural[c, j] = product[:, columns]
            for r in range(rows):
                turned[j, pl.ds(c * rows + r, devices, stride=channels * rows), :] = natural[
                    c, j, pl.ds(r, devices, stride=rows), :
                ]
    for s in range(devices):
        for j, columns in blocks(width):
            out[s, :, columns] = turned[j, s * channels * rows : (s + 1) * channels * rows, :].astype(BF16)


def finish(group, width, tri, gate, x_t, w_t, gain, bias):
    rows = tri.shape[1] // HC
    normed = jnp.concatenate(
        [
            norm_channels(tri[j, pl.ds(r, HC, stride=rows), :], gain, bias).astype(BF16)
            for r in group
            for j, _ in blocks(width)
        ],
        axis=1,
    )
    branch = jnp.dot(w_t, normed, preferred_element_type=F32)
    return {
        (r, j): (
            x_t[r, :, columns].astype(F32)
            + gate[r, :, columns] * branch[:, k * width + j * 128 : k * width + (j + 1) * 128]
        ).astype(BF16)
        for k, r in enumerate(group)
        for j, columns in blocks(width)
    }


def middle_kernel(recv, gate, x_t, marks, row_marks, weights, vectors, out, new_t, slabs, tri):
    rows, _, width = x_t.shape
    widen(recv, tri)

    def prepare(group):
        mid = (vectors[MID_GAIN[0]], vectors[MID_BIAS[0]])
        states = finish(group, width, tri, gate, x_t, weights[W_OUT[0], :], *mid)
        parts = []
        for r in group:
            for j, columns in blocks(width):
                new_t[r, :, columns] = states[r, j]
                same = same_chain(marks, row_marks, r, columns)
                parts.append(
                    norm_input(states[r, j].astype(F32), same, vectors[GAIN], vectors[BIAS], vectors[EMBED])
                )
        return jnp.concatenate(parts, axis=1)

    def consume(group, normed):
        project(group, normed, marks, row_marks, weights[W_AB, :], slabs)

    overlapped(rows, prepare, consume)
    write_slabs(slabs, out)


def last_kernel(recv_in, gate_in, x_in, weights_in, vectors_in, out, recv, gate, x_t, weights, vectors, tri, result, sems):
    rows, _, width = x_t.shape
    devices, depth, _ = recv.shape
    parts = [pl.ds(d, devices // 4) for d in range(0, devices, devices // 4)]
    todo = groups(rows)
    pairs = [(recv_in.at[part], recv.at[part]) for part in parts]
    pairs.append((weights_in.at[W_OUT[1]], weights))
    pairs += [(vectors_in.at[i], vectors.at[k]) for k, i in enumerate((MID_GAIN[1], MID_BIAS[1]))]
    for group in todo:
        part = pl.ds(group[0], len(group))
        pairs += [(gate_in.at[part], gate.at[part]), (x_in.at[part], x_t.at[part])]
    copies = fetch(pairs, sems)
    for k, part in enumerate(parts):
        copies[k].wait()
        for d in range(part.start, part.start + part.size):
            for j, columns in blocks(width):
                tri[j, d * depth : (d + 1) * depth, :] = recv[d, :, columns].astype(F32)
    for copy in copies[4:7]:
        copy.wait()
    done = []
    for k, group in enumerate(todo):
        for copy in copies[7 + 2 * k : 9 + 2 * k]:
            copy.wait()
        states = finish(group, width, tri, gate, x_t, weights[...], vectors[0], vectors[1])
        for (r, j), state in states.items():
            result[r, j * 128 : (j + 1) * 128, :] = state.astype(F32).T.astype(BF16)
        part = pl.ds(group[0], len(group))
        done.append(pltpu.make_async_copy(result.at[part], out.at[part], sems.at[k]))
        done[-1].start()
    for copy in done:
        copy.wait()


def call(kernel, outs, scratch, arrays, anywhere, flops, limit=VMEM_LIMIT, far=0):
    size = sum(a.size * a.dtype.itemsize for a in list(arrays) + list(outs))
    return pl.pallas_call(
        kernel,
        out_shape=outs,
        in_specs=[WHOLE] * len(arrays) + [ANYWHERE] * len(anywhere),
        out_specs=[ANYWHERE] * far + [WHOLE] * (len(outs) - far),
        scratch_shapes=scratch,
        compiler_params=pltpu.CompilerParams(vmem_limit_bytes=limit),
        cost_estimate=pl.CostEstimate(flops=flops, bytes_accessed=size, transcendentals=0),
    )(*arrays, *anywhere)


def local(
    pair, residue_mask, chain_ids, ln_in_gain, ln_in_bias, chain_embed, w_ab, w_gate, ln_mid_gain, ln_mid_bias, w_out
):
    rows, width, _ = pair.shape
    devices = lax.axis_size("row")
    half = devices // 2
    channels = HC // devices
    cols = width // 128
    pairs = rows * width

    sent = jax.ShapeDtypeStruct((devices, 2 * channels * rows, width), BF16)
    back = jax.ShapeDtypeStruct((devices, channels * rows, width), BF16)
    own_back = jax.ShapeDtypeStruct((half, 2 * channels * rows, width), BF16)
    own_slab = jax.ShapeDtypeStruct((2 * channels * rows, width), BF16)
    state_t = jax.ShapeDtypeStruct((rows, C, width), BF16)
    gate_t = jax.ShapeDtypeStruct((rows, C, width), F32)
    mark = jax.ShapeDtypeStruct((2, width), F32)
    row_mark = jax.ShapeDtypeStruct((2, (rows + 7) // 8 * 8, 128), F32)
    turned = jax.ShapeDtypeStruct((7 * HC, C), BF16)
    columns = jax.ShapeDtypeStruct((7, C, 128), F32)

    vector = pltpu.VMEM((C, 128), F32)
    ids = pltpu.VMEM((width,), jnp.int32)
    w_wide = pltpu.VMEM((C, 4 * HC), BF16)
    slabs_wide = pltpu.VMEM((cols, 2 * HC * rows, 128), F32)
    tri_wide = pltpu.VMEM((cols, HC * rows, 128), F32)
    norms = (ln_in_gain, ln_in_bias, chain_embed)

    def sems(n):
        return pltpu.SemaphoreType.DMA((n,))

    def exchange(slabs, groups=None):
        return lax.all_to_all(
            slabs, "row", split_axis=0, concat_axis=0, tiled=True, axis_index_groups=groups
        )

    halves = [list(range(h * half, (h + 1) * half)) for h in range(2)]
    *own, slabs, x_t, marks, row_marks = call(
        first_kernel, [own_slab] * half + [sent, state_t, mark, row_mark],
        [
            pltpu.VMEM(pair.shape, BF16), pltpu.VMEM(state_t.shape, BF16), w_wide, pltpu.VMEM((3, 2, C), F32), ids, ids,
            pltpu.VMEM((4 * HC, C), BF16), vector, vector, vector, slabs_wide, pltpu.VMEM(own_back.shape, BF16),
            pltpu.VMEM(own_back.shape, BF16), sems(6), sems(len(groups(rows))), sems(8 + half),
        ],
        (), (residue_mask, chain_ids, pair, *norms, w_ab), 2 * pairs * C * 4 * HC, FIRST_VMEM_LIMIT, half + 2,
    )
    recv = exchange(slabs)
    own = [own[0]] + [lax.ppermute(own[o], "row", [(i, i ^ o) for i in range(devices)]) for o in range(1, half)]
    gate, weights, vectors = call(
        gate_kernel, [gate_t, turned, columns],
        [pltpu.VMEM((5, 2, C), F32), pltpu.VMEM((2, 2, C, C), BF16), w_wide, sems(8)],
        (x_t, marks, row_marks), (*norms, w_gate, w_ab, ln_mid_gain, ln_mid_bias, w_out), 2 * pairs * C * C,
    )
    products = call(
        functools.partial(first_products_kernel, rows), [own_back],
        [
            pltpu.VMEM(own_back.shape, BF16), tri_wide, slabs_wide, pltpu.VMEM((2 * channels, cols, width, 128), F32),
            tri_wide, sems(half),
        ],
        (recv,), own, 2 * channels * width**3, PRODUCTS_VMEM_LIMIT,
    )[0]
    tri = exchange(products, halves)
    slabs, x_t = call(
        middle_kernel, [sent, state_t], [slabs_wide, tri_wide],
        (tri, gate, x_t, marks, row_marks, weights, vectors), (), 2 * pairs * C * 5 * HC,
    )
    recv = exchange(slabs)
    gate = call(
        second_gate_kernel, [gate_t], [], (x_t, marks, row_marks, weights, vectors), (), 2 * pairs * C * C
    )[0]
    products = call(
        functools.partial(second_products_kernel, rows), [back],
        [slabs_wide, pltpu.VMEM((channels, cols, width, 128), F32), tri_wide], (recv,), (), 2 * channels * width**3,
    )[0]
    tri = exchange(products)
    return call(
        last_kernel, [jax.ShapeDtypeStruct(pair.shape, BF16)],
        [
            pltpu.VMEM(back.shape, BF16), pltpu.VMEM(gate_t.shape, F32), pltpu.VMEM(state_t.shape, BF16),
            pltpu.VMEM((HC, C), BF16), pltpu.VMEM((2, C, 128), F32), tri_wide, pltpu.VMEM(pair.shape, BF16),
            sems(7 + 2 * len(groups(rows))),
        ],
        (), (tri, gate, x_t, weights, vectors), 2 * pairs * C * C, FIRST_VMEM_LIMIT, 1,
    )[0]


def solution(mesh):
    in_specs = (P(("grp", "row"), None, None), P("grp"), P("grp")) + (P(),) * 8
    out_specs = P(("grp", "row"), None, None)
    return jax.shard_map(local, mesh=mesh, in_specs=in_specs, out_specs=out_specs, check_vma=False)
```

```python
import functools

import jax
import jax.numpy as jnp
from jax import lax
from jax.experimental import pallas as pl
from jax.experimental.pallas import tpu as pltpu
from jax.sharding import PartitionSpec as P

C = 128
HC = 128
EPS = 1e-05
F32 = jnp.float32
BF16 = jnp.bfloat16
VMEM_LIMIT = 32 * 1024 * 1024
PRODUCTS_VMEM_LIMIT = 48 * 1024 * 1024
FIRST_VMEM_LIMIT = 60 * 1024 * 1024
GROUP = 2

WHOLE = pl.BlockSpec(memory_space=pltpu.VMEM)
ANYWHERE = pl.BlockSpec(memory_space=pl.ANY)


def blocks(width):
    return [(j, slice(j * 128, (j + 1) * 128)) for j in range(width // 128)]


def column(vector_ref, layer):
    return jnp.broadcast_to(vector_ref[layer : layer + 1, :], (C, C)).T


def turn(ref):
    return ref[...].astype(F32).T.astype(BF16)


def norm_channels(values, gain, bias):
    mean = jnp.sum(values, axis=0, keepdims=True) * (1.0 / C)
    centred = values - mean
    var = jnp.sum(centred * centred, axis=0, keepdims=True) * (1.0 / C)
    return centred * lax.rsqrt(var + EPS) * gain + bias


def norm_input(values, same, g, b, e):
    return (norm_channels(values, g, b) + same * e).astype(BF16)


def same_chain(marks, row_marks, r, columns):
    return (marks[1:2, columns] == row_marks[1, r : r + 1, :]).astype(F32)


def project(group, normed, marks, row_marks, w_t, slabs):
    rows = slabs.shape[1] // (2 * HC)
    width = slabs.shape[0] * 128
    proj = jnp.dot(w_t, normed, preferred_element_type=F32)
    for k, r in enumerate(group):
        for j, columns in blocks(width):
            mask = marks[0:1, columns] * row_marks[0, r : r + 1, :]
            for side in range(2):
                p = proj[2 * side * HC : (2 * side + 2) * HC, k * width + j * 128 : k * width + (j + 1) * 128]
                value = jax.nn.sigmoid(p[:HC]) * p[HC:] * mask
                slabs[j, pl.ds(side * HC * rows + r, HC, stride=rows), :] = value


def write_slabs(slabs, out):
    devices, depth, width = out.shape
    half = depth // 2
    for side in range(2):
        for d in range(devices):
            start = (side * devices + d) * half
            for j, columns in blocks(width):
                out[d, side * half : (side + 1) * half, columns] = slabs[j, start : start + half, :].astype(BF16)


def write_crossing(slabs, out, own):
    devices, depth, width = out.shape
    half = devices // 2
    me = lax.axis_index("row")
    side_rows = half * depth
    for d in range(devices):
        side = jnp.where(me // half == d // half, 0, side_rows)
        start = pl.multiple_of(side + d % half * depth, 8)
        for j, columns in blocks(width):
            out[d, :, columns] = slabs[j, pl.ds(start, depth), :].astype(BF16)
    for o, ref in enumerate(own):
        start = pl.multiple_of(side_rows + (me % half ^ o) * depth, 8)
        for j, columns in blocks(width):
            ref[:, columns] = slabs[j, pl.ds(start, depth), :].astype(BF16)


def spread(depth):
    return depth + 4 if depth % 8 == 0 else depth


def widen(recv, wide, pitch):
    devices, depth, width = recv.shape
    for s in range(devices):
        for j, columns in blocks(width):
            wide[j, s * pitch : s * pitch + depth, :] = recv[s, :, columns].astype(F32)


def fetch(pairs, sems):
    copies = [pltpu.make_async_copy(src, dst, sems.at[i]) for i, (src, dst) in enumerate(pairs)]
    for copy in copies:
        copy.start()
    return copies


def groups(rows):
    return [range(i, min(i + GROUP, rows)) for i in range(0, rows, GROUP)]


def overlapped(rows, prepare, consume):
    todo = groups(rows)
    ready = prepare(todo[0])
    for i, group in enumerate(todo):
        current = ready
        if i + 1 < len(todo):
            ready = prepare(todo[i + 1])
        consume(group, current)


def first_kernel(residue_mask, chain_ids, x_in, gain, bias, embed, w_ab, *refs):
    own = refs[:-16]
    out, x_t, marks, row_marks, x, w, vectors, mask_ids, chain, w_t, g, b, e, slabs, sems, x_sems = refs[-16:]
    rows, width, _ = x.shape
    smalls = fetch(
        [
            (residue_mask, mask_ids), (chain_ids, chain), (gain, vectors.at[0]), (bias, vectors.at[1]),
            (embed, vectors.at[2]), (w_ab.at[0], w),
        ],
        sems,
    )
    larges = fetch([(x_in.at[pl.ds(r[0], len(r))], x.at[pl.ds(r[0], len(r))]) for r in groups(rows)], x_sems)
    for copy in smalls:
        copy.wait()
    w_t[...] = turn(w)
    g[...] = column(vectors.at[0], 0)
    b[...] = column(vectors.at[1], 0)
    e[...] = column(vectors.at[2], 0)
    shape = (row_marks.shape[1], width)
    start = lax.axis_index("row") * rows
    at_row = lax.broadcasted_iota(jnp.int32, shape, 1) == lax.broadcasted_iota(jnp.int32, shape, 0) + start
    for i, ref in enumerate((mask_ids, chain)):
        values = ref[...].astype(F32).reshape(1, width)
        marks[i : i + 1, :] = values
        picked = jnp.sum(jnp.where(at_row, values, 0.0), axis=1, keepdims=True)
        row_marks[i] = jnp.broadcast_to(picked, row_marks.shape[1:])

    def prepare(group):
        larges[group[0] // GROUP].wait()
        parts = []
        for r in group:
            for _, columns in blocks(width):
                values = x[r, columns, :].astype(F32).T
                x_t[r, :, columns] = values.astype(BF16)
                same = same_chain(marks, row_marks, r, columns)
                parts.append(norm_input(values, same, g[...], b[...], e[...]))
        return jnp.concatenate(parts, axis=1)

    def consume(group, normed):
        project(group, normed, marks, row_marks, w_t[...], slabs)

    overlapped(rows, prepare, consume)
    write_crossing(slabs, out, own)


def write_gates(x_t, marks, row_marks, g, b, e, w_t, out):
    rows, _, width = x_t.shape

    def prepare(group):
        return jnp.concatenate(
            [
                norm_input(x_t[r, :, columns].astype(F32), same_chain(marks, row_marks, r, columns), g, b, e)
                for r in group
                for _, columns in blocks(width)
            ],
            axis=1,
        )

    def consume(group, normed):
        gates = jax.nn.sigmoid(jnp.dot(w_t, normed, preferred_element_type=F32))
        for k, r in enumerate(group):
            out[r] = gates[:, k * width : (k + 1) * width]

    overlapped(rows, prepare, consume)


W_AB, W_OUT, W_GATE = slice(0, 4 * HC), [slice(4 * HC, 5 * HC), slice(5 * HC, 6 * HC)], slice(6 * HC, 7 * HC)
GAIN, BIAS, EMBED, MID_GAIN, MID_BIAS = 0, 1, 2, [3, 5], [4, 6]


def gate_kernel(
    x_t, marks, row_marks, gain, bias, embed, w_gate, w_ab, mid_gain, mid_bias, w_out, out, weights, columns_out,
    vectors, w_square, w_wide, sems,
):
    copies = fetch(
        [
            (gain, vectors.at[0]), (bias, vectors.at[1]), (embed, vectors.at[2]), (mid_gain, vectors.at[3]),
            (mid_bias, vectors.at[4]), (w_gate, w_square.at[0]), (w_out, w_square.at[1]), (w_ab.at[1], w_wide),
        ],
        sems,
    )
    for copy in copies:
        copy.wait()
    weights[W_AB, :] = turn(w_wide)
    weights[W_GATE, :] = turn(w_square.at[0, 1])
    for layer in range(2):
        weights[W_OUT[layer], :] = turn(w_square.at[1, layer])
        columns_out[MID_GAIN[layer]] = column(vectors.at[3], layer)
        columns_out[MID_BIAS[layer]] = column(vectors.at[4], layer)
    for i in (GAIN, BIAS, EMBED):
        columns_out[i] = column(vectors.at[i], 1)
    first = [column(vectors.at[i], 0) for i in (GAIN, BIAS, EMBED)]
    write_gates(x_t, marks, row_marks, *first, turn(w_square.at[0, 0]), out)


def second_gate_kernel(x_t, marks, row_marks, weights, columns, out):
    write_gates(x_t, marks, row_marks, columns[GAIN], columns[BIAS], columns[EMBED], weights[W_GATE, :], out)


def first_products_kernel(rows, recv, *refs):
    own, (out, left_wide, right_wide, natural, turned) = refs[:-5], refs[-5:]
    devices, depth, width = recv.shape
    half = devices // 2
    channels = depth // rows
    me = lax.axis_index("row")
    mine = me // half * half
    other = half - mine
    pitch = spread(depth)
    for q in range(half):
        to_other = (other + q) * pitch
        to_own = (mine + (me % half ^ q)) * pitch
        for j, columns in blocks(width):
            left_wide[j, q * pitch : q * pitch + depth, :] = recv[mine + q, :, columns].astype(F32)
            right_wide[j, pl.ds(to_other, depth), :] = recv[other + q, :, columns].astype(F32)
            right_wide[j, pl.ds(to_own, depth), :] = own[q][:, columns].astype(F32)
    for c in range(channels):
        left, right = [], []
        for j, _ in blocks(width):
            pieces = [left_wide[j, pl.ds(c * rows + r, half, stride=pitch), :].astype(BF16) for r in range(rows)]
            left.append(jnp.concatenate(pieces, axis=0))
            for r in range(rows):
                natural[c, j, pl.ds(r, devices, stride=rows), :] = right_wide[
                    j, pl.ds(c * rows + r, devices, stride=pitch), :
                ]
            right.append(natural[c, j].astype(BF16))
        product = lax.dot_general(
            jnp.concatenate(left, axis=1), jnp.concatenate(right, axis=1), (((1,), (1,)), ((), ())),
            preferred_element_type=F32,
        )
        for j, columns in blocks(width):
            for r in range(rows):
                turned[j, pl.ds(c * rows + r, half, stride=pitch), :] = product[r * half : (r + 1) * half, columns]
    for q in range(half):
        for j, columns in blocks(width):
            out[q, :, columns] = turned[j, q * pitch : q * pitch + depth, :].astype(BF16)


def second_products_kernel(rows, recv, out, wide, natural, turned):
    devices, depth, width = recv.shape
    channels = depth // (2 * rows)
    pitch, out_pitch = spread(depth), spread(channels * rows)
    widen(recv, wide, pitch)

    def by_row(side, c):
        return jnp.concatenate(
            [
                jnp.concatenate(
                    [
                        wide[j, pl.ds((side * channels + c) * rows + r, devices, stride=pitch), :].astype(BF16)
                        for r in range(rows)
                    ],
                    axis=0,
                )
                for j, _ in blocks(width)
            ],
            axis=1,
        )

    for c in range(channels):
        product = lax.dot_general(
            by_row(0, c), by_row(1, c), (((0,), (0,)), ((), ())), preferred_element_type=F32
        )
        for j, columns in blocks(width):
            natural[c, j] = product[:, columns]
            for r in range(rows):
                turned[j, pl.ds(c * rows + r, devices, stride=out_pitch), :] = natural[
                    c, j, pl.ds(r, devices, stride=rows), :
                ]
    for s in range(devices):
        for j, columns in blocks(width):
            out[s, :, columns] = turned[j, s * out_pitch : s * out_pitch + channels * rows, :].astype(BF16)


def finish(layer, group, width, tri, gate, x_t, weights, vectors):
    rows = tri.shape[1] // HC
    gain, bias = vectors[MID_GAIN[layer]], vectors[MID_BIAS[layer]]
    normed = jnp.concatenate(
        [
            norm_channels(tri[j, pl.ds(r, HC, stride=rows), :], gain, bias).astype(BF16)
            for r in group
            for j, _ in blocks(width)
        ],
        axis=1,
    )
    branch = jnp.dot(weights[W_OUT[layer], :], normed, preferred_element_type=F32)
    return {
        (r, j): (
            x_t[r, :, columns].astype(F32)
            + gate[r, :, columns] * branch[:, k * width + j * 128 : k * width + (j + 1) * 128]
        ).astype(BF16)
        for k, r in enumerate(group)
        for j, columns in blocks(width)
    }


def middle_kernel(recv, gate, x_t, marks, row_marks, weights, vectors, out, new_t, slabs, tri):
    rows, _, width = x_t.shape
    widen(recv, tri, recv.shape[1])

    def prepare(group):
        states = finish(0, group, width, tri, gate, x_t, weights, vectors)
        parts = []
        for r in group:
            for j, columns in blocks(width):
                new_t[r, :, columns] = states[r, j]
                same = same_chain(marks, row_marks, r, columns)
                parts.append(
                    norm_input(states[r, j].astype(F32), same, vectors[GAIN], vectors[BIAS], vectors[EMBED])
                )
        return jnp.concatenate(parts, axis=1)

    def consume(group, normed):
        project(group, normed, marks, row_marks, weights[W_AB, :], slabs)

    overlapped(rows, prepare, consume)
    write_slabs(slabs, out)


def last_kernel(recv, gate, x_t, weights, vectors, out, tri):
    rows, _, width = x_t.shape
    widen(recv, tri, recv.shape[1])
    for group in groups(rows):
        for (r, j), state in finish(1, group, width, tri, gate, x_t, weights, vectors).items():
            out[r, j * 128 : (j + 1) * 128, :] = state.astype(F32).T.astype(BF16)


def call(kernel, outs, scratch, arrays, anywhere, flops, limit=VMEM_LIMIT):
    size = sum(a.size * a.dtype.itemsize for a in list(arrays) + list(outs))
    return pl.pallas_call(
        kernel,
        out_shape=outs,
        in_specs=[WHOLE] * len(arrays) + [ANYWHERE] * len(anywhere),
        out_specs=[WHOLE] * len(outs),
        scratch_shapes=scratch,
        compiler_params=pltpu.CompilerParams(vmem_limit_bytes=limit),
        cost_estimate=pl.CostEstimate(flops=flops, bytes_accessed=size, transcendentals=0),
    )(*arrays, *anywhere)


def local(
    pair, residue_mask, chain_ids, ln_in_gain, ln_in_bias, chain_embed, w_ab, w_gate, ln_mid_gain, ln_mid_bias, w_out
):
    rows, width, _ = pair.shape
    devices = lax.axis_size("row")
    half = devices // 2
    channels = HC // devices
    cols = width // 128
    pairs = rows * width

    sent = jax.ShapeDtypeStruct((devices, 2 * channels * rows, width), BF16)
    back = jax.ShapeDtypeStruct((devices, channels * rows, width), BF16)
    own_back = jax.ShapeDtypeStruct((half, 2 * channels * rows, width), BF16)
    own_slab = jax.ShapeDtypeStruct((2 * channels * rows, width), BF16)
    state_t = jax.ShapeDtypeStruct((rows, C, width), BF16)
    gate_t = jax.ShapeDtypeStruct((rows, C, width), F32)
    mark = jax.ShapeDtypeStruct((2, width), F32)
    row_mark = jax.ShapeDtypeStruct((2, (rows + 7) // 8 * 8, 128), F32)
    turned = jax.ShapeDtypeStruct((7 * HC, C), BF16)
    columns = jax.ShapeDtypeStruct((7, C, 128), F32)

    vector = pltpu.VMEM((C, 128), F32)
    ids = pltpu.VMEM((width,), jnp.int32)
    w_wide = pltpu.VMEM((C, 4 * HC), BF16)
    slabs_wide = pltpu.VMEM((cols, 2 * HC * rows, 128), F32)
    own_spread = pltpu.VMEM((cols, half * spread(2 * channels * rows), 128), F32)
    all_spread = pltpu.VMEM((cols, devices * spread(2 * channels * rows), 128), F32)
    back_spread = pltpu.VMEM((cols, devices * spread(channels * rows), 128), F32)
    tri_wide = pltpu.VMEM((cols, HC * rows, 128), F32)
    norms = (ln_in_gain, ln_in_bias, chain_embed)

    def sems(n):
        return pltpu.SemaphoreType.DMA((n,))

    def exchange(slabs, groups=None):
        return lax.all_to_all(
            slabs, "row", split_axis=0, concat_axis=0, tiled=True, axis_index_groups=groups
        )

    halves = [list(range(h * half, (h + 1) * half)) for h in range(2)]
    *own, slabs, x_t, marks, row_marks = call(
        first_kernel, [own_slab] * half + [sent, state_t, mark, row_mark],
        [
            pltpu.VMEM(pair.shape, BF16), w_wide, pltpu.VMEM((3, 2, C), F32), ids, ids, pltpu.VMEM((4 * HC, C), BF16),
            vector, vector, vector, slabs_wide, sems(6), sems(len(groups(rows))),
        ],
        (), (residue_mask, chain_ids, pair, *norms, w_ab), 2 * pairs * C * 4 * HC, FIRST_VMEM_LIMIT,
    )
    recv = exchange(slabs)
    own = [own[0]] + [lax.ppermute(own[o], "row", [(i, i ^ o) for i in range(devices)]) for o in range(1, half)]
    gate, weights, vectors = call(
        gate_kernel, [gate_t, turned, columns],
        [pltpu.VMEM((5, 2, C), F32), pltpu.VMEM((2, 2, C, C), BF16), w_wide, sems(8)],
        (x_t, marks, row_marks), (*norms, w_gate, w_ab, ln_mid_gain, ln_mid_bias, w_out), 2 * pairs * C * C,
    )
    products = call(
        functools.partial(first_products_kernel, rows), [own_back],
        [
            own_spread, all_spread, pltpu.VMEM((2 * channels, cols, width, 128), F32), own_spread,
        ],
        (recv, *own), (), 2 * channels * width**3, PRODUCTS_VMEM_LIMIT,
    )[0]
    tri = exchange(products, halves)
    slabs, x_t = call(
        middle_kernel, [sent, state_t], [slabs_wide, tri_wide],
        (tri, gate, x_t, marks, row_marks, weights, vectors), (), 2 * pairs * C * 5 * HC,
    )
    recv = exchange(slabs)
    gate = call(
        second_gate_kernel, [gate_t], [], (x_t, marks, row_marks, weights, vectors), (), 2 * pairs * C * C
    )[0]
    products = call(
        functools.partial(second_products_kernel, rows), [back],
        [all_spread, pltpu.VMEM((channels, cols, width, 128), F32), back_spread], (recv,), (), 2 * channels * width**3,
    )[0]
    tri = exchange(products)
    return call(
        last_kernel, [jax.ShapeDtypeStruct(pair.shape, BF16)], [tri_wide], (tri, gate, x_t, weights, vectors), (),
        2 * pairs * C * C,
    )[0]


def solution(mesh):
    in_specs = (P(("grp", "row"), None, None), P("grp"), P("grp")) + (P(),) * 8
    out_specs = P(("grp", "row"), None, None)
    return jax.shard_map(local, mesh=mesh, in_specs=in_specs, out_specs=out_specs, check_vma=False)
```

```python
import functools

import jax
import jax.numpy as jnp
from jax import lax
from jax.experimental import pallas as pl
from jax.experimental.pallas import tpu as pltpu
from jax.sharding import PartitionSpec as P

C = 128
HC = 128
EPS = 1e-05
F32 = jnp.float32
BF16 = jnp.bfloat16
VMEM_LIMIT = 32 * 1024 * 1024
PRODUCTS_VMEM_LIMIT = 48 * 1024 * 1024
FIRST_VMEM_LIMIT = 60 * 1024 * 1024
GROUP = 2

WHOLE = pl.BlockSpec(memory_space=pltpu.VMEM)
ANYWHERE = pl.BlockSpec(memory_space=pl.ANY)


def blocks(width):
    return [(j, slice(j * 128, (j + 1) * 128)) for j in range(width // 128)]


def column(vector_ref, layer):
    return jnp.broadcast_to(vector_ref[layer : layer + 1, :], (C, C)).T


def turn(ref):
    return ref[...].astype(F32).T.astype(BF16)


def norm_channels(values, gain, bias):
    mean = jnp.sum(values, axis=0, keepdims=True) * (1.0 / C)
    centred = values - mean
    var = jnp.sum(centred * centred, axis=0, keepdims=True) * (1.0 / C)
    return centred * lax.rsqrt(var + EPS) * gain + bias


def norm_input(values, same, g, b, e):
    return (norm_channels(values, g, b) + same * e).astype(BF16)


def same_chain(marks, row_marks, r, columns):
    return (marks[1:2, columns] == row_marks[1, r : r + 1, :]).astype(F32)


def project(group, normed, marks, row_marks, w_t, slabs):
    rows = slabs.shape[1] // (2 * HC)
    width = slabs.shape[0] * 128
    proj = jnp.dot(w_t, normed, preferred_element_type=F32)
    for k, r in enumerate(group):
        for j, columns in blocks(width):
            mask = marks[0:1, columns] * row_marks[0, r : r + 1, :]
            for side in range(2):
                p = proj[2 * side * HC : (2 * side + 2) * HC, k * width + j * 128 : k * width + (j + 1) * 128]
                value = jax.nn.sigmoid(p[:HC]) * p[HC:] * mask
                slabs[j, pl.ds(side * HC * rows + r, HC, stride=rows), :] = value


def write_slabs(slabs, out):
    devices, depth, width = out.shape
    half = depth // 2
    for side in range(2):
        for d in range(devices):
            start = (side * devices + d) * half
            for j, columns in blocks(width):
                out[d, side * half : (side + 1) * half, columns] = slabs[j, start : start + half, :].astype(BF16)


def over(count, body):
    if count <= 16:
        for i in range(count):
            body(i)
    else:
        lax.fori_loop(0, count, lambda i, carry: (body(i), carry)[1], 0)


def write_crossing(slabs, out, own):
    devices, depth, width = out.shape
    half = devices // 2
    me = lax.axis_index("row")
    mine = me // half * half
    side_rows = half * depth

    def slab(q):
        for first, side in ((mine, 0), (half - mine, side_rows)):
            for j, columns in blocks(width):
                out[first + q, :, columns] = slabs[j, pl.ds(side + q * depth, depth), :].astype(BF16)

    over(half, slab)
    for o, ref in enumerate(own):
        start = pl.multiple_of(side_rows + (me % half ^ o) * depth, 8)
        for j, columns in blocks(width):
            ref[:, columns] = slabs[j, pl.ds(start, depth), :].astype(BF16)


def spread(depth):
    return depth + 4 if depth % 8 == 0 else depth


def widen(recv, wide, pitch):
    devices, depth, width = recv.shape
    for s in range(devices):
        for j, columns in blocks(width):
            wide[j, s * pitch : s * pitch + depth, :] = recv[s, :, columns].astype(F32)


def fetch(pairs, sems):
    copies = [pltpu.make_async_copy(src, dst, sems.at[i]) for i, (src, dst) in enumerate(pairs)]
    for copy in copies:
        copy.start()
    return copies


def groups(rows):
    return [range(i, min(i + GROUP, rows)) for i in range(0, rows, GROUP)]


def overlapped(rows, prepare, consume):
    todo = groups(rows)
    ready = prepare(todo[0])
    for i, group in enumerate(todo):
        current = ready
        if i + 1 < len(todo):
            ready = prepare(todo[i + 1])
        consume(group, current)


def first_kernel(residue_mask, chain_ids, x_in, gain, bias, embed, w_ab, *refs):
    own = refs[:-16]
    out, x_t, marks, row_marks, x, w, vectors, mask_ids, chain, w_t, g, b, e, slabs, sems, x_sems = refs[-16:]
    rows, width, _ = x.shape
    smalls = fetch(
        [
            (residue_mask, mask_ids), (chain_ids, chain), (gain, vectors.at[0]), (bias, vectors.at[1]),
            (embed, vectors.at[2]), (w_ab.at[0], w),
        ],
        sems,
    )
    larges = fetch([(x_in.at[pl.ds(r[0], len(r))], x.at[pl.ds(r[0], len(r))]) for r in groups(rows)], x_sems)
    for copy in smalls:
        copy.wait()
    w_t[...] = turn(w)
    g[...] = column(vectors.at[0], 0)
    b[...] = column(vectors.at[1], 0)
    e[...] = column(vectors.at[2], 0)
    shape = (row_marks.shape[1], width)
    start = lax.axis_index("row") * rows
    at_row = lax.broadcasted_iota(jnp.int32, shape, 1) == lax.broadcasted_iota(jnp.int32, shape, 0) + start
    for i, ref in enumerate((mask_ids, chain)):
        values = ref[...].astype(F32).reshape(1, width)
        marks[i : i + 1, :] = values
        picked = jnp.sum(jnp.where(at_row, values, 0.0), axis=1, keepdims=True)
        row_marks[i] = jnp.broadcast_to(picked, row_marks.shape[1:])

    def prepare(group):
        larges[group[0] // GROUP].wait()
        parts = []
        for r in group:
            for _, columns in blocks(width):
                values = x[r, columns, :].astype(F32).T
                x_t[r, :, columns] = values.astype(BF16)
                same = same_chain(marks, row_marks, r, columns)
                parts.append(norm_input(values, same, g[...], b[...], e[...]))
        return jnp.concatenate(parts, axis=1)

    def consume(group, normed):
        project(group, normed, marks, row_marks, w_t[...], slabs)

    overlapped(rows, prepare, consume)
    write_crossing(slabs, out, own)


def write_gates(x_t, marks, row_marks, g, b, e, w_t, out):
    rows, _, width = x_t.shape

    def prepare(group):
        return jnp.concatenate(
            [
                norm_input(x_t[r, :, columns].astype(F32), same_chain(marks, row_marks, r, columns), g, b, e)
                for r in group
                for _, columns in blocks(width)
            ],
            axis=1,
        )

    def consume(group, normed):
        gates = jax.nn.sigmoid(jnp.dot(w_t, normed, preferred_element_type=F32))
        for k, r in enumerate(group):
            out[r] = gates[:, k * width : (k + 1) * width].astype(BF16)

    overlapped(rows, prepare, consume)


W_AB, W_OUT, W_GATE = slice(0, 4 * HC), [slice(4 * HC, 5 * HC), slice(5 * HC, 6 * HC)], slice(6 * HC, 7 * HC)
GAIN, BIAS, EMBED, MID_GAIN, MID_BIAS = 0, 1, 2, [3, 5], [4, 6]


def gate_kernel(
    x_t, marks, row_marks, gain, bias, embed, w_gate, w_ab, mid_gain, mid_bias, w_out, out, weights, columns_out,
    vectors, w_square, w_wide, sems,
):
    copies = fetch(
        [
            (gain, vectors.at[0]), (bias, vectors.at[1]), (embed, vectors.at[2]), (mid_gain, vectors.at[3]),
            (mid_bias, vectors.at[4]), (w_gate, w_square.at[0]), (w_out, w_square.at[1]), (w_ab.at[1], w_wide),
        ],
        sems,
    )
    for copy in copies:
        copy.wait()
    weights[W_AB, :] = turn(w_wide)
    weights[W_GATE, :] = turn(w_square.at[0, 1])
    for layer in range(2):
        weights[W_OUT[layer], :] = turn(w_square.at[1, layer])
        columns_out[MID_GAIN[layer]] = column(vectors.at[3], layer)
        columns_out[MID_BIAS[layer]] = column(vectors.at[4], layer)
    for i in (GAIN, BIAS, EMBED):
        columns_out[i] = column(vectors.at[i], 1)
    first = [column(vectors.at[i], 0) for i in (GAIN, BIAS, EMBED)]
    write_gates(x_t, marks, row_marks, *first, turn(w_square.at[0, 0]), out)


def second_gate_kernel(x_t, marks, row_marks, weights, columns, out):
    write_gates(x_t, marks, row_marks, columns[GAIN], columns[BIAS], columns[EMBED], weights[W_GATE, :], out)


def first_products_kernel(rows, recv, *refs):
    own, (out, left_wide, right_wide, natural, turned) = refs[:-5], refs[-5:]
    devices, depth, width = recv.shape
    half = devices // 2
    channels = depth // rows
    me = lax.axis_index("row")
    mine = me // half * half
    other = half - mine
    pitch = spread(depth)

    def slab(q):
        for j, columns in blocks(width):
            left_wide[j, pl.ds(q * pitch, depth), :] = recv[mine + q, :, columns].astype(F32)
            right_wide[j, pl.ds((other + q) * pitch, depth), :] = recv[other + q, :, columns].astype(F32)

    over(half, slab)
    for o, ref in enumerate(own):
        for j, columns in blocks(width):
            right_wide[j, pl.ds((mine + (me % half ^ o)) * pitch, depth), :] = ref[:, columns].astype(F32)
    for c in range(channels):
        left, right = [], []
        for j, _ in blocks(width):
            pieces = [left_wide[j, pl.ds(c * rows + r, half, stride=pitch), :].astype(BF16) for r in range(rows)]
            left.append(jnp.concatenate(pieces, axis=0))
            for r in range(rows):
                natural[c, j, pl.ds(r, devices, stride=rows), :] = right_wide[
                    j, pl.ds(c * rows + r, devices, stride=pitch), :
                ]
            right.append(natural[c, j].astype(BF16))
        product = lax.dot_general(
            jnp.concatenate(left, axis=1), jnp.concatenate(right, axis=1), (((1,), (1,)), ((), ())),
            preferred_element_type=F32,
        )
        for j, columns in blocks(width):
            for r in range(rows):
                turned[j, pl.ds(c * rows + r, half, stride=pitch), :] = product[r * half : (r + 1) * half, columns]
    for q in range(half):
        for j, columns in blocks(width):
            out[q, :, columns] = turned[j, q * pitch : q * pitch + depth, :].astype(BF16)


def second_products_kernel(rows, recv, out, wide, natural, turned):
    devices, depth, width = recv.shape
    channels = depth // (2 * rows)
    pitch, out_pitch = spread(depth), spread(channels * rows)
    widen(recv, wide, pitch)

    def by_row(side, c):
        return jnp.concatenate(
            [
                jnp.concatenate(
                    [
                        wide[j, pl.ds((side * channels + c) * rows + r, devices, stride=pitch), :].astype(BF16)
                        for r in range(rows)
                    ],
                    axis=0,
                )
                for j, _ in blocks(width)
            ],
            axis=1,
        )

    for c in range(channels):
        product = lax.dot_general(
            by_row(0, c), by_row(1, c), (((0,), (0,)), ((), ())), preferred_element_type=F32
        )
        for j, columns in blocks(width):
            natural[c, j] = product[:, columns]
            for r in range(rows):
                turned[j, pl.ds(c * rows + r, devices, stride=out_pitch), :] = natural[
                    c, j, pl.ds(r, devices, stride=rows), :
                ]
    for s in range(devices):
        for j, columns in blocks(width):
            out[s, :, columns] = turned[j, s * out_pitch : s * out_pitch + channels * rows, :].astype(BF16)


def finish(layer, group, width, tri, gate, x_t, weights, vectors):
    rows = tri.shape[1] // HC
    gain, bias = vectors[MID_GAIN[layer]], vectors[MID_BIAS[layer]]
    normed = jnp.concatenate(
        [
            norm_channels(tri[j, pl.ds(r, HC, stride=rows), :], gain, bias).astype(BF16)
            for r in group
            for j, _ in blocks(width)
        ],
        axis=1,
    )
    branch = jnp.dot(weights[W_OUT[layer], :], normed, preferred_element_type=F32)
    return {
        (r, j): (
            x_t[r, :, columns].astype(F32)
            + gate[r, :, columns].astype(F32) * branch[:, k * width + j * 128 : k * width + (j + 1) * 128]
        ).astype(BF16)
        for k, r in enumerate(group)
        for j, columns in blocks(width)
    }


def middle_kernel(recv, gate, x_t, marks, row_marks, weights, vectors, out, new_t, slabs, tri):
    rows, _, width = x_t.shape
    widen(recv, tri, recv.shape[1])

    def prepare(group):
        states = finish(0, group, width, tri, gate, x_t, weights, vectors)
        parts = []
        for r in group:
            for j, columns in blocks(width):
                new_t[r, :, columns] = states[r, j]
                same = same_chain(marks, row_marks, r, columns)
                parts.append(
                    norm_input(states[r, j].astype(F32), same, vectors[GAIN], vectors[BIAS], vectors[EMBED])
                )
        return jnp.concatenate(parts, axis=1)

    def consume(group, normed):
        project(group, normed, marks, row_marks, weights[W_AB, :], slabs)

    overlapped(rows, prepare, consume)
    write_slabs(slabs, out)


def last_kernel(recv, gate, x_t, weights, vectors, out, tri):
    rows, _, width = x_t.shape
    widen(recv, tri, recv.shape[1])
    for group in groups(rows):
        for (r, j), state in finish(1, group, width, tri, gate, x_t, weights, vectors).items():
            out[r, j * 128 : (j + 1) * 128, :] = state.astype(F32).T.astype(BF16)


def call(kernel, outs, scratch, arrays, anywhere, flops, limit=VMEM_LIMIT):
    size = sum(a.size * a.dtype.itemsize for a in list(arrays) + list(outs))
    return pl.pallas_call(
        kernel,
        out_shape=outs,
        in_specs=[WHOLE] * len(arrays) + [ANYWHERE] * len(anywhere),
        out_specs=[WHOLE] * len(outs),
        scratch_shapes=scratch,
        compiler_params=pltpu.CompilerParams(vmem_limit_bytes=limit),
        cost_estimate=pl.CostEstimate(flops=flops, bytes_accessed=size, transcendentals=0),
    )(*arrays, *anywhere)


def local(
    pair, residue_mask, chain_ids, ln_in_gain, ln_in_bias, chain_embed, w_ab, w_gate, ln_mid_gain, ln_mid_bias, w_out
):
    rows, width, _ = pair.shape
    devices = lax.axis_size("row")
    half = devices // 2
    channels = HC // devices
    cols = width // 128
    pairs = rows * width

    sent = jax.ShapeDtypeStruct((devices, 2 * channels * rows, width), BF16)
    back = jax.ShapeDtypeStruct((devices, channels * rows, width), BF16)
    own_back = jax.ShapeDtypeStruct((half, 2 * channels * rows, width), BF16)
    own_slab = jax.ShapeDtypeStruct((2 * channels * rows, width), BF16)
    state_t = jax.ShapeDtypeStruct((rows, C, width), BF16)
    gate_t = jax.ShapeDtypeStruct((rows, C, width), BF16)
    mark = jax.ShapeDtypeStruct((2, width), F32)
    row_mark = jax.ShapeDtypeStruct((2, (rows + 7) // 8 * 8, 128), F32)
    turned = jax.ShapeDtypeStruct((7 * HC, C), BF16)
    columns = jax.ShapeDtypeStruct((7, C, 128), F32)

    vector = pltpu.VMEM((C, 128), F32)
    ids = pltpu.VMEM((width,), jnp.int32)
    w_wide = pltpu.VMEM((C, 4 * HC), BF16)
    slabs_wide = pltpu.VMEM((cols, 2 * HC * rows, 128), F32)
    own_spread = pltpu.VMEM((cols, half * spread(2 * channels * rows), 128), F32)
    all_spread = pltpu.VMEM((cols, devices * spread(2 * channels * rows), 128), F32)
    back_spread = pltpu.VMEM((cols, devices * spread(channels * rows), 128), F32)
    tri_wide = pltpu.VMEM((cols, HC * rows, 128), F32)
    norms = (ln_in_gain, ln_in_bias, chain_embed)

    def sems(n):
        return pltpu.SemaphoreType.DMA((n,))

    def exchange(slabs, groups=None):
        return lax.all_to_all(
            slabs, "row", split_axis=0, concat_axis=0, tiled=True, axis_index_groups=groups
        )

    halves = [list(range(h * half, (h + 1) * half)) for h in range(2)]
    *own, slabs, x_t, marks, row_marks = call(
        first_kernel, [own_slab] * half + [sent, state_t, mark, row_mark],
        [
            pltpu.VMEM(pair.shape, BF16), w_wide, pltpu.VMEM((3, 2, C), F32), ids, ids, pltpu.VMEM((4 * HC, C), BF16),
            vector, vector, vector, slabs_wide, sems(6), sems(len(groups(rows))),
        ],
        (), (residue_mask, chain_ids, pair, *norms, w_ab), 2 * pairs * C * 4 * HC, FIRST_VMEM_LIMIT,
    )
    recv = exchange(slabs)
    own = [own[0]] + [lax.ppermute(own[o], "row", [(i, i ^ o) for i in range(devices)]) for o in range(1, half)]
    gate, weights, vectors = call(
        gate_kernel, [gate_t, turned, columns],
        [pltpu.VMEM((5, 2, C), F32), pltpu.VMEM((2, 2, C, C), BF16), w_wide, sems(8)],
        (x_t, marks, row_marks), (*norms, w_gate, w_ab, ln_mid_gain, ln_mid_bias, w_out), 2 * pairs * C * C,
    )
    products = call(
        functools.partial(first_products_kernel, rows), [own_back],
        [
            own_spread, all_spread, pltpu.VMEM((2 * channels, cols, width, 128), F32), own_spread,
        ],
        (recv, *own), (), 2 * channels * width**3, PRODUCTS_VMEM_LIMIT,
    )[0]
    tri = exchange(products, halves)
    slabs, x_t = call(
        middle_kernel, [sent, state_t], [slabs_wide, tri_wide],
        (tri, gate, x_t, marks, row_marks, weights, vectors), (), 2 * pairs * C * 5 * HC,
    )
    recv = exchange(slabs)
    gate = call(
        second_gate_kernel, [gate_t], [], (x_t, marks, row_marks, weights, vectors), (), 2 * pairs * C * C
    )[0]
    products = call(
        functools.partial(second_products_kernel, rows), [back],
        [all_spread, pltpu.VMEM((channels, cols, width, 128), F32), back_spread], (recv,), (), 2 * channels * width**3,
    )[0]
    tri = exchange(products)
    return call(
        last_kernel, [jax.ShapeDtypeStruct(pair.shape, BF16)], [tri_wide], (tri, gate, x_t, weights, vectors), (),
        2 * pairs * C * C, FIRST_VMEM_LIMIT,
    )[0]


def solution(mesh):
    in_specs = (P(("grp", "row"), None, None), P("grp"), P("grp")) + (P(),) * 8
    out_specs = P(("grp", "row"), None, None)
    return jax.shard_map(local, mesh=mesh, in_specs=in_specs, out_specs=out_specs, check_vma=False)
```

```python
import functools

import jax
import jax.numpy as jnp
from jax import lax
from jax.experimental import pallas as pl
from jax.experimental.pallas import tpu as pltpu
from jax.sharding import PartitionSpec as P

C = 128
HC = 128
EPS = 1e-05
F32 = jnp.float32
BF16 = jnp.bfloat16
VMEM_LIMIT = 32 * 1024 * 1024
PRODUCTS_VMEM_LIMIT = 48 * 1024 * 1024
FIRST_VMEM_LIMIT = 60 * 1024 * 1024
GROUP = 2

WHOLE = pl.BlockSpec(memory_space=pltpu.VMEM)
ANYWHERE = pl.BlockSpec(memory_space=pl.ANY)


def blocks(width):
    return [(j, slice(j * 128, (j + 1) * 128)) for j in range(width // 128)]


def column(vector_ref, layer):
    return jnp.broadcast_to(vector_ref[layer : layer + 1, :], (C, C)).T


def turn(ref):
    return ref[...].astype(F32).T.astype(BF16)


def norm_channels(values, gain, bias):
    mean = jnp.sum(values, axis=0, keepdims=True) * (1.0 / C)
    centred = values - mean
    var = jnp.sum(centred * centred, axis=0, keepdims=True) * (1.0 / C)
    return centred * lax.rsqrt(var + EPS) * gain + bias


def norm_input(values, same, g, b, e):
    return (norm_channels(values, g, b) + same * e).astype(BF16)


def same_chain(marks, row_marks, r, columns):
    return (marks[1:2, columns] == row_marks[1, r : r + 1, :]).astype(F32)


def project(group, normed, marks, row_marks, w_t, put):
    width = marks.shape[1]
    proj = jnp.dot(w_t, normed, preferred_element_type=F32)
    for k, r in enumerate(group):
        for j, columns in blocks(width):
            mask = marks[0:1, columns] * row_marks[0, r : r + 1, :]
            for side in range(2):
                p = proj[2 * side * HC : (2 * side + 2) * HC, k * width + j * 128 : k * width + (j + 1) * 128]
                put(side, r, j, jax.nn.sigmoid(p[:HC]) * p[HC:] * mask)


def over(count, body):
    if count <= 16:
        for i in range(count):
            body(i)
    else:
        lax.fori_loop(0, count, lambda i, carry: (body(i), carry)[1], 0)


def write_crossing(slabs, out, own):
    devices, depth, width = out.shape
    half = devices // 2
    me = lax.axis_index("row")
    mine = me // half * half
    side_rows = half * depth

    def slab(q):
        for first, side in ((mine, 0), (half - mine, side_rows)):
            for j, columns in blocks(width):
                out[first + q, :, columns] = slabs[j, pl.ds(side + q * depth, depth), :].astype(BF16)

    over(half, slab)
    for o, ref in enumerate(own):
        start = pl.multiple_of(side_rows + (me % half ^ o) * depth, 8)
        for j, columns in blocks(width):
            ref[:, columns] = slabs[j, pl.ds(start, depth), :].astype(BF16)


def spread(depth):
    return depth + 4 if depth % 8 == 0 else depth


def widen(recv, wide, pitch):
    devices, depth, width = recv.shape
    for s in range(devices):
        for j, columns in blocks(width):
            wide[j, s * pitch : s * pitch + depth, :] = recv[s, :, columns].astype(F32)


def fetch(pairs, sems):
    copies = [pltpu.make_async_copy(src, dst, sems.at[i]) for i, (src, dst) in enumerate(pairs)]
    for copy in copies:
        copy.start()
    return copies


def groups(rows):
    return [range(i, min(i + GROUP, rows)) for i in range(0, rows, GROUP)]


def overlapped(rows, prepare, consume):
    todo = groups(rows)
    ready = prepare(todo[0])
    for i, group in enumerate(todo):
        current = ready
        if i + 1 < len(todo):
            ready = prepare(todo[i + 1])
        consume(group, current)


def first_kernel(residue_mask, chain_ids, x_in, gain, bias, embed, w_ab, *refs):
    own = refs[:-16]
    out, x_t, marks, row_marks, x, w, vectors, mask_ids, chain, w_t, g, b, e, slabs, sems, x_sems = refs[-16:]
    rows, width, _ = x.shape
    smalls = fetch(
        [
            (residue_mask, mask_ids), (chain_ids, chain), (gain, vectors.at[0]), (bias, vectors.at[1]),
            (embed, vectors.at[2]), (w_ab.at[0], w),
        ],
        sems,
    )
    larges = fetch([(x_in.at[pl.ds(r[0], len(r))], x.at[pl.ds(r[0], len(r))]) for r in groups(rows)], x_sems)
    for copy in smalls:
        copy.wait()
    w_t[...] = turn(w)
    g[...] = column(vectors.at[0], 0)
    b[...] = column(vectors.at[1], 0)
    e[...] = column(vectors.at[2], 0)
    shape = (row_marks.shape[1], width)
    start = lax.axis_index("row") * rows
    at_row = lax.broadcasted_iota(jnp.int32, shape, 1) == lax.broadcasted_iota(jnp.int32, shape, 0) + start
    for i, ref in enumerate((mask_ids, chain)):
        values = ref[...].astype(F32).reshape(1, width)
        marks[i : i + 1, :] = values
        picked = jnp.sum(jnp.where(at_row, values, 0.0), axis=1, keepdims=True)
        row_marks[i] = jnp.broadcast_to(picked, row_marks.shape[1:])

    def prepare(group):
        larges[group[0] // GROUP].wait()
        parts = []
        for r in group:
            for _, columns in blocks(width):
                values = x[r, columns, :].astype(F32).T
                x_t[r, :, columns] = values.astype(BF16)
                same = same_chain(marks, row_marks, r, columns)
                parts.append(norm_input(values, same, g[...], b[...], e[...]))
        return jnp.concatenate(parts, axis=1)

    def put(side, r, j, values):
        slabs[j, pl.ds(side * HC * rows + r, HC, stride=rows), :] = values

    def consume(group, normed):
        project(group, normed, marks, row_marks, w_t[...], put)

    overlapped(rows, prepare, consume)
    write_crossing(slabs, out, own)


def write_gates(x_t, marks, row_marks, g, b, e, w_t, out):
    rows, _, width = x_t.shape

    def prepare(group):
        return jnp.concatenate(
            [
                norm_input(x_t[r, :, columns].astype(F32), same_chain(marks, row_marks, r, columns), g, b, e)
                for r in group
                for _, columns in blocks(width)
            ],
            axis=1,
        )

    def consume(group, normed):
        gates = jax.nn.sigmoid(jnp.dot(w_t, normed, preferred_element_type=F32))
        for k, r in enumerate(group):
            out[r] = gates[:, k * width : (k + 1) * width]

    overlapped(rows, prepare, consume)


W_AB, W_OUT, W_GATE = slice(0, 4 * HC), [slice(4 * HC, 5 * HC), slice(5 * HC, 6 * HC)], slice(6 * HC, 7 * HC)
GAIN, BIAS, EMBED, MID_GAIN, MID_BIAS = 0, 1, 2, [3, 5], [4, 6]


def gate_kernel(
    x_t, marks, row_marks, gain, bias, embed, w_gate, w_ab, mid_gain, mid_bias, w_out, out, weights, columns_out,
    vectors, w_square, w_wide, sems,
):
    copies = fetch(
        [
            (gain, vectors.at[0]), (bias, vectors.at[1]), (embed, vectors.at[2]), (mid_gain, vectors.at[3]),
            (mid_bias, vectors.at[4]), (w_gate, w_square.at[0]), (w_out, w_square.at[1]), (w_ab.at[1], w_wide),
        ],
        sems,
    )
    for copy in copies:
        copy.wait()
    weights[W_AB, :] = turn(w_wide)
    weights[W_GATE, :] = turn(w_square.at[0, 1])
    for layer in range(2):
        weights[W_OUT[layer], :] = turn(w_square.at[1, layer])
        columns_out[MID_GAIN[layer]] = column(vectors.at[3], layer)
        columns_out[MID_BIAS[layer]] = column(vectors.at[4], layer)
    for i in (GAIN, BIAS, EMBED):
        columns_out[i] = column(vectors.at[i], 1)
    first = [column(vectors.at[i], 0) for i in (GAIN, BIAS, EMBED)]
    write_gates(x_t, marks, row_marks, *first, turn(w_square.at[0, 0]), out)


def second_gate_kernel(x_t, marks, row_marks, weights, columns, out):
    write_gates(x_t, marks, row_marks, columns[GAIN], columns[BIAS], columns[EMBED], weights[W_GATE, :], out)


def first_products_kernel(rows, recv, *refs):
    own, (out, left_wide, right_wide, natural, turned) = refs[:-5], refs[-5:]
    devices, depth, width = recv.shape
    half = devices // 2
    channels = depth // rows
    me = lax.axis_index("row")
    mine = me // half * half
    other = half - mine
    pitch = spread(depth)

    def slab(q):
        for j, columns in blocks(width):
            left_wide[j, pl.ds(q * pitch, depth), :] = recv[mine + q, :, columns].astype(F32)
            right_wide[j, pl.ds((other + q) * pitch, depth), :] = recv[other + q, :, columns].astype(F32)

    over(half, slab)
    for o, ref in enumerate(own):
        for j, columns in blocks(width):
            right_wide[j, pl.ds((mine + (me % half ^ o)) * pitch, depth), :] = ref[:, columns].astype(F32)
    for c in range(channels):
        left, right = [], []
        for j, _ in blocks(width):
            pieces = [left_wide[j, pl.ds(c * rows + r, half, stride=pitch), :].astype(BF16) for r in range(rows)]
            left.append(jnp.concatenate(pieces, axis=0))
            for r in range(rows):
                natural[c, j, pl.ds(r, devices, stride=rows), :] = right_wide[
                    j, pl.ds(c * rows + r, devices, stride=pitch), :
                ]
            right.append(natural[c, j].astype(BF16))
        product = lax.dot_general(
            jnp.concatenate(left, axis=1), jnp.concatenate(right, axis=1), (((1,), (1,)), ((), ())),
            preferred_element_type=F32,
        )
        for j, columns in blocks(width):
            for r in range(rows):
                turned[j, pl.ds(c * rows + r, half, stride=pitch), :] = product[r * half : (r + 1) * half, columns]
    for q in range(half):
        for j, columns in blocks(width):
            out[q, :, columns] = turned[j, q * pitch : q * pitch + depth, :].astype(BF16)


def split_channels(devices):
    once = 3 * HC // (4 * devices)
    return HC // (devices // 2) - 2 * once, once


def second_products_kernel(rows, recv, *refs):
    own, (out, wide, own_wide, natural, turned) = refs[:-5], refs[-5:]
    devices, depth, width = recv.shape
    half = devices // 2
    twice, once = split_channels(devices)
    own_depth = own[0].shape[0]
    pitch, own_pitch, out_pitch = spread(depth), spread(own_depth), spread((twice + once) * rows)
    widen(recv, wide, pitch)
    for o, ref in enumerate(own):
        for j, columns in blocks(width):
            own_wide[j, o * own_pitch : o * own_pitch + own_depth, :] = ref[:, columns].astype(F32)

    def by_row(ref, start, count, stride):
        return jnp.concatenate(
            [
                jnp.concatenate(
                    [ref[j, pl.ds(start + r, count, stride=stride), :].astype(BF16) for r in range(rows)], axis=0
                )
                for j, _ in blocks(width)
            ],
            axis=1,
        )

    for t in range(twice + once):
        if t < twice:
            left, right = (by_row(own_wide, (side * twice + t) * rows, half, own_pitch) for side in range(2))
        else:
            left, right = (by_row(wide, (side * once + t - twice) * rows, devices, pitch) for side in range(2))
        product = lax.dot_general(left, right, (((0,), (0,)), ((), ())), preferred_element_type=F32)
        for j, columns in blocks(width):
            natural[t, j] = product[:, columns]
            for r in range(rows):
                turned[j, pl.ds(t * rows + r, devices, stride=out_pitch), :] = natural[
                    t, j, pl.ds(r, devices, stride=rows), :
                ]
    for s in range(devices):
        for j, columns in blocks(width):
            out[s, :, columns] = turned[j, s * out_pitch : s * out_pitch + out.shape[1], :].astype(BF16)


def finish(layer, group, width, values, gate, x_t, weights, vectors):
    gain, bias = vectors[MID_GAIN[layer]], vectors[MID_BIAS[layer]]
    normed = jnp.concatenate(
        [
            norm_channels(values(r, j), gain, bias).astype(BF16)
            for r in group
            for j, _ in blocks(width)
        ],
        axis=1,
    )
    branch = jnp.dot(weights[W_OUT[layer], :], normed, preferred_element_type=F32)
    return {
        (r, j): (
            x_t[r, :, columns].astype(F32)
            + gate[r, :, columns] * branch[:, k * width + j * 128 : k * width + (j + 1) * 128]
        ).astype(BF16)
        for k, r in enumerate(group)
        for j, columns in blocks(width)
    }


def middle_kernel(recv, gate, x_t, marks, row_marks, weights, vectors, *refs):
    own, (out, new_t, slabs, own_slabs, tri) = refs[:-5], refs[-5:]
    rows, _, width = x_t.shape
    devices, depth, _ = out.shape
    half = devices // 2
    twice, once = split_channels(devices)
    own_depth = own[0].shape[0]
    pitch, own_pitch = spread(depth), spread(own_depth)
    widen(recv, tri, recv.shape[1])

    def values(r, j):
        return tri[j, pl.ds(r, HC, stride=rows), :]

    def prepare(group):
        states = finish(0, group, width, values, gate, x_t, weights, vectors)
        parts = []
        for r in group:
            for j, columns in blocks(width):
                new_t[r, :, columns] = states[r, j]
                same = same_chain(marks, row_marks, r, columns)
                parts.append(
                    norm_input(states[r, j].astype(F32), same, vectors[GAIN], vectors[BIAS], vectors[EMBED])
                )
        return jnp.concatenate(parts, axis=1)

    def put(side, r, j, value):
        for ch in range(twice):
            own_slabs[j, pl.ds((side * twice + ch) * rows + r, half, stride=own_pitch), :] = value[
                ch * half : (ch + 1) * half
            ]
        for ch in range(once):
            start = twice * half + ch * devices
            slabs[j, pl.ds((side * once + ch) * rows + r, devices, stride=pitch), :] = value[start : start + devices]

    def consume(group, normed):
        project(group, normed, marks, row_marks, weights[W_AB, :], put)

    overlapped(rows, prepare, consume)
    for d in range(devices):
        for j, columns in blocks(width):
            out[d, :, columns] = slabs[j, d * pitch : d * pitch + depth, :].astype(BF16)
    place = lax.axis_index("row") % half
    for o, ref in enumerate(own):
        for j, columns in blocks(width):
            ref[:, columns] = own_slabs[j, pl.ds((place ^ o) * own_pitch, own_depth), :].astype(BF16)


def last_kernel(recv, gate, x_t, weights, vectors, out, tri):
    rows, _, width = x_t.shape
    devices, depth, _ = recv.shape
    half = devices // 2
    twice, once = split_channels(devices)
    pitch = spread(depth)
    widen(recv, tri, pitch)

    def values(r, j):
        def part(first, count, t):
            return tri[j, pl.ds(first * pitch + t * rows + r, count, stride=pitch), :]

        sums = [part(0, half, t) + part(half, half, t) for t in range(twice)]
        return jnp.concatenate(sums + [part(0, devices, twice + t) for t in range(once)], axis=0)

    for group in groups(rows):
        for (r, j), state in finish(1, group, width, values, gate, x_t, weights, vectors).items():
            out[r, j * 128 : (j + 1) * 128, :] = state.astype(F32).T.astype(BF16)


def call(kernel, outs, scratch, arrays, anywhere, flops, limit=VMEM_LIMIT):
    size = sum(a.size * a.dtype.itemsize for a in list(arrays) + list(outs))
    return pl.pallas_call(
        kernel,
        out_shape=outs,
        in_specs=[WHOLE] * len(arrays) + [ANYWHERE] * len(anywhere),
        out_specs=[WHOLE] * len(outs),
        scratch_shapes=scratch,
        compiler_params=pltpu.CompilerParams(vmem_limit_bytes=limit),
        cost_estimate=pl.CostEstimate(flops=flops, bytes_accessed=size, transcendentals=0),
    )(*arrays, *anywhere)


def local(
    pair, residue_mask, chain_ids, ln_in_gain, ln_in_bias, chain_embed, w_ab, w_gate, ln_mid_gain, ln_mid_bias, w_out
):
    rows, width, _ = pair.shape
    devices = lax.axis_size("row")
    half = devices // 2
    channels = HC // devices
    cols = width // 128
    pairs = rows * width

    sent = jax.ShapeDtypeStruct((devices, 2 * channels * rows, width), BF16)
    twice, once = split_channels(devices)
    sent_once = jax.ShapeDtypeStruct((devices, 2 * once * rows, width), BF16)
    sent_twice = jax.ShapeDtypeStruct((2 * twice * rows, width), BF16)
    back = jax.ShapeDtypeStruct((devices, (twice + once) * rows, width), BF16)
    own_back = jax.ShapeDtypeStruct((half, 2 * channels * rows, width), BF16)
    own_slab = jax.ShapeDtypeStruct((2 * channels * rows, width), BF16)
    state_t = jax.ShapeDtypeStruct((rows, C, width), BF16)
    gate_t = jax.ShapeDtypeStruct((rows, C, width), F32)
    mark = jax.ShapeDtypeStruct((2, width), F32)
    row_mark = jax.ShapeDtypeStruct((2, (rows + 7) // 8 * 8, 128), F32)
    turned = jax.ShapeDtypeStruct((7 * HC, C), BF16)
    columns = jax.ShapeDtypeStruct((7, C, 128), F32)

    vector = pltpu.VMEM((C, 128), F32)
    ids = pltpu.VMEM((width,), jnp.int32)
    w_wide = pltpu.VMEM((C, 4 * HC), BF16)
    slabs_wide = pltpu.VMEM((cols, 2 * HC * rows, 128), F32)
    own_spread = pltpu.VMEM((cols, half * spread(2 * channels * rows), 128), F32)
    all_spread = pltpu.VMEM((cols, devices * spread(2 * channels * rows), 128), F32)
    once_spread = pltpu.VMEM((cols, devices * spread(2 * once * rows), 128), F32)
    twice_spread = pltpu.VMEM((cols, half * spread(2 * twice * rows), 128), F32)
    back_spread = pltpu.VMEM((cols, devices * spread((twice + once) * rows), 128), F32)
    tri_wide = pltpu.VMEM((cols, HC * rows, 128), F32)
    norms = (ln_in_gain, ln_in_bias, chain_embed)

    def sems(n):
        return pltpu.SemaphoreType.DMA((n,))

    def exchange(slabs, groups=None):
        return lax.all_to_all(
            slabs, "row", split_axis=0, concat_axis=0, tiled=True, axis_index_groups=groups
        )

    def exchange_own(slabs):
        return slabs[:1] + [
            lax.ppermute(slabs[o], "row", [(i, i ^ o) for i in range(devices)]) for o in range(1, half)
        ]

    halves = [list(range(h * half, (h + 1) * half)) for h in range(2)]
    *own, slabs, x_t, marks, row_marks = call(
        first_kernel, [own_slab] * half + [sent, state_t, mark, row_mark],
        [
            pltpu.VMEM(pair.shape, BF16), w_wide, pltpu.VMEM((3, 2, C), F32), ids, ids, pltpu.VMEM((4 * HC, C), BF16),
            vector, vector, vector, slabs_wide, sems(6), sems(len(groups(rows))),
        ],
        (), (residue_mask, chain_ids, pair, *norms, w_ab), 2 * pairs * C * 4 * HC, FIRST_VMEM_LIMIT,
    )
    recv = exchange(slabs)
    own = exchange_own(own)
    gate, weights, vectors = call(
        gate_kernel, [gate_t, turned, columns],
        [pltpu.VMEM((5, 2, C), F32), pltpu.VMEM((2, 2, C, C), BF16), w_wide, sems(8)],
        (x_t, marks, row_marks), (*norms, w_gate, w_ab, ln_mid_gain, ln_mid_bias, w_out), 2 * pairs * C * C,
    )
    products = call(
        functools.partial(first_products_kernel, rows), [own_back],
        [
            own_spread, all_spread, pltpu.VMEM((2 * channels, cols, width, 128), F32), own_spread,
        ],
        (recv, *own), (), 2 * channels * width**3, PRODUCTS_VMEM_LIMIT,
    )[0]
    tri = exchange(products, halves)
    *own, slabs, x_t = call(
        middle_kernel, [sent_twice] * half + [sent_once, state_t], [once_spread, twice_spread, tri_wide],
        (tri, gate, x_t, marks, row_marks, weights, vectors), (), 2 * pairs * C * 5 * HC,
    )
    recv = exchange(slabs)
    own = exchange_own(own)
    gate = call(
        second_gate_kernel, [gate_t], [], (x_t, marks, row_marks, weights, vectors), (), 2 * pairs * C * C
    )[0]
    products = call(
        functools.partial(second_products_kernel, rows), [back],
        [once_spread, twice_spread, pltpu.VMEM((twice + once, cols, width, 128), F32), back_spread],
        (recv, *own), (), 2 * channels * width**3,
    )[0]
    tri = exchange(products)
    return call(
        last_kernel, [jax.ShapeDtypeStruct(pair.shape, BF16)], [back_spread], (tri, gate, x_t, weights, vectors), (),
        2 * pairs * C * C,
    )[0]


def solution(mesh):
    in_specs = (P(("grp", "row"), None, None), P("grp"), P("grp")) + (P(),) * 8
    out_specs = P(("grp", "row"), None, None)
    return jax.shard_map(local, mesh=mesh, in_specs=in_specs, out_specs=out_specs, check_vma=False)
```

```python
import functools

import jax
import jax.numpy as jnp
from jax import lax
from jax.experimental import pallas as pl
from jax.experimental.pallas import tpu as pltpu
from jax.sharding import PartitionSpec as P

C = 128
HC = 128
EPS = 1e-05
F32 = jnp.float32
BF16 = jnp.bfloat16
VMEM_LIMIT = 32 * 1024 * 1024
PRODUCTS_VMEM_LIMIT = 48 * 1024 * 1024
FIRST_VMEM_LIMIT = 60 * 1024 * 1024
GROUP = 4

WHOLE = pl.BlockSpec(memory_space=pltpu.VMEM)
ANYWHERE = pl.BlockSpec(memory_space=pl.ANY)


def blocks(width):
    return [(j, slice(j * 128, (j + 1) * 128)) for j in range(width // 128)]


def column(vector_ref, layer):
    return jnp.broadcast_to(vector_ref[layer : layer + 1, :], (C, C)).T


def turn(ref):
    return ref[...].astype(F32).T.astype(BF16)


def norm_channels(values, gain, bias):
    mean = jnp.sum(values, axis=0, keepdims=True) * (1.0 / C)
    centred = values - mean
    var = jnp.sum(centred * centred, axis=0, keepdims=True) * (1.0 / C)
    return centred * lax.rsqrt(var + EPS) * gain + bias


def norm_input(values, same, g, b, e):
    return (norm_channels(values, g, b) + same * e).astype(BF16)


def same_chain(marks, row_marks, r, columns):
    return (marks[1:2, columns] == row_marks[1, r : r + 1, :]).astype(F32)


def project(group, normed, marks, row_marks, w_t, slabs):
    rows = slabs.shape[1] // (2 * HC)
    width = slabs.shape[0] * 128
    proj = jnp.dot(w_t, normed, preferred_element_type=F32)
    for k, r in enumerate(group):
        for j, columns in blocks(width):
            mask = marks[0:1, columns] * row_marks[0, r : r + 1, :]
            for side in range(2):
                p = proj[2 * side * HC : (2 * side + 2) * HC, k * width + j * 128 : k * width + (j + 1) * 128]
                value = jax.nn.sigmoid(p[:HC]) * p[HC:] * mask
                slabs[j, pl.ds(side * HC * rows + r, HC, stride=rows), :] = value


def write_slabs(slabs, out):
    devices, depth, width = out.shape
    half = depth // 2
    for side in range(2):
        for d in range(devices):
            start = (side * devices + d) * half
            for j, columns in blocks(width):
                out[d, side * half : (side + 1) * half, columns] = slabs[j, start : start + half, :].astype(BF16)


def over(count, body):
    if count <= 16:
        for i in range(count):
            body(i)
    else:
        lax.fori_loop(0, count, lambda i, carry: (body(i), carry)[1], 0)


def write_crossing(slabs, out, own):
    devices, depth, width = out.shape
    half = devices // 2
    me = lax.axis_index("row")
    mine = me // half * half
    side_rows = half * depth

    def slab(q):
        for first, side in ((mine, 0), (half - mine, side_rows)):
            for j, columns in blocks(width):
                out[first + q, :, columns] = slabs[j, pl.ds(side + q * depth, depth), :].astype(BF16)

    over(half, slab)
    for o, ref in enumerate(own):
        start = pl.multiple_of(side_rows + (me % half ^ o) * depth, 8)
        for j, columns in blocks(width):
            ref[:, columns] = slabs[j, pl.ds(start, depth), :].astype(BF16)


def spread(depth):
    return depth + 4 if depth % 8 == 0 else depth


def widen(recv, wide, pitch):
    devices, depth, width = recv.shape
    for s in range(devices):
        for j, columns in blocks(width):
            wide[j, s * pitch : s * pitch + depth, :] = recv[s, :, columns].astype(F32)


def fetch(pairs, sems):
    copies = [pltpu.make_async_copy(src, dst, sems.at[i]) for i, (src, dst) in enumerate(pairs)]
    for copy in copies:
        copy.start()
    return copies


def groups(rows):
    return [range(i, min(i + GROUP, rows)) for i in range(0, rows, GROUP)]


def overlapped(rows, prepare, consume):
    todo = groups(rows)
    ready = prepare(todo[0])
    for i, group in enumerate(todo):
        current = ready
        if i + 1 < len(todo):
            ready = prepare(todo[i + 1])
        consume(group, current)


def first_kernel(residue_mask, chain_ids, x_in, gain, bias, embed, w_ab, *refs):
    own = refs[:-16]
    out, x_t, marks, row_marks, x, w, vectors, mask_ids, chain, w_t, g, b, e, slabs, sems, x_sems = refs[-16:]
    rows, width, _ = x.shape
    smalls = fetch(
        [
            (residue_mask, mask_ids), (chain_ids, chain), (gain, vectors.at[0]), (bias, vectors.at[1]),
            (embed, vectors.at[2]), (w_ab.at[0], w),
        ],
        sems,
    )
    larges = fetch([(x_in.at[pl.ds(r[0], len(r))], x.at[pl.ds(r[0], len(r))]) for r in groups(rows)], x_sems)
    for copy in smalls:
        copy.wait()
    w_t[...] = turn(w)
    g[...] = column(vectors.at[0], 0)
    b[...] = column(vectors.at[1], 0)
    e[...] = column(vectors.at[2], 0)
    shape = (row_marks.shape[1], width)
    start = lax.axis_index("row") * rows
    at_row = lax.broadcasted_iota(jnp.int32, shape, 1) == lax.broadcasted_iota(jnp.int32, shape, 0) + start
    for i, ref in enumerate((mask_ids, chain)):
        values = ref[...].astype(F32).reshape(1, width)
        marks[i : i + 1, :] = values
        picked = jnp.sum(jnp.where(at_row, values, 0.0), axis=1, keepdims=True)
        row_marks[i] = jnp.broadcast_to(picked, row_marks.shape[1:])

    def prepare(group):
        larges[group[0] // GROUP].wait()
        parts = []
        for r in group:
            for _, columns in blocks(width):
                values = x[r, columns, :].astype(F32).T
                x_t[r, :, columns] = values.astype(BF16)
                same = same_chain(marks, row_marks, r, columns)
                parts.append(norm_input(values, same, g[...], b[...], e[...]))
        return jnp.concatenate(parts, axis=1)

    def consume(group, normed):
        project(group, normed, marks, row_marks, w_t[...], slabs)

    overlapped(rows, prepare, consume)
    write_crossing(slabs, out, own)


def write_gates(x_t, marks, row_marks, g, b, e, w_t, out):
    rows, _, width = x_t.shape

    def prepare(group):
        return jnp.concatenate(
            [
                norm_input(x_t[r, :, columns].astype(F32), same_chain(marks, row_marks, r, columns), g, b, e)
                for r in group
                for _, columns in blocks(width)
            ],
            axis=1,
        )

    def consume(group, normed):
        gates = jax.nn.sigmoid(jnp.dot(w_t, normed, preferred_element_type=F32))
        for k, r in enumerate(group):
            out[r] = gates[:, k * width : (k + 1) * width]

    overlapped(rows, prepare, consume)


W_AB, W_OUT, W_GATE = slice(0, 4 * HC), [slice(4 * HC, 5 * HC), slice(5 * HC, 6 * HC)], slice(6 * HC, 7 * HC)
GAIN, BIAS, EMBED, MID_GAIN, MID_BIAS = 0, 1, 2, [3, 5], [4, 6]


def gate_kernel(
    x_t, marks, row_marks, gain, bias, embed, w_gate, w_ab, mid_gain, mid_bias, w_out, out, weights, columns_out,
    vectors, w_square, w_wide, sems,
):
    copies = fetch(
        [
            (gain, vectors.at[0]), (bias, vectors.at[1]), (embed, vectors.at[2]), (mid_gain, vectors.at[3]),
            (mid_bias, vectors.at[4]), (w_gate, w_square.at[0]), (w_out, w_square.at[1]), (w_ab.at[1], w_wide),
        ],
        sems,
    )
    for copy in copies:
        copy.wait()
    weights[W_AB, :] = turn(w_wide)
    weights[W_GATE, :] = turn(w_square.at[0, 1])
    for layer in range(2):
        weights[W_OUT[layer], :] = turn(w_square.at[1, layer])
        columns_out[MID_GAIN[layer]] = column(vectors.at[3], layer)
        columns_out[MID_BIAS[layer]] = column(vectors.at[4], layer)
    for i in (GAIN, BIAS, EMBED):
        columns_out[i] = column(vectors.at[i], 1)
    first = [column(vectors.at[i], 0) for i in (GAIN, BIAS, EMBED)]
    write_gates(x_t, marks, row_marks, *first, turn(w_square.at[0, 0]), out)


def second_gate_kernel(x_t, marks, row_marks, weights, columns, out, x_out, w_out, columns_out):
    x_out[...] = x_t[...]
    w_out[...] = weights[W_OUT[1], :]
    columns_out[0] = columns[MID_GAIN[1]]
    columns_out[1] = columns[MID_BIAS[1]]
    write_gates(x_t, marks, row_marks, columns[GAIN], columns[BIAS], columns[EMBED], weights[W_GATE, :], out)


def first_products_kernel(rows, recv, *refs):
    own, (out, left_wide, right_wide, natural, turned) = refs[:-5], refs[-5:]
    devices, depth, width = recv.shape
    half = devices // 2
    channels = depth // rows
    me = lax.axis_index("row")
    mine = me // half * half
    other = half - mine
    pitch = spread(depth)

    def slab(q):
        for j, columns in blocks(width):
            left_wide[j, pl.ds(q * pitch, depth), :] = recv[mine + q, :, columns].astype(F32)
            right_wide[j, pl.ds((other + q) * pitch, depth), :] = recv[other + q, :, columns].astype(F32)

    over(half, slab)
    for o, ref in enumerate(own):
        for j, columns in blocks(width):
            right_wide[j, pl.ds((mine + (me % half ^ o)) * pitch, depth), :] = ref[:, columns].astype(F32)
    for c in range(channels):
        left, right = [], []
        for j, _ in blocks(width):
            pieces = [left_wide[j, pl.ds(c * rows + r, half, stride=pitch), :].astype(BF16) for r in range(rows)]
            left.append(jnp.concatenate(pieces, axis=0))
            for r in range(rows):
                natural[c, j, pl.ds(r, devices, stride=rows), :] = right_wide[
                    j, pl.ds(c * rows + r, devices, stride=pitch), :
                ]
            right.append(natural[c, j].astype(BF16))
        product = lax.dot_general(
            jnp.concatenate(left, axis=1), jnp.concatenate(right, axis=1), (((1,), (1,)), ((), ())),
            preferred_element_type=F32,
        )
        for j, columns in blocks(width):
            for r in range(rows):
                turned[j, pl.ds(c * rows + r, half, stride=pitch), :] = product[r * half : (r + 1) * half, columns]
    for q in range(half):
        for j, columns in blocks(width):
            out[q, :, columns] = turned[j, q * pitch : q * pitch + depth, :].astype(BF16)


def second_products_kernel(rows, recv, out, wide, natural, turned):
    devices, depth, width = recv.shape
    channels = depth // (2 * rows)
    pitch, out_pitch = spread(depth), spread(channels * rows)
    widen(recv, wide, pitch)

    def by_row(side, c):
        return jnp.concatenate(
            [
                jnp.concatenate(
                    [
                        wide[j, pl.ds((side * channels + c) * rows + r, devices, stride=pitch), :].astype(BF16)
                        for r in range(rows)
                    ],
                    axis=0,
                )
                for j, _ in blocks(width)
            ],
            axis=1,
        )

    for c in range(channels):
        product = lax.dot_general(
            by_row(0, c), by_row(1, c), (((0,), (0,)), ((), ())), preferred_element_type=F32
        )
        for j, columns in blocks(width):
            natural[c, j] = product[:, columns]
            for r in range(rows):
                turned[j, pl.ds(c * rows + r, devices, stride=out_pitch), :] = natural[
                    c, j, pl.ds(r, devices, stride=rows), :
                ]
    for s in range(devices):
        for j, columns in blocks(width):
            out[s, :, columns] = turned[j, s * out_pitch : s * out_pitch + channels * rows, :].astype(BF16)


def finish(group, width, tri, gate, x_t, w_t, gain, bias):
    rows = tri.shape[1] // HC
    normed = jnp.concatenate(
        [
            norm_channels(tri[j, pl.ds(r, HC, stride=rows), :], gain, bias).astype(BF16)
            for r in group
            for j, _ in blocks(width)
        ],
        axis=1,
    )
    branch = jnp.dot(w_t, normed, preferred_element_type=F32)
    return {
        (r, j): (
            x_t[r, :, columns].astype(F32)
            + gate[r, :, columns] * branch[:, k * width + j * 128 : k * width + (j + 1) * 128]
        ).astype(BF16)
        for k, r in enumerate(group)
        for j, columns in blocks(width)
    }


def middle_kernel(recv, gate, x_t, marks, row_marks, weights, vectors, out, new_t, slabs, tri):
    rows, _, width = x_t.shape
    widen(recv, tri, recv.shape[1])

    def prepare(group):
        mid = (vectors[MID_GAIN[0]], vectors[MID_BIAS[0]])
        states = finish(group, width, tri, gate, x_t, weights[W_OUT[0], :], *mid)
        parts = []
        for r in group:
            for j, columns in blocks(width):
                new_t[r, :, columns] = states[r, j]
                same = same_chain(marks, row_marks, r, columns)
                parts.append(
                    norm_input(states[r, j].astype(F32), same, vectors[GAIN], vectors[BIAS], vectors[EMBED])
                )
        return jnp.concatenate(parts, axis=1)

    def consume(group, normed):
        project(group, normed, marks, row_marks, weights[W_AB, :], slabs)

    overlapped(rows, prepare, consume)
    write_slabs(slabs, out)


def last_kernel(recv, gate, x_t, w_t, vectors, out, tri):
    rows, _, width = x_t.shape
    widen(recv, tri, recv.shape[1])
    for group in groups(rows):
        for (r, j), state in finish(group, width, tri, gate, x_t, w_t[...], vectors[0], vectors[1]).items():
            out[r, j * 128 : (j + 1) * 128, :] = state.astype(F32).T.astype(BF16)


def call(kernel, outs, scratch, arrays, anywhere, flops, limit=VMEM_LIMIT):
    size = sum(a.size * a.dtype.itemsize for a in list(arrays) + list(outs))
    return pl.pallas_call(
        kernel,
        out_shape=outs,
        in_specs=[WHOLE] * len(arrays) + [ANYWHERE] * len(anywhere),
        out_specs=[WHOLE] * len(outs),
        scratch_shapes=scratch,
        compiler_params=pltpu.CompilerParams(vmem_limit_bytes=limit),
        cost_estimate=pl.CostEstimate(flops=flops, bytes_accessed=size, transcendentals=0),
    )(*arrays, *anywhere)


def local(
    pair, residue_mask, chain_ids, ln_in_gain, ln_in_bias, chain_embed, w_ab, w_gate, ln_mid_gain, ln_mid_bias, w_out
):
    rows, width, _ = pair.shape
    devices = lax.axis_size("row")
    half = devices // 2
    channels = HC // devices
    cols = width // 128
    pairs = rows * width

    sent = jax.ShapeDtypeStruct((devices, 2 * channels * rows, width), BF16)
    back = jax.ShapeDtypeStruct((devices, channels * rows, width), BF16)
    own_back = jax.ShapeDtypeStruct((half, 2 * channels * rows, width), BF16)
    own_slab = jax.ShapeDtypeStruct((2 * channels * rows, width), BF16)
    state_t = jax.ShapeDtypeStruct((rows, C, width), BF16)
    gate_t = jax.ShapeDtypeStruct((rows, C, width), F32)
    mark = jax.ShapeDtypeStruct((2, width), F32)
    row_mark = jax.ShapeDtypeStruct((2, (rows + 7) // 8 * 8, 128), F32)
    turned = jax.ShapeDtypeStruct((7 * HC, C), BF16)
    columns = jax.ShapeDtypeStruct((7, C, 128), F32)

    vector = pltpu.VMEM((C, 128), F32)
    ids = pltpu.VMEM((width,), jnp.int32)
    w_wide = pltpu.VMEM((C, 4 * HC), BF16)
    slabs_wide = pltpu.VMEM((cols, 2 * HC * rows, 128), F32)
    own_spread = pltpu.VMEM((cols, half * spread(2 * channels * rows), 128), F32)
    all_spread = pltpu.VMEM((cols, devices * spread(2 * channels * rows), 128), F32)
    back_spread = pltpu.VMEM((cols, devices * spread(channels * rows), 128), F32)
    tri_wide = pltpu.VMEM((cols, HC * rows, 128), F32)
    norms = (ln_in_gain, ln_in_bias, chain_embed)

    def sems(n):
        return pltpu.SemaphoreType.DMA((n,))

    def exchange(slabs, groups=None):
        return lax.all_to_all(
            slabs, "row", split_axis=0, concat_axis=0, tiled=True, axis_index_groups=groups
        )

    halves = [list(range(h * half, (h + 1) * half)) for h in range(2)]
    *own, slabs, x_t, marks, row_marks = call(
        first_kernel, [own_slab] * half + [sent, state_t, mark, row_mark],
        [
            pltpu.VMEM(pair.shape, BF16), w_wide, pltpu.VMEM((3, 2, C), F32), ids, ids, pltpu.VMEM((4 * HC, C), BF16),
            vector, vector, vector, slabs_wide, sems(6), sems(len(groups(rows))),
        ],
        (), (residue_mask, chain_ids, pair, *norms, w_ab), 2 * pairs * C * 4 * HC, FIRST_VMEM_LIMIT,
    )
    recv = exchange(slabs)
    own = [own[0]] + [lax.ppermute(own[o], "row", [(i, i ^ o) for i in range(devices)]) for o in range(1, half)]
    gate, weights, vectors = call(
        gate_kernel, [gate_t, turned, columns],
        [pltpu.VMEM((5, 2, C), F32), pltpu.VMEM((2, 2, C, C), BF16), w_wide, sems(8)],
        (x_t, marks, row_marks), (*norms, w_gate, w_ab, ln_mid_gain, ln_mid_bias, w_out), 2 * pairs * C * C,
    )
    products = call(
        functools.partial(first_products_kernel, rows), [own_back],
        [
            own_spread, all_spread, pltpu.VMEM((2 * channels, cols, width, 128), F32), own_spread,
        ],
        (recv, *own), (), 2 * channels * width**3, PRODUCTS_VMEM_LIMIT,
    )[0]
    tri = exchange(products, halves)
    slabs, x_t = call(
        middle_kernel, [sent, state_t], [slabs_wide, tri_wide],
        (tri, gate, x_t, marks, row_marks, weights, vectors), (), 2 * pairs * C * 5 * HC,
    )
    recv = exchange(slabs)
    w_last = jax.ShapeDtypeStruct((HC, C), BF16)
    columns_last = jax.ShapeDtypeStruct((2, C, 128), F32)
    gate, x_t, weights, vectors = call(
        second_gate_kernel, [gate_t, state_t, w_last, columns_last], [], (x_t, marks, row_marks, weights, vectors), (),
        2 * pairs * C * C,
    )
    recv, gate, x_t, weights, vectors = lax.optimization_barrier((recv, gate, x_t, weights, vectors))
    products = call(
        functools.partial(second_products_kernel, rows), [back],
        [all_spread, pltpu.VMEM((channels, cols, width, 128), F32), back_spread], (recv,), (), 2 * channels * width**3,
    )[0]
    tri = exchange(products)
    return call(
        last_kernel, [jax.ShapeDtypeStruct(pair.shape, BF16)], [tri_wide], (tri, gate, x_t, weights, vectors), (),
        2 * pairs * C * C,
    )[0]


def solution(mesh):
    in_specs = (P(("grp", "row"), None, None), P("grp"), P("grp")) + (P(),) * 8
    out_specs = P(("grp", "row"), None, None)
    return jax.shard_map(local, mesh=mesh, in_specs=in_specs, out_specs=out_specs, check_vma=False)
```

```python
import functools

import jax
import jax.numpy as jnp
from jax import lax
from jax.experimental import pallas as pl
from jax.experimental.pallas import tpu as pltpu
from jax.sharding import PartitionSpec as P

C = 128
HC = 128
EPS = 1e-05
F32 = jnp.float32
BF16 = jnp.bfloat16
VMEM_LIMIT = 32 * 1024 * 1024
PRODUCTS_VMEM_LIMIT = 60 * 1024 * 1024
FIRST_VMEM_LIMIT = 60 * 1024 * 1024
GROUP = 4

WHOLE = pl.BlockSpec(memory_space=pltpu.VMEM)
ANYWHERE = pl.BlockSpec(memory_space=pl.ANY)


def blocks(width):
    return [(j, slice(j * 128, (j + 1) * 128)) for j in range(width // 128)]


def column(vector_ref, layer):
    return jnp.broadcast_to(vector_ref[layer : layer + 1, :], (C, C)).T


def turn(ref):
    return ref[...].astype(F32).T.astype(BF16)


def norm_channels(values, gain, bias):
    mean = jnp.sum(values, axis=0, keepdims=True) * (1.0 / C)
    centred = values - mean
    var = jnp.sum(centred * centred, axis=0, keepdims=True) * (1.0 / C)
    return centred * lax.rsqrt(var + EPS) * gain + bias


def norm_input(values, same, g, b, e):
    return (norm_channels(values, g, b) + same * e).astype(BF16)


def same_chain(marks, row_marks, r, columns):
    return (marks[1:2, columns] == row_marks[1, r : r + 1, :]).astype(F32)


def project(group, normed, marks, row_marks, w_t, slabs):
    rows = slabs.shape[1] // (2 * HC)
    width = slabs.shape[0] * 128
    proj = jnp.dot(w_t, normed, preferred_element_type=F32)
    for k, r in enumerate(group):
        for j, columns in blocks(width):
            mask = marks[0:1, columns] * row_marks[0, r : r + 1, :]
            for side in range(2):
                p = proj[2 * side * HC : (2 * side + 2) * HC, k * width + j * 128 : k * width + (j + 1) * 128]
                value = jax.nn.sigmoid(p[:HC]) * p[HC:] * mask
                slabs[j, pl.ds(side * HC * rows + r, HC, stride=rows), :] = value


def write_slabs(slabs, out):
    devices, depth, width = out.shape
    half = depth // 2
    for side in range(2):
        for d in range(devices):
            start = (side * devices + d) * half
            for j, columns in blocks(width):
                out[d, side * half : (side + 1) * half, columns] = slabs[j, start : start + half, :].astype(BF16)


def over(count, body):
    if count <= 16:
        for i in range(count):
            body(i)
    else:
        lax.fori_loop(0, count, lambda i, carry: (body(i), carry)[1], 0)


def write_crossing(slabs, out, own):
    devices, depth, width = out.shape
    half = devices // 2
    me = lax.axis_index("row")
    mine = me // half * half
    side_rows = half * depth

    def slab(q):
        for first, side in ((mine, 0), (half - mine, side_rows)):
            for j, columns in blocks(width):
                out[first + q, :, columns] = slabs[j, pl.ds(side + q * depth, depth), :].astype(BF16)

    over(half, slab)
    for o, ref in enumerate(own):
        start = pl.multiple_of(side_rows + (me % half ^ o) * depth, 8)
        for j, columns in blocks(width):
            ref[:, columns] = slabs[j, pl.ds(start, depth), :].astype(BF16)


def spread(depth):
    return depth + 4 if depth % 8 == 0 else depth


def widen(recv, wide, pitch):
    devices, depth, width = recv.shape
    for s in range(devices):
        for j, columns in blocks(width):
            wide[j, s * pitch : s * pitch + depth, :] = recv[s, :, columns].astype(F32)


def fetch(pairs, sems):
    copies = [pltpu.make_async_copy(src, dst, sems.at[i]) for i, (src, dst) in enumerate(pairs)]
    for copy in copies:
        copy.start()
    return copies


def groups(rows):
    return [range(i, min(i + GROUP, rows)) for i in range(0, rows, GROUP)]


def overlapped(rows, prepare, consume):
    todo = groups(rows)
    ready = prepare(todo[0])
    for i, group in enumerate(todo):
        current = ready
        if i + 1 < len(todo):
            ready = prepare(todo[i + 1])
        consume(group, current)


def first_kernel(residue_mask, chain_ids, x_in, gain, bias, embed, w_ab, *refs):
    own = refs[:-16]
    out, x_t, marks, row_marks, x, w, vectors, mask_ids, chain, w_t, g, b, e, slabs, sems, x_sems = refs[-16:]
    rows, width, _ = x.shape
    smalls = fetch(
        [
            (residue_mask, mask_ids), (chain_ids, chain), (gain, vectors.at[0]), (bias, vectors.at[1]),
            (embed, vectors.at[2]), (w_ab.at[0], w),
        ],
        sems,
    )
    larges = fetch([(x_in.at[pl.ds(r[0], len(r))], x.at[pl.ds(r[0], len(r))]) for r in groups(rows)], x_sems)
    for copy in smalls:
        copy.wait()
    w_t[...] = turn(w)
    g[...] = column(vectors.at[0], 0)
    b[...] = column(vectors.at[1], 0)
    e[...] = column(vectors.at[2], 0)
    shape = (row_marks.shape[1], width)
    start = lax.axis_index("row") * rows
    at_row = lax.broadcasted_iota(jnp.int32, shape, 1) == lax.broadcasted_iota(jnp.int32, shape, 0) + start
    for i, ref in enumerate((mask_ids, chain)):
        values = ref[...].astype(F32).reshape(1, width)
        marks[i : i + 1, :] = values
        picked = jnp.sum(jnp.where(at_row, values, 0.0), axis=1, keepdims=True)
        row_marks[i] = jnp.broadcast_to(picked, row_marks.shape[1:])

    def prepare(group):
        larges[group[0] // GROUP].wait()
        parts = []
        for r in group:
            for _, columns in blocks(width):
                values = x[r, columns, :].astype(F32).T
                x_t[r, :, columns] = values.astype(BF16)
                same = same_chain(marks, row_marks, r, columns)
                parts.append(norm_input(values, same, g[...], b[...], e[...]))
        return jnp.concatenate(parts, axis=1)

    def consume(group, normed):
        project(group, normed, marks, row_marks, w_t[...], slabs)

    overlapped(rows, prepare, consume)
    write_crossing(slabs, out, own)


def write_gates(x_t, marks, row_marks, g, b, e, w_t, out):
    rows, _, width = x_t.shape

    def prepare(group):
        return jnp.concatenate(
            [
                norm_input(x_t[r, :, columns].astype(F32), same_chain(marks, row_marks, r, columns), g, b, e)
                for r in group
                for _, columns in blocks(width)
            ],
            axis=1,
        )

    def consume(group, normed):
        gates = jax.nn.sigmoid(jnp.dot(w_t, normed, preferred_element_type=F32))
        for k, r in enumerate(group):
            out[r] = gates[:, k * width : (k + 1) * width]

    overlapped(rows, prepare, consume)


W_AB, W_OUT, W_GATE = slice(0, 4 * HC), [slice(4 * HC, 5 * HC), slice(5 * HC, 6 * HC)], slice(6 * HC, 7 * HC)
GAIN, BIAS, EMBED, MID_GAIN, MID_BIAS = 0, 1, 2, [3, 5], [4, 6]


def gate_kernel(
    x_t, marks, row_marks, gain, bias, embed, w_gate, w_ab, mid_gain, mid_bias, w_out, out, weights, columns_out,
    vectors, w_square, w_wide, sems,
):
    copies = fetch(
        [
            (gain, vectors.at[0]), (bias, vectors.at[1]), (embed, vectors.at[2]), (mid_gain, vectors.at[3]),
            (mid_bias, vectors.at[4]), (w_gate, w_square.at[0]), (w_out, w_square.at[1]), (w_ab.at[1], w_wide),
        ],
        sems,
    )
    for copy in copies:
        copy.wait()
    weights[W_AB, :] = turn(w_wide)
    weights[W_GATE, :] = turn(w_square.at[0, 1])
    for layer in range(2):
        weights[W_OUT[layer], :] = turn(w_square.at[1, layer])
        columns_out[MID_GAIN[layer]] = column(vectors.at[3], layer)
        columns_out[MID_BIAS[layer]] = column(vectors.at[4], layer)
    for i in (GAIN, BIAS, EMBED):
        columns_out[i] = column(vectors.at[i], 1)
    first = [column(vectors.at[i], 0) for i in (GAIN, BIAS, EMBED)]
    write_gates(x_t, marks, row_marks, *first, turn(w_square.at[0, 0]), out)


def second_gate_kernel(x_t, marks, row_marks, weights, columns, out, x_out, w_out, columns_out):
    x_out[...] = x_t[...]
    w_out[...] = weights[W_OUT[1], :]
    columns_out[0] = columns[MID_GAIN[1]]
    columns_out[1] = columns[MID_BIAS[1]]
    write_gates(x_t, marks, row_marks, columns[GAIN], columns[BIAS], columns[EMBED], weights[W_GATE, :], out)


def first_products_kernel(rows, recv, *refs):
    own, (out, left_wide, right_wide, natural, turned) = refs[:-5], refs[-5:]
    devices, depth, width = recv.shape
    half = devices // 2
    channels = depth // rows
    me = lax.axis_index("row")
    mine = me // half * half
    other = half - mine
    pitch = spread(depth)

    def slab(q):
        for j, columns in blocks(width):
            left_wide[j, pl.ds(q * pitch, depth), :] = recv[mine + q, :, columns].astype(F32)
            right_wide[j, pl.ds((other + q) * pitch, depth), :] = recv[other + q, :, columns].astype(F32)

    over(half, slab)
    for o, ref in enumerate(own):
        for j, columns in blocks(width):
            right_wide[j, pl.ds((mine + (me % half ^ o)) * pitch, depth), :] = ref[:, columns].astype(F32)
    for c in range(channels):
        left, right = [], []
        for j, _ in blocks(width):
            pieces = [left_wide[j, pl.ds(c * rows + r, half, stride=pitch), :].astype(BF16) for r in range(rows)]
            left.append(jnp.concatenate(pieces, axis=0))
            for r in range(rows):
                natural[c, j, pl.ds(r, devices, stride=rows), :] = right_wide[
                    j, pl.ds(c * rows + r, devices, stride=pitch), :
                ]
            right.append(natural[c, j].astype(BF16))
        product = lax.dot_general(
            jnp.concatenate(left, axis=1), jnp.concatenate(right, axis=1), (((1,), (1,)), ((), ())),
            preferred_element_type=F32,
        )
        for j, columns in blocks(width):
            for r in range(rows):
                turned[j, pl.ds(c * rows + r, half, stride=pitch), :] = product[r * half : (r + 1) * half, columns]
    for q in range(half):
        for j, columns in blocks(width):
            out[q, :, columns] = turned[j, q * pitch : q * pitch + depth, :].astype(BF16)


def second_products_kernel(rows, recv, out, wide, natural, turned):
    devices, depth, width = recv.shape
    channels = depth // (2 * rows)
    pitch, out_pitch = spread(depth), spread(channels * rows)
    widen(recv, wide, pitch)

    def by_row(side, c):
        return jnp.concatenate(
            [
                jnp.concatenate(
                    [
                        wide[j, pl.ds((side * channels + c) * rows + r, devices, stride=pitch), :].astype(BF16)
                        for r in range(rows)
                    ],
                    axis=0,
                )
                for j, _ in blocks(width)
            ],
            axis=1,
        )

    for c in range(channels):
        product = lax.dot_general(
            by_row(0, c), by_row(1, c), (((0,), (0,)), ((), ())), preferred_element_type=F32
        )
        for j, columns in blocks(width):
            natural[c, j] = product[:, columns]
            for r in range(rows):
                turned[j, pl.ds(c * rows + r, devices, stride=out_pitch), :] = natural[
                    c, j, pl.ds(r, devices, stride=rows), :
                ]
    for s in range(devices):
        for j, columns in blocks(width):
            out[s, :, columns] = turned[j, s * out_pitch : s * out_pitch + channels * rows, :].astype(BF16)


def finish(group, width, tri, gate, x_t, w_t, gain, bias):
    rows = tri.shape[1] // HC
    normed = jnp.concatenate(
        [
            norm_channels(tri[j, pl.ds(r, HC, stride=rows), :], gain, bias).astype(BF16)
            for r in group
            for j, _ in blocks(width)
        ],
        axis=1,
    )
    branch = jnp.dot(w_t, normed, preferred_element_type=F32)
    return {
        (r, j): (
            x_t[r, :, columns].astype(F32)
            + gate[r, :, columns] * branch[:, k * width + j * 128 : k * width + (j + 1) * 128]
        ).astype(BF16)
        for k, r in enumerate(group)
        for j, columns in blocks(width)
    }


def middle_kernel(recv, gate, x_t, marks, row_marks, weights, vectors, out, new_t, slabs, tri):
    rows, _, width = x_t.shape
    widen(recv, tri, recv.shape[1])

    def prepare(group):
        mid = (vectors[MID_GAIN[0]], vectors[MID_BIAS[0]])
        states = finish(group, width, tri, gate, x_t, weights[W_OUT[0], :], *mid)
        parts = []
        for r in group:
            for j, columns in blocks(width):
                new_t[r, :, columns] = states[r, j]
                same = same_chain(marks, row_marks, r, columns)
                parts.append(
                    norm_input(states[r, j].astype(F32), same, vectors[GAIN], vectors[BIAS], vectors[EMBED])
                )
        return jnp.concatenate(parts, axis=1)

    def consume(group, normed):
        project(group, normed, marks, row_marks, weights[W_AB, :], slabs)

    overlapped(rows, prepare, consume)
    write_slabs(slabs, out)


def last_kernel(recv, gate, x_t, w_t, vectors, out, tri):
    rows, _, width = x_t.shape
    widen(recv, tri, recv.shape[1])
    for group in groups(rows):
        for (r, j), state in finish(group, width, tri, gate, x_t, w_t[...], vectors[0], vectors[1]).items():
            out[r, j * 128 : (j + 1) * 128, :] = state.astype(F32).T.astype(BF16)


def call(kernel, outs, scratch, arrays, anywhere, flops, limit=VMEM_LIMIT):
    size = sum(a.size * a.dtype.itemsize for a in list(arrays) + list(outs))
    return pl.pallas_call(
        kernel,
        out_shape=outs,
        in_specs=[WHOLE] * len(arrays) + [ANYWHERE] * len(anywhere),
        out_specs=[WHOLE] * len(outs),
        scratch_shapes=scratch,
        compiler_params=pltpu.CompilerParams(vmem_limit_bytes=limit),
        cost_estimate=pl.CostEstimate(flops=flops, bytes_accessed=size, transcendentals=0),
    )(*arrays, *anywhere)


def local(
    pair, residue_mask, chain_ids, ln_in_gain, ln_in_bias, chain_embed, w_ab, w_gate, ln_mid_gain, ln_mid_bias, w_out
):
    rows, width, _ = pair.shape
    devices = lax.axis_size("row")
    half = devices // 2
    channels = HC // devices
    cols = width // 128
    pairs = rows * width

    sent = jax.ShapeDtypeStruct((devices, 2 * channels * rows, width), BF16)
    back = jax.ShapeDtypeStruct((devices, channels * rows, width), BF16)
    own_back = jax.ShapeDtypeStruct((half, 2 * channels * rows, width), BF16)
    own_slab = jax.ShapeDtypeStruct((2 * channels * rows, width), BF16)
    state_t = jax.ShapeDtypeStruct((rows, C, width), BF16)
    gate_t = jax.ShapeDtypeStruct((rows, C, width), F32)
    mark = jax.ShapeDtypeStruct((2, width), F32)
    row_mark = jax.ShapeDtypeStruct((2, (rows + 7) // 8 * 8, 128), F32)
    turned = jax.ShapeDtypeStruct((7 * HC, C), BF16)
    columns = jax.ShapeDtypeStruct((7, C, 128), F32)

    vector = pltpu.VMEM((C, 128), F32)
    ids = pltpu.VMEM((width,), jnp.int32)
    w_wide = pltpu.VMEM((C, 4 * HC), BF16)
    slabs_wide = pltpu.VMEM((cols, 2 * HC * rows, 128), F32)
    own_spread = pltpu.VMEM((cols, half * spread(2 * channels * rows), 128), F32)
    all_spread = pltpu.VMEM((cols, devices * spread(2 * channels * rows), 128), F32)
    back_spread = pltpu.VMEM((cols, devices * spread(channels * rows), 128), F32)
    tri_wide = pltpu.VMEM((cols, HC * rows, 128), F32)
    norms = (ln_in_gain, ln_in_bias, chain_embed)

    def sems(n):
        return pltpu.SemaphoreType.DMA((n,))

    def exchange(slabs, groups=None):
        return lax.all_to_all(
            slabs, "row", split_axis=0, concat_axis=0, tiled=True, axis_index_groups=groups
        )

    halves = [list(range(h * half, (h + 1) * half)) for h in range(2)]
    *own, slabs, x_t, marks, row_marks = call(
        first_kernel, [own_slab] * half + [sent, state_t, mark, row_mark],
        [
            pltpu.VMEM(pair.shape, BF16), w_wide, pltpu.VMEM((3, 2, C), F32), ids, ids, pltpu.VMEM((4 * HC, C), BF16),
            vector, vector, vector, slabs_wide, sems(6), sems(len(groups(rows))),
        ],
        (), (residue_mask, chain_ids, pair, *norms, w_ab), 2 * pairs * C * 4 * HC, FIRST_VMEM_LIMIT,
    )
    recv = exchange(slabs)
    gate, weights, vectors = call(
        gate_kernel, [gate_t, turned, columns],
        [pltpu.VMEM((5, 2, C), F32), pltpu.VMEM((2, 2, C, C), BF16), w_wide, sems(8)],
        (x_t, marks, row_marks), (*norms, w_gate, w_ab, ln_mid_gain, ln_mid_bias, w_out), 2 * pairs * C * C,
    )
    gate, weights, vectors, *own[5:] = lax.optimization_barrier((gate, weights, vectors, *own[5:]))
    own = [own[0]] + [lax.ppermute(own[o], "row", [(i, i ^ o) for i in range(devices)]) for o in range(1, half)]
    products = call(
        functools.partial(first_products_kernel, rows), [own_back],
        [
            own_spread, all_spread, pltpu.VMEM((2 * channels, cols, width, 128), F32), own_spread,
        ],
        (recv, *own), (), 2 * channels * width**3, PRODUCTS_VMEM_LIMIT,
    )[0]
    tri = exchange(products, halves)
    slabs, x_t = call(
        middle_kernel, [sent, state_t], [slabs_wide, tri_wide],
        (tri, gate, x_t, marks, row_marks, weights, vectors), (), 2 * pairs * C * 5 * HC,
    )
    recv = exchange(slabs)
    w_last = jax.ShapeDtypeStruct((HC, C), BF16)
    columns_last = jax.ShapeDtypeStruct((2, C, 128), F32)
    gate, x_t, weights, vectors = call(
        second_gate_kernel, [gate_t, state_t, w_last, columns_last], [], (x_t, marks, row_marks, weights, vectors), (),
        2 * pairs * C * C,
    )
    recv, gate, x_t, weights, vectors = lax.optimization_barrier((recv, gate, x_t, weights, vectors))
    products = call(
        functools.partial(second_products_kernel, rows), [back],
        [all_spread, pltpu.VMEM((channels, cols, width, 128), F32), back_spread], (recv,), (), 2 * channels * width**3,
    )[0]
    tri = exchange(products)
    return call(
        last_kernel, [jax.ShapeDtypeStruct(pair.shape, BF16)], [tri_wide], (tri, gate, x_t, weights, vectors), (),
        2 * pairs * C * C,
    )[0]


def solution(mesh):
    in_specs = (P(("grp", "row"), None, None), P("grp"), P("grp")) + (P(),) * 8
    out_specs = P(("grp", "row"), None, None)
    return jax.shard_map(local, mesh=mesh, in_specs=in_specs, out_specs=out_specs, check_vma=False)
```

```python
import functools

import jax
import jax.numpy as jnp
from jax import lax
from jax.experimental import pallas as pl
from jax.experimental.pallas import tpu as pltpu
from jax.sharding import PartitionSpec as P

C = 128
HC = 128
EPS = 1e-05
F32 = jnp.float32
BF16 = jnp.bfloat16
VMEM_LIMIT = 32 * 1024 * 1024
PRODUCTS_VMEM_LIMIT = 60 * 1024 * 1024
FIRST_VMEM_LIMIT = 60 * 1024 * 1024
GROUP = 6

WHOLE = pl.BlockSpec(memory_space=pltpu.VMEM)
ANYWHERE = pl.BlockSpec(memory_space=pl.ANY)


def blocks(width):
    return [(j, slice(j * 128, (j + 1) * 128)) for j in range(width // 128)]


def column(vector_ref, layer):
    return jnp.broadcast_to(vector_ref[layer : layer + 1, :], (C, C)).T


def turn(ref):
    return ref[...].astype(F32).T.astype(BF16)


def norm_channels(values, gain, bias):
    mean = jnp.sum(values, axis=0, keepdims=True) * (1.0 / C)
    centred = values - mean
    var = jnp.sum(centred * centred, axis=0, keepdims=True) * (1.0 / C)
    return centred * lax.rsqrt(var + EPS) * gain + bias


def norm_input(values, same, g, b, e):
    return (norm_channels(values, g, b) + same * e).astype(BF16)


def same_chain(marks, row_marks, r, columns):
    return (marks[1:2, columns] == row_marks[1, r : r + 1, :]).astype(F32)


def project(group, normed, marks, row_marks, w_t, slabs):
    rows = slabs.shape[1] // (2 * HC)
    width = slabs.shape[0] * 128
    proj = jnp.dot(w_t, normed, preferred_element_type=F32)
    for k, r in enumerate(group):
        for j, columns in blocks(width):
            mask = marks[0:1, columns] * row_marks[0, r : r + 1, :]
            for side in range(2):
                p = proj[2 * side * HC : (2 * side + 2) * HC, k * width + j * 128 : k * width + (j + 1) * 128]
                value = jax.nn.sigmoid(p[:HC]) * p[HC:] * mask
                slabs[j, pl.ds(side * HC * rows + r, HC, stride=rows), :] = value


def write_slabs(slabs, out):
    devices, depth, width = out.shape
    half = depth // 2
    for side in range(2):
        for d in range(devices):
            start = (side * devices + d) * half
            for j, columns in blocks(width):
                out[d, side * half : (side + 1) * half, columns] = slabs[j, start : start + half, :].astype(BF16)


def over(count, body):
    if count <= 16:
        for i in range(count):
            body(i)
    else:
        lax.fori_loop(0, count, lambda i, carry: (body(i), carry)[1], 0)


def write_crossing(slabs, out, own):
    devices, depth, width = out.shape
    half = devices // 2
    me = lax.axis_index("row")
    mine = me // half * half
    side_rows = half * depth

    def slab(q):
        for first, side in ((mine, 0), (half - mine, side_rows)):
            for j, columns in blocks(width):
                out[first + q, :, columns] = slabs[j, pl.ds(side + q * depth, depth), :].astype(BF16)

    over(half, slab)
    for o, ref in enumerate(own):
        start = pl.multiple_of(side_rows + (me % half ^ o) * depth, 8)
        for j, columns in blocks(width):
            ref[:, columns] = slabs[j, pl.ds(start, depth), :].astype(BF16)


def spread(depth):
    return depth + 4 if depth % 8 == 0 else depth


def widen(recv, wide, pitch):
    devices, depth, width = recv.shape
    for s in range(devices):
        for j, columns in blocks(width):
            wide[j, s * pitch : s * pitch + depth, :] = recv[s, :, columns].astype(F32)


def fetch(pairs, sems):
    copies = [pltpu.make_async_copy(src, dst, sems.at[i]) for i, (src, dst) in enumerate(pairs)]
    for copy in copies:
        copy.start()
    return copies


def groups(rows):
    return [range(i, min(i + GROUP, rows)) for i in range(0, rows, GROUP)]


def overlapped(rows, prepare, consume):
    todo = groups(rows)
    ready = prepare(todo[0])
    for i, group in enumerate(todo):
        current = ready
        if i + 1 < len(todo):
            ready = prepare(todo[i + 1])
        consume(group, current)


def first_kernel(residue_mask, chain_ids, x_in, gain, bias, embed, w_ab, *refs):
    own = refs[:-16]
    out, x_t, marks, row_marks, x, w, vectors, mask_ids, chain, w_t, g, b, e, slabs, sems, x_sems = refs[-16:]
    rows, width, _ = x.shape
    smalls = fetch(
        [
            (residue_mask, mask_ids), (chain_ids, chain), (gain, vectors.at[0]), (bias, vectors.at[1]),
            (embed, vectors.at[2]), (w_ab.at[0], w),
        ],
        sems,
    )
    larges = fetch([(x_in.at[pl.ds(r[0], len(r))], x.at[pl.ds(r[0], len(r))]) for r in groups(rows)], x_sems)
    for copy in smalls:
        copy.wait()
    w_t[...] = turn(w)
    g[...] = column(vectors.at[0], 0)
    b[...] = column(vectors.at[1], 0)
    e[...] = column(vectors.at[2], 0)
    shape = (row_marks.shape[1], width)
    start = lax.axis_index("row") * rows
    at_row = lax.broadcasted_iota(jnp.int32, shape, 1) == lax.broadcasted_iota(jnp.int32, shape, 0) + start
    for i, ref in enumerate((mask_ids, chain)):
        values = ref[...].astype(F32).reshape(1, width)
        marks[i : i + 1, :] = values
        picked = jnp.sum(jnp.where(at_row, values, 0.0), axis=1, keepdims=True)
        row_marks[i] = jnp.broadcast_to(picked, row_marks.shape[1:])

    def prepare(group):
        larges[group[0] // GROUP].wait()
        parts = []
        for r in group:
            for _, columns in blocks(width):
                values = x[r, columns, :].astype(F32).T
                x_t[r, :, columns] = values.astype(BF16)
                same = same_chain(marks, row_marks, r, columns)
                parts.append(norm_input(values, same, g[...], b[...], e[...]))
        return jnp.concatenate(parts, axis=1)

    def consume(group, normed):
        project(group, normed, marks, row_marks, w_t[...], slabs)

    overlapped(rows, prepare, consume)
    write_crossing(slabs, out, own)


def write_gates(x_t, marks, row_marks, g, b, e, w_t, out):
    rows, _, width = x_t.shape

    def prepare(group):
        return jnp.concatenate(
            [
                norm_input(x_t[r, :, columns].astype(F32), same_chain(marks, row_marks, r, columns), g, b, e)
                for r in group
                for _, columns in blocks(width)
            ],
            axis=1,
        )

    def consume(group, normed):
        gates = jax.nn.sigmoid(jnp.dot(w_t, normed, preferred_element_type=F32))
        for k, r in enumerate(group):
            out[r] = gates[:, k * width : (k + 1) * width]

    overlapped(rows, prepare, consume)


W_AB, W_OUT, W_GATE = slice(0, 4 * HC), [slice(4 * HC, 5 * HC), slice(5 * HC, 6 * HC)], slice(6 * HC, 7 * HC)
GAIN, BIAS, EMBED, MID_GAIN, MID_BIAS = 0, 1, 2, [3, 5], [4, 6]


def gate_kernel(
    x_t, marks, row_marks, gain, bias, embed, w_gate, w_ab, mid_gain, mid_bias, w_out, out, weights, columns_out,
    vectors, w_square, w_wide, sems,
):
    copies = fetch(
        [
            (gain, vectors.at[0]), (bias, vectors.at[1]), (embed, vectors.at[2]), (mid_gain, vectors.at[3]),
            (mid_bias, vectors.at[4]), (w_gate, w_square.at[0]), (w_out, w_square.at[1]), (w_ab.at[1], w_wide),
        ],
        sems,
    )
    for copy in copies:
        copy.wait()
    weights[W_AB, :] = turn(w_wide)
    weights[W_GATE, :] = turn(w_square.at[0, 1])
    for layer in range(2):
        weights[W_OUT[layer], :] = turn(w_square.at[1, layer])
        columns_out[MID_GAIN[layer]] = column(vectors.at[3], layer)
        columns_out[MID_BIAS[layer]] = column(vectors.at[4], layer)
    for i in (GAIN, BIAS, EMBED):
        columns_out[i] = column(vectors.at[i], 1)
    first = [column(vectors.at[i], 0) for i in (GAIN, BIAS, EMBED)]
    write_gates(x_t, marks, row_marks, *first, turn(w_square.at[0, 0]), out)


def second_gate_kernel(x_t, marks, row_marks, weights, columns, out, x_out, w_out, columns_out):
    x_out[...] = x_t[...]
    w_out[...] = weights[W_OUT[1], :]
    columns_out[0] = columns[MID_GAIN[1]]
    columns_out[1] = columns[MID_BIAS[1]]
    write_gates(x_t, marks, row_marks, columns[GAIN], columns[BIAS], columns[EMBED], weights[W_GATE, :], out)


def first_products_kernel(rows, recv, *refs):
    own, (out, left_wide, right_wide, natural, turned) = refs[:-5], refs[-5:]
    devices, depth, width = recv.shape
    half = devices // 2
    channels = depth // rows
    me = lax.axis_index("row")
    mine = me // half * half
    other = half - mine
    pitch = spread(depth)

    def slab(q):
        for j, columns in blocks(width):
            left_wide[j, pl.ds(q * pitch, depth), :] = recv[mine + q, :, columns].astype(F32)
            right_wide[j, pl.ds((other + q) * pitch, depth), :] = recv[other + q, :, columns].astype(F32)

    over(half, slab)
    for o, ref in enumerate(own):
        for j, columns in blocks(width):
            right_wide[j, pl.ds((mine + (me % half ^ o)) * pitch, depth), :] = ref[:, columns].astype(F32)
    for c in range(channels):
        left, right = [], []
        for j, _ in blocks(width):
            pieces = [left_wide[j, pl.ds(c * rows + r, half, stride=pitch), :].astype(BF16) for r in range(rows)]
            left.append(jnp.concatenate(pieces, axis=0))
            for r in range(rows):
                natural[c, j, pl.ds(r, devices, stride=rows), :] = right_wide[
                    j, pl.ds(c * rows + r, devices, stride=pitch), :
                ]
            right.append(natural[c, j].astype(BF16))
        product = lax.dot_general(
            jnp.concatenate(left, axis=1), jnp.concatenate(right, axis=1), (((1,), (1,)), ((), ())),
            preferred_element_type=F32,
        )
        for j, columns in blocks(width):
            for r in range(rows):
                turned[j, pl.ds(c * rows + r, half, stride=pitch), :] = product[r * half : (r + 1) * half, columns]
    for q in range(half):
        for j, columns in blocks(width):
            out[q, :, columns] = turned[j, q * pitch : q * pitch + depth, :].astype(BF16)


def second_products_kernel(rows, recv, out, wide, natural, turned):
    devices, depth, width = recv.shape
    channels = depth // (2 * rows)
    pitch, out_pitch = spread(depth), spread(channels * rows)
    widen(recv, wide, pitch)

    def by_row(side, c):
        return jnp.concatenate(
            [
                jnp.concatenate(
                    [
                        wide[j, pl.ds((side * channels + c) * rows + r, devices, stride=pitch), :].astype(BF16)
                        for r in range(rows)
                    ],
                    axis=0,
                )
                for j, _ in blocks(width)
            ],
            axis=1,
        )

    for c in range(channels):
        product = lax.dot_general(
            by_row(0, c), by_row(1, c), (((0,), (0,)), ((), ())), preferred_element_type=F32
        )
        for j, columns in blocks(width):
            natural[c, j] = product[:, columns]
            for r in range(rows):
                turned[j, pl.ds(c * rows + r, devices, stride=out_pitch), :] = natural[
                    c, j, pl.ds(r, devices, stride=rows), :
                ]
    for s in range(devices):
        for j, columns in blocks(width):
            out[s, :, columns] = turned[j, s * out_pitch : s * out_pitch + channels * rows, :].astype(BF16)


def finish(group, width, tri, gate, x_t, w_t, gain, bias):
    rows = tri.shape[1] // HC
    normed = jnp.concatenate(
        [
            norm_channels(tri[j, pl.ds(r, HC, stride=rows), :], gain, bias).astype(BF16)
            for r in group
            for j, _ in blocks(width)
        ],
        axis=1,
    )
    branch = jnp.dot(w_t, normed, preferred_element_type=F32)
    return {
        (r, j): (
            x_t[r, :, columns].astype(F32)
            + gate[r, :, columns] * branch[:, k * width + j * 128 : k * width + (j + 1) * 128]
        ).astype(BF16)
        for k, r in enumerate(group)
        for j, columns in blocks(width)
    }


def middle_kernel(recv, gate, x_t, marks, row_marks, weights, vectors, out, new_t, slabs, tri):
    rows, _, width = x_t.shape
    widen(recv, tri, recv.shape[1])

    def prepare(group):
        mid = (vectors[MID_GAIN[0]], vectors[MID_BIAS[0]])
        states = finish(group, width, tri, gate, x_t, weights[W_OUT[0], :], *mid)
        parts = []
        for r in group:
            for j, columns in blocks(width):
                new_t[r, :, columns] = states[r, j]
                same = same_chain(marks, row_marks, r, columns)
                parts.append(
                    norm_input(states[r, j].astype(F32), same, vectors[GAIN], vectors[BIAS], vectors[EMBED])
                )
        return jnp.concatenate(parts, axis=1)

    def consume(group, normed):
        project(group, normed, marks, row_marks, weights[W_AB, :], slabs)

    overlapped(rows, prepare, consume)
    write_slabs(slabs, out)


def last_kernel(recv, gate, x_t, w_t, vectors, out, tri):
    rows, _, width = x_t.shape
    widen(recv, tri, recv.shape[1])
    for group in groups(rows):
        for (r, j), state in finish(group, width, tri, gate, x_t, w_t[...], vectors[0], vectors[1]).items():
            out[r, j * 128 : (j + 1) * 128, :] = state.astype(F32).T.astype(BF16)


def call(kernel, outs, scratch, arrays, anywhere, flops, limit=VMEM_LIMIT):
    size = sum(a.size * a.dtype.itemsize for a in list(arrays) + list(outs))
    return pl.pallas_call(
        kernel,
        out_shape=outs,
        in_specs=[WHOLE] * len(arrays) + [ANYWHERE] * len(anywhere),
        out_specs=[WHOLE] * len(outs),
        scratch_shapes=scratch,
        compiler_params=pltpu.CompilerParams(vmem_limit_bytes=limit),
        cost_estimate=pl.CostEstimate(flops=flops, bytes_accessed=size, transcendentals=0),
    )(*arrays, *anywhere)


def local(
    pair, residue_mask, chain_ids, ln_in_gain, ln_in_bias, chain_embed, w_ab, w_gate, ln_mid_gain, ln_mid_bias, w_out
):
    rows, width, _ = pair.shape
    devices = lax.axis_size("row")
    half = devices // 2
    channels = HC // devices
    cols = width // 128
    pairs = rows * width

    sent = jax.ShapeDtypeStruct((devices, 2 * channels * rows, width), BF16)
    back = jax.ShapeDtypeStruct((devices, channels * rows, width), BF16)
    own_back = jax.ShapeDtypeStruct((half, 2 * channels * rows, width), BF16)
    own_slab = jax.ShapeDtypeStruct((2 * channels * rows, width), BF16)
    state_t = jax.ShapeDtypeStruct((rows, C, width), BF16)
    gate_t = jax.ShapeDtypeStruct((rows, C, width), F32)
    mark = jax.ShapeDtypeStruct((2, width), F32)
    row_mark = jax.ShapeDtypeStruct((2, (rows + 7) // 8 * 8, 128), F32)
    turned = jax.ShapeDtypeStruct((7 * HC, C), BF16)
    columns = jax.ShapeDtypeStruct((7, C, 128), F32)

    vector = pltpu.VMEM((C, 128), F32)
    ids = pltpu.VMEM((width,), jnp.int32)
    w_wide = pltpu.VMEM((C, 4 * HC), BF16)
    slabs_wide = pltpu.VMEM((cols, 2 * HC * rows, 128), F32)
    own_spread = pltpu.VMEM((cols, half * spread(2 * channels * rows), 128), F32)
    all_spread = pltpu.VMEM((cols, devices * spread(2 * channels * rows), 128), F32)
    back_spread = pltpu.VMEM((cols, devices * spread(channels * rows), 128), F32)
    tri_wide = pltpu.VMEM((cols, HC * rows, 128), F32)
    norms = (ln_in_gain, ln_in_bias, chain_embed)

    def sems(n):
        return pltpu.SemaphoreType.DMA((n,))

    def exchange(slabs, groups=None):
        return lax.all_to_all(
            slabs, "row", split_axis=0, concat_axis=0, tiled=True, axis_index_groups=groups
        )

    halves = [list(range(h * half, (h + 1) * half)) for h in range(2)]
    *own, slabs, x_t, marks, row_marks = call(
        first_kernel, [own_slab] * half + [sent, state_t, mark, row_mark],
        [
            pltpu.VMEM(pair.shape, BF16), w_wide, pltpu.VMEM((3, 2, C), F32), ids, ids, pltpu.VMEM((4 * HC, C), BF16),
            vector, vector, vector, slabs_wide, sems(6), sems(len(groups(rows))),
        ],
        (), (residue_mask, chain_ids, pair, *norms, w_ab), 2 * pairs * C * 4 * HC, FIRST_VMEM_LIMIT,
    )
    recv = exchange(slabs)
    gate, weights, vectors = call(
        gate_kernel, [gate_t, turned, columns],
        [pltpu.VMEM((5, 2, C), F32), pltpu.VMEM((2, 2, C, C), BF16), w_wide, sems(8)],
        (x_t, marks, row_marks), (*norms, w_gate, w_ab, ln_mid_gain, ln_mid_bias, w_out), 2 * pairs * C * C,
    )
    gate, weights, vectors, *own[5:] = lax.optimization_barrier((gate, weights, vectors, *own[5:]))
    own = [own[0]] + [lax.ppermute(own[o], "row", [(i, i ^ o) for i in range(devices)]) for o in range(1, half)]
    products = call(
        functools.partial(first_products_kernel, rows), [own_back],
        [
            own_spread, all_spread, pltpu.VMEM((2 * channels, cols, width, 128), F32), own_spread,
        ],
        (recv, *own), (), 2 * channels * width**3, PRODUCTS_VMEM_LIMIT,
    )[0]
    tri = exchange(products, halves)
    slabs, x_t = call(
        middle_kernel, [sent, state_t], [slabs_wide, tri_wide],
        (tri, gate, x_t, marks, row_marks, weights, vectors), (), 2 * pairs * C * 5 * HC,
    )
    recv = exchange(slabs)
    w_last = jax.ShapeDtypeStruct((HC, C), BF16)
    columns_last = jax.ShapeDtypeStruct((2, C, 128), F32)
    gate, x_t, weights, vectors = call(
        second_gate_kernel, [gate_t, state_t, w_last, columns_last], [], (x_t, marks, row_marks, weights, vectors), (),
        2 * pairs * C * C,
    )
    recv, gate, x_t, weights, vectors = lax.optimization_barrier((recv, gate, x_t, weights, vectors))
    products = call(
        functools.partial(second_products_kernel, rows), [back],
        [all_spread, pltpu.VMEM((channels, cols, width, 128), F32), back_spread], (recv,), (), 2 * channels * width**3,
    )[0]
    tri = exchange(products)
    return call(
        last_kernel, [jax.ShapeDtypeStruct(pair.shape, BF16)], [tri_wide], (tri, gate, x_t, weights, vectors), (),
        2 * pairs * C * C,
    )[0]


def solution(mesh):
    in_specs = (P(("grp", "row"), None, None), P("grp"), P("grp")) + (P(),) * 8
    out_specs = P(("grp", "row"), None, None)
    return jax.shard_map(local, mesh=mesh, in_specs=in_specs, out_specs=out_specs, check_vma=False)
```
